256 devices in a mesh: gx: 8 (over x, core), gy: 32 (over z, y).
Axes of the slice: x: 4, y: 4, z: 8, core: 2. Of those that a mesh axis runs over, the one named last changes fastest.
Arguments:
- fields: float32 [8, 1024, 8192], P(None, 'gx', 'gy'), may hold values from -6 to 6
- velocity: float32 [2, 1024, 8192], P(None, 'gx', 'gy'), may hold values from -1 to 1
- mode_gain: float32 [256, 256, 2, 128], P('gx', 'gy'), may hold values from -5 to 5
- lift_weight: float32 [8, 128], replicated, may hold values from -2 to 2
- project_weight: float32 [128, 8], replicated, may hold values from -0.5 to 0.5
- obs_height: float32 [256, 256, 128], P(('gx', 'gy')), may hold values from -6 to 6
- obs_weight: float32 [256, 256, 128], P(('gx', 'gy')), may hold values from 0.25 to 4
- cell_rows: int32 [256, 256, 128], P(('gx', 'gy')), may hold values from 0 to 127
- cell_cols: int32 [256, 256, 128], P(('gx', 'gy')), may hold values from 0 to 255
- counts: int32 [256, 256], P(('gx', 'gy')), may hold values from 0 to 128, as said below
Outputs:
- corrected: float32 [8, 1024, 8192], P(None, 'gx', 'gy')
- surface_gradient: float32 [1024, 8192], P('gx', 'gy')
The draws below stay inside these ranges and needn't reach their ends.
Inputs may be any that keep to these rules, and one draw needn't show every extreme that they name: The first counts[o, s] points of a block are live, the rest are padding; some owning tile has every block full.
All inputs are finite; a program needn't handle non-finite values.
Results may differ from the reference program's by a relative error of at most 0.000076.
Values sent between devices are 32-bit elements; how exact they have to be, the bound alone decides.
No kernel may reach another device: no remote copies, remote signals or barrier semaphores. Data moves between devices by JAX's collectives and lax.ppermute only.
A program may use at most 128 MiB of HBM per device.

```python
import math
import jax
import jax.numpy as jnp
from jax import lax

F = 8
C = 128
MX = 256
MY = 256
PTS = 128
CX = 128
CY = 256
NX = 1024
NY = 8192
N_GY = 32
DEVICES = 256


def draw_counts(key, part):
    key = jax.random.fold_in(key, 5)
    level_key, count_key, owner_key = jax.random.split(key, 3)
    load_level = jax.random.randint(level_key, (DEVICES, 1), 0, 4)
    ceiling = jnp.where(load_level == 3, PTS, jnp.where(load_level == 2, PTS // 2, jnp.where(load_level == 1, PTS // 4, PTS // 8)))
    drawn_counts = jax.random.randint(count_key, (DEVICES, DEVICES), 0, ceiling + 1)
    busiest = jax.random.randint(owner_key, (), 0, DEVICES)
    owner_rows = jnp.arange(DEVICES)[:, None]
    return jnp.where(owner_rows == busiest, PTS, drawn_counts).astype(jnp.int32)


def place_ends(entries, stream_key, least, top_value):
    longest = entries.shape.index(max(entries.shape))
    spots = []
    for shift in (0, 1):
        where = [jax.random.randint(jax.random.fold_in(stream_key, axis), (), 0, length) for axis, length in enumerate(entries.shape)]
        where[longest] = (where[longest] + shift) % entries.shape[longest]
        spots.append(tuple(where))
    return entries.at[spots[0]].set(least).at[spots[1]].set(top_value)


def steps_of(key, shape, pieces, smallest, high):
    def one(position, parts):
        steps = jax.random.uniform(jax.random.fold_in(jax.random.fold_in(key, 6), position), (parts,), jnp.float32, smallest / len(pieces), high / len(pieces))
        return jnp.repeat(jnp.exp(steps), shape[position] // parts).reshape((-1,) + (1,) * (len(shape) - position - 1))

    gain = one(*pieces[0])
    for cut in pieces[1:]:
        gain = gain * one(*cut)
    return gain


def bell_draw(stream_key, dims, scale, most, pieces=(), held_as=jnp.bfloat16):
    level = steps_of(stream_key, dims, pieces, -0.22, 0.18) if pieces else 1.0
    entries = jax.random.normal(stream_key, dims, jnp.float32) * scale * level
    return jnp.minimum(jnp.maximum(entries, -most), most).astype(held_as)


def setup_inputs(seed: int = 0) -> dict:
    arg_keys = jax.random.split(jax.random.key(seed), 11)
    fields = bell_draw(arg_keys[0], (F, NX, NY), 1.0, 6.0, ((1, 8), (2, 32)), jnp.float32)
    velocity = jnp.clip(jax.random.uniform(arg_keys[1], (2, NX, NY), jnp.float32, -1.0, 1.0) * steps_of(arg_keys[1], (2, NX, NY), ((1, 8), (2, 32)), -0.4, 0.0), -1.0, 1.0)
    mode_gain = bell_draw(arg_keys[2], (MX, MY, 2, C), 0.7, 5.0, ((0, 8), (1, 32)), jnp.float32)
    lift_weight = bell_draw(arg_keys[3], (F, C), F ** -0.5, 2.0, (), jnp.float32)
    project_weight = bell_draw(arg_keys[4], (C, F), C ** -0.5, 0.5, (), jnp.float32)
    obs_height = bell_draw(arg_keys[5], (DEVICES, DEVICES, PTS), 1.0, 6.0, ((0, 256),), jnp.float32)
    obs_weight = jnp.clip(jnp.exp(math.log(4.0) - 2.7725887 * jax.random.uniform(arg_keys[6], (DEVICES, DEVICES, PTS), jnp.float32) ** steps_of(arg_keys[6], (DEVICES, DEVICES, PTS), ((0, 256),), -0.2, 0.2)), 0.25, 4.0)
    cell_rows = place_ends(jax.random.randint(arg_keys[7], (DEVICES, DEVICES, PTS), 0, CX), jax.random.fold_in(arg_keys[7], 1), 0, CX - 1).astype(jnp.int32)
    cell_cols = place_ends(jax.random.randint(arg_keys[8], (DEVICES, DEVICES, PTS), 0, CY), jax.random.fold_in(arg_keys[8], 1), 0, CY - 1).astype(jnp.int32)
    counts = draw_counts(jax.random.fold_in(arg_keys[10], 71), 0)
    return {"fields": fields, "velocity": velocity, "mode_gain": mode_gain, "lift_weight": lift_weight, "project_weight": project_weight, "obs_height": obs_height, "obs_weight": obs_weight, "cell_rows": cell_rows, "cell_cols": cell_cols, "counts": counts}


time_step = 0.2
diffusion = 0.25
highest = lax.Precision.HIGHEST

def advance(fields, velocity):
    nx_total = fields.shape[1]
    ny_total = fields.shape[2]
    padded = jnp.pad(fields, ((0, 0), (1, 1), (1, 1)))
    flow_pad = jnp.pad(velocity, ((0, 0), (1, 1), (1, 1)))
    west_side = padded[:, :-1, 1:-1]
    east_side = padded[:, 1:, 1:-1]
    speed_x = flow_pad[0, 1:, 1:-1]
    faces_x = jnp.arange(nx_total + 1)
    open_x = ((faces_x >= 1) & (faces_x <= nx_total - 1)).astype(fields.dtype)[:, None]
    flux_x = (jnp.maximum(speed_x, 0.0) * west_side + jnp.minimum(speed_x, 0.0) * east_side - diffusion * (east_side - west_side)) * open_x
    south_side = padded[:, 1:-1, :-1]
    north_side = padded[:, 1:-1, 1:]
    speed_y = flow_pad[1, 1:-1, 1:]
    faces_y = jnp.arange(ny_total + 1)
    open_y = ((faces_y >= 1) & (faces_y <= ny_total - 1)).astype(fields.dtype)[None, :]
    flux_y = (jnp.maximum(speed_y, 0.0) * south_side + jnp.minimum(speed_y, 0.0) * north_side - diffusion * (north_side - south_side)) * open_y
    return fields - time_step * (flux_x[:, 1:] - flux_x[:, :-1] + flux_y[:, :, 1:] - flux_y[:, :, :-1])

def reference(fields, velocity, mode_gain, lift_weight, project_weight, obs_height, obs_weight, cell_rows, cell_cols, counts):
    stepped = advance(fields, velocity)
    kept_rows = jnp.concatenate((jnp.arange(MX // 2), jnp.arange(NX - MX // 2, NX))).astype(jnp.int32)

    def forward_one(single):
        return jnp.fft.rfft2(single)[kept_rows, :MY]
    low_modes = lax.map(forward_one, stepped)
    scale_in = 1.0 / math.sqrt(NX * NY)
    real_part = jnp.real(low_modes) * scale_in
    imag_part = jnp.imag(low_modes) * scale_in
    lifted_real = jnp.einsum('fmn,fc->mnc', real_part, lift_weight, precision=highest)
    lifted_imag = jnp.einsum('fmn,fc->mnc', imag_part, lift_weight, precision=highest)
    gain_real = mode_gain[:, :, 0, :]
    gain_imag = mode_gain[:, :, 1, :]
    mixed_real = gain_real * lifted_real - gain_imag * lifted_imag
    mixed_imag = gain_real * lifted_imag + gain_imag * lifted_real
    out_real = jnp.einsum('mnc,cf->fmn', mixed_real, project_weight, precision=highest)
    out_imag = jnp.einsum('mnc,cf->fmn', mixed_imag, project_weight, precision=highest)
    outgoing = lax.complex(out_real, out_imag)

    def inverse_one(single):
        spectrum = jnp.zeros((NX, NY // 2 + 1), single.dtype)
        spectrum = spectrum.at[kept_rows, :MY].set(single)
        return jnp.fft.irfft2(spectrum, s=(NX, NY))
    correction = lax.map(inverse_one, outgoing) * (NX * NY / math.sqrt(MX * MY))
    corrected = stepped + correction.astype(stepped.dtype)
    surface = corrected[0].reshape(-1)
    owners = jnp.arange(DEVICES)
    base_x = owners // N_GY * CX
    base_y = owners % N_GY * CY
    global_x = base_x[:, None, None] + cell_rows
    global_y = base_y[:, None, None] + cell_cols
    flat_index = (global_x * NY + global_y).astype(jnp.int32)
    is_live = (jnp.arange(PTS)[None, None, :] < counts[:, :, None]).astype(corrected.dtype)
    heights = jnp.transpose(obs_height, (1, 0, 2))
    weights = jnp.transpose(obs_weight, (1, 0, 2))
    misfit = weights * (surface[flat_index] - heights) * is_live
    gradient = jnp.zeros((NX * NY,), corrected.dtype).at[flat_index.reshape(-1)].add(misfit.reshape(-1))
    return (corrected, gradient.reshape(NX, NY))
```

```python
import math

import jax
import jax.numpy as jnp
import numpy as np
from jax import lax
from jax.experimental import pallas as pl
from jax.experimental.pallas import tpu as pltpu
from jax.sharding import PartitionSpec as P

MX = 256
MY = 256
NX = 1024
NY = 8192
F = 8
CX = 128
CY = 256
GX = 8
GY = 32
DEV = GX * GY
HALF = MY // 2

time_step = 0.2
diffusion = 0.25
highest = lax.Precision.HIGHEST


def tables():
    x = np.arange(NX)
    rows = np.zeros((DEV + 8, NX))
    for gx in range(GX):
        for gy in range(GY):
            q = GY * (gx // 2) + gy
            ang = 2.0 * np.pi * ((q * x) % NX) / NX
            rows[gx * GY + gy] = np.cos(ang) if gx % 2 == 0 else -np.sin(ang)
    ang = 2.0 * np.pi * ((MX // 2 * x) % NX) / NX
    rows[GY] = np.cos(ang)
    rows[DEV] = -np.sin(ang)
    n = np.arange(MY)
    j = np.arange(CY)
    ang = 2.0 * np.pi * ((j[:, None] * n[None, :]) % NY) / NY
    local = np.concatenate((np.cos(ang), -np.sin(ang)), axis=1)
    g = np.arange(GY)
    ang = 2.0 * np.pi * ((g[:, None] * n[None, :]) % GY) / GY
    turn = np.concatenate((np.cos(ang), np.sin(ang)), axis=1)
    return rows.astype(np.float32), local.astype(np.float32), turn.astype(np.float32)


ROWS, LOCAL, TURN = tables()


def gain_moves():
    first, second = [], []
    for gx in range(GX):
        for gy in range(GY):
            source = gx * GY + gy
            m = 32 * gx + gy
            if gx < GX // 2:
                first.append((source, 2 * gx * GY + gy))
                second.append((source, (2 * gx + 1) * GY + gy))
            else:
                q = 0 if m == MX // 2 else MX - m
                x, y = q // GY, q % GY
                first.append((source, (2 * x + 1) * GY + y))
                second.append((source, 2 * x * GY + y))
    return first, second


def all_to_all(array, axis):
    return lax.all_to_all(array, axis, split_axis=0, concat_axis=0, tiled=True)


def advance(fields, velocity):
    gx = lax.axis_index("gx")
    gy = lax.axis_index("gy")
    up_x = [(i, i + 1) for i in range(GX - 1)]
    down_x = [(i + 1, i) for i in range(GX - 1)]
    up_y = [(i, i + 1) for i in range(GY - 1)]
    down_y = [(i + 1, i) for i in range(GY - 1)]
    west = lax.ppermute(fields[:, -1, :], "gx", up_x)
    east = lax.ppermute(
        jnp.concatenate((fields[:, 0, :], velocity[:1, 0, :]), axis=0), "gx", down_x
    )
    south = lax.ppermute(fields[:, :, -1], "gy", up_y)
    north = lax.ppermute(
        jnp.concatenate((fields[:, :, 0], velocity[1:, :, 0]), axis=0), "gy", down_y
    )
    wide = jnp.concatenate((west[:, None, :], fields, east[:F, None, :]), axis=1)
    speed = jnp.concatenate((velocity[0], east[F:]), axis=0)
    face = gx * CX + jnp.arange(CX + 1, dtype=jnp.int32)
    open_x = ((face >= 1) & (face <= NX - 1)).astype(jnp.float32)[:, None]
    low, high = wide[:, :-1], wide[:, 1:]
    flux_x = (
        jnp.maximum(speed, 0.0) * low + jnp.minimum(speed, 0.0) * high - diffusion * (high - low)
    ) * open_x
    wide = jnp.concatenate((south[:, :, None], fields, north[:F, :, None]), axis=2)
    speed = jnp.concatenate((velocity[1], north[F:].T), axis=1)
    face = gy * CY + jnp.arange(CY + 1, dtype=jnp.int32)
    open_y = ((face >= 1) & (face <= NY - 1)).astype(jnp.float32)[None, :]
    low, high = wide[:, :, :-1], wide[:, :, 1:]
    flux_y = (
        jnp.maximum(speed, 0.0) * low + jnp.minimum(speed, 0.0) * high - diffusion * (high - low)
    ) * open_y
    return fields - time_step * (
        flux_x[:, 1:] - flux_x[:, :-1] + flux_y[:, :, 1:] - flux_y[:, :, :-1]
    )


CHUNK = 16
CPTS = CHUNK * 128


def scatter_kernel(rows_ref, cols_ref, weight_ref, height_ref, sum_w_ref, sum_wh_ref, a_ref, b_ref, acc_ref):
    step = pl.program_id(0)
    weight = weight_ref[...]
    product = weight * height_ref[...]
    pieces = []
    for value in (weight, product):
        for _ in range(3):
            piece = value.astype(jnp.bfloat16)
            pieces.append(piece)
            value = value - piece.astype(jnp.float32)
    rows = rows_ref[...].astype(jnp.float32).astype(jnp.bfloat16)
    cols = cols_ref[...].astype(jnp.float32).astype(jnp.bfloat16)
    spot_r = lax.broadcasted_iota(jnp.int32, (CX, 128), 0).astype(jnp.float32).astype(jnp.bfloat16)
    spot_c = lax.broadcasted_iota(jnp.int32, (CY, 128), 0).astype(jnp.float32).astype(jnp.bfloat16)
    zero = jnp.zeros((CX, 128), jnp.bfloat16)
    one_c = jnp.ones((CY, 128), jnp.bfloat16)
    zero_c = jnp.zeros((CY, 128), jnp.bfloat16)
    for s in range(CHUNK):
        lanes = pl.ds(s * 128, 128)
        hit = spot_r == jnp.broadcast_to(rows[s : s + 1], (CX, 128))
        for k, piece in enumerate(pieces):
            a_ref[pl.ds(k * CX, CX), lanes] = jnp.where(
                hit, jnp.broadcast_to(piece[s : s + 1], (CX, 128)), zero
            )
        hit = spot_c == jnp.broadcast_to(cols[s : s + 1], (CY, 128))
        b_ref[:, lanes] = jnp.where(hit, one_c, zero_c)
    part = lax.dot_general(
        a_ref[...], b_ref[...], (((1,), (1,)), ((), ())), preferred_element_type=jnp.float32
    )

    @pl.when(step == 0)
    def _():
        acc_ref[...] = part

    @pl.when(step > 0)
    def _():
        acc_ref[...] += part

    @pl.when(step == pl.num_programs(0) - 1)
    def _():
        sum_w_ref[...] = acc_ref[0:CX] + acc_ref[CX : 2 * CX] + acc_ref[2 * CX : 3 * CX]
        sum_wh_ref[...] = (
            acc_ref[3 * CX : 4 * CX] + acc_ref[4 * CX : 5 * CX] + acc_ref[5 * CX : 6 * CX]
        )


def scatter(rows, cols, weight, height):
    steps = rows.shape[0] // CHUNK
    block = pl.BlockSpec((CHUNK, 128), lambda i: (i, 0))
    whole = pl.BlockSpec((CX, CY), lambda i: (0, 0))
    return pl.pallas_call(
        scatter_kernel,
        grid=(steps,),
        in_specs=[block] * 4,
        out_specs=[whole, whole],
        out_shape=[jax.ShapeDtypeStruct((CX, CY), jnp.float32)] * 2,
        scratch_shapes=[
            pltpu.VMEM((6 * CX, CPTS), jnp.bfloat16),
            pltpu.VMEM((CY, CPTS), jnp.bfloat16),
            pltpu.VMEM((6 * CX, CY), jnp.float32),
        ],
        compiler_params=pltpu.CompilerParams(vmem_limit_bytes=24 * 1024 * 1024),
        cost_estimate=pl.CostEstimate(
            flops=2 * 6 * CX * CY * 128 * rows.shape[0],
            bytes_accessed=4 * 128 * 4 * rows.shape[0],
            transcendentals=0,
        ),
    )(rows, cols, weight, height)


def body(
    fields,
    velocity,
    mode_gain,
    lift_weight,
    project_weight,
    obs_height,
    obs_weight,
    cell_rows,
    cell_cols,
    counts,
):
    gx = lax.axis_index("gx")
    gy = lax.axis_index("gy")
    core = gx % 2
    special = ((gx < 2) & (gy == 0)).astype(jnp.float32)
    swap = [(i, i ^ 1) for i in range(GX)]

    gains = lax.all_to_all(mode_gain, "gy", split_axis=0, concat_axis=1, tiled=True)[0]
    low_gain, high_gain = gains[:HALF], gains[HALF:]
    first, second = gain_moves()
    positive = gx < GX // 2
    gain_a = lax.ppermute(jnp.where(positive, low_gain, high_gain), ("gx", "gy"), first)
    gain_b = lax.ppermute(jnp.where(positive, high_gain, low_gain), ("gx", "gy"), second)

    stepped = advance(fields, velocity)

    columns = all_to_all(stepped, "gx").reshape(NX, CY)
    rows = jnp.asarray(ROWS)
    parts = jnp.dot(rows, columns, precision=highest)
    extra = parts[DEV]
    extra = jnp.where(
        (jnp.arange(DEV)[:, None] // GY) % 2 == 0, extra[None, :HALF], extra[None, HALF:]
    )
    sent = jnp.concatenate((parts[:DEV], extra, obs_height[0], obs_weight[0]), axis=1)
    got = all_to_all(sent, ("gx", "gy"))

    live = jnp.arange(128, dtype=jnp.int32)[None, :] < counts[0][:, None]
    weight = jnp.where(live, got[:, 512:640], 0.0)
    sum_w, sum_wh = scatter(cell_rows[0], cell_cols[0], weight, got[:, 384:512])

    scale = 1.0 / math.sqrt(NX * NY)
    local = jnp.asarray(LOCAL)
    turn_r, turn_i = jnp.asarray(TURN[:, :MY]), jnp.asarray(TURN[:, MY:])
    local_half = jnp.where(core == 0, local[:HALF], local[HALF:])

    def along_y(block, table):
        modes = jnp.dot(block, table, precision=highest).reshape(F, GY, 2 * MY)
        real, imag = modes[:, :, :MY], modes[:, :, MY:]
        out_r = jnp.sum(real * turn_r + imag * turn_i, axis=1)
        out_i = jnp.sum(imag * turn_r - real * turn_i, axis=1)
        return jnp.stack((out_r, out_i)) * scale

    mine = jnp.stack((along_y(got[:, :256], local), along_y(got[:, 256:384], local_half)))
    keep = jnp.where(core == 0, mine[..., :HALF], mine[..., HALF:])
    give = jnp.where(core == 0, mine[..., HALF:], mine[..., :HALF])
    other = lax.ppermute(give, "gx", swap)
    real_part = jnp.where(core == 0, keep[0], other[0])
    imag_part = jnp.where(core == 0, other[0], keep[0])
    extra_part = keep[1] + other[1]

    plain = 1.0 - special
    plus = jnp.stack(
        (real_part[0] - plain * imag_part[1], real_part[1] + plain * imag_part[0])
    )
    base = plain * real_part + special * imag_part
    turned = plain * imag_part + special * extra_part
    minus = jnp.stack((base[0] + turned[1], base[1] - turned[0]))

    def mix(coeffs, gain):
        lifted = jnp.einsum("pfn,fc->pnc", coeffs, lift_weight, precision=highest)
        gain_r, gain_i = gain[:, 0], gain[:, 1]
        mixed = jnp.stack(
            (
                gain_r * lifted[0] - gain_i * lifted[1],
                gain_r * lifted[1] + gain_i * lifted[0],
            )
        )
        return jnp.einsum("pnc,cf->pfn", mixed, project_weight, precision=highest)

    out_a = mix(jnp.where(core == 0, plus, minus), gain_a)
    out_b = mix(jnp.where(core == 0, minus, plus), gain_b)
    n_index = core * HALF + jnp.arange(HALF, dtype=jnp.int32)
    n_weight = jnp.where(n_index == 0, 1.0, 2.0).astype(jnp.float32) / math.sqrt(MX * MY)
    plus = jnp.where(core == 0, out_a, out_b) * n_weight
    minus = jnp.where(core == 0, out_b, out_a) * n_weight

    even = plus + plain * minus
    gap = plus - minus
    odd = plain * jnp.stack((gap[1], -gap[0])) + special * minus
    spare = jnp.stack((-minus[1], minus[0]))
    keep = jnp.stack((jnp.where(core == 0, even, odd), spare))
    give = jnp.stack((jnp.where(core == 0, odd, even), spare))
    other = lax.ppermute(give, "gx", swap)
    lower = jnp.where(core == 0, keep, other)
    upper = jnp.where(core == 0, other, keep)
    modes = jnp.concatenate((lower, upper), axis=-1)

    def back_y(coeffs, table):
        real, imag = coeffs[0][:, None, :], coeffs[1][:, None, :]
        turned = jnp.concatenate(
            (real * turn_r - imag * turn_i, real * turn_i + imag * turn_r), axis=-1
        ).reshape(DEV, 2 * MY)
        return lax.dot_general(turned, table, (((1,), (1,)), ((), ())), precision=highest)

    sent = jnp.concatenate((back_y(modes[0], local), back_y(modes[1], local_half)), axis=1)
    got = all_to_all(sent, ("gx", "gy"))

    spare_row = jnp.concatenate((got[0, 256:384], got[GY, 256:384]))
    block = jnp.concatenate(
        (got[:, :256], spare_row[None], jnp.zeros((7, 256), jnp.float32)), axis=0
    )
    correction = lax.dot_general(rows, block, (((0,), (0,)), ((), ())), precision=highest)
    correction = all_to_all(correction.reshape(GX, CX, CY), "gx")
    corrected = stepped + correction
    gradient = corrected[0] * sum_w - sum_wh
    return (corrected, gradient)


def solution(mesh):
    return jax.shard_map(
        body,
        mesh=mesh,
        in_specs=(
            P(None, "gx", "gy"),
            P(None, "gx", "gy"),
            P("gx", "gy", None, None),
            P(),
            P(),
            P(("gx", "gy"), None, None),
            P(("gx", "gy"), None, None),
            P(("gx", "gy"), None, None),
            P(("gx", "gy"), None, None),
            P(("gx", "gy"), None),
        ),
        out_specs=(P(None, "gx", "gy"), P("gx", "gy")),
        check_vma=False,
    )
```

```python
import math

import jax
import jax.numpy as jnp
import numpy as np
from jax import lax
from jax.experimental import pallas as pl
from jax.experimental.pallas import tpu as pltpu
from jax.sharding import PartitionSpec as P

MX = 256
MY = 256
NX = 1024
NY = 8192
F = 8
CX = 128
CY = 256
GX = 8
GY = 32
DEV = GX * GY
HALF = MY // 2

time_step = 0.2
diffusion = 0.25
highest = lax.Precision.HIGHEST


ORDER = np.array(
    [GX * gy + 4 * high + low for high in range(2) for low in range(4) for gy in range(GY)]
)


def tables():
    x = np.arange(MX)
    q = np.arange(MX // 2)
    ang = 2.0 * np.pi * (q[:, None] * x[None, :]) / NX
    fore_x = np.concatenate((np.cos(ang), -np.sin(ang)))
    m = np.arange(MX)
    q = np.where(m < MX // 2, m, m - MX)
    ang = 2.0 * np.pi * (x[:, None] * q[None, :]) / NX
    back_x = np.concatenate((np.cos(ang), -np.sin(ang)), axis=1)
    ang = 2.0 * np.pi * np.arange(8) / 8.0
    period = np.stack([np.tile(row[:, None], (1, CY)) for row in (np.cos(ang), -np.sin(ang))])
    ang = 2.0 * np.pi * (ORDER[:, None] * np.arange(CY)[None, :]) / NY
    fore_y = np.concatenate((np.cos(ang), np.sin(ang)))
    back_y = np.concatenate((np.cos(ang.T), np.sin(ang.T)))
    turn = np.zeros((2, 4, 4, GY, 2, 2, 32))
    for quarter in range(4):
        for low in range(4):
            for high in range(2):
                n = 8 * quarter + 4 * high + low
                ang = 2.0 * np.pi * ((n * np.arange(GY)) % GY) / GY
                turn[0, quarter, low, :, :, high] = np.cos(ang)[:, None, None]
                turn[1, quarter, low, :, :, high] = np.sin(ang)[:, None, None]
    turn = turn.reshape(2, 4, 4, GY, 128)
    return tuple(
        array.astype(np.float32) for array in (fore_x, back_x, period, fore_y, back_y, turn)
    )


FORE_X, BACK_X, PERIOD, FORE_Y, BACK_Y, TURN = tables()
SCALE_IN = 1.0 / math.sqrt(NX * NY)
SCALE_OUT = 1.0 / math.sqrt(MX * MY)


def all_to_all(array, axis):
    return lax.all_to_all(array, axis, split_axis=0, concat_axis=0, tiled=True)


def dot(a, b, contract=((1,), (0,))):
    return lax.dot_general(
        a, b, (contract, ((), ())), precision=highest, preferred_element_type=jnp.float32
    )


def shape(*dims):
    return jax.ShapeDtypeStruct(dims, jnp.float32)


def local_kernel(kernel, out_shape, operands, scalars=(), flops=0, scratch=()):
    vmem = pl.BlockSpec(memory_space=pltpu.VMEM)
    smem = pl.BlockSpec(memory_space=pltpu.SMEM)
    size = sum(4 * math.prod(a.shape) for a in (*operands, *out_shape))
    return pl.pallas_call(
        kernel,
        in_specs=[smem] * len(scalars) + [vmem] * len(operands),
        out_specs=[vmem] * len(out_shape),
        out_shape=out_shape,
        scratch_shapes=scratch,
        compiler_params=pltpu.CompilerParams(vmem_limit_bytes=24 * 1024 * 1024),
        cost_estimate=pl.CostEstimate(flops=flops, bytes_accessed=size, transcendentals=0),
    )(*scalars, *operands)


def edge_kernel(fields_ref, velocity_ref, last_x_ref, first_x_ref, last_y_ref, first_y_ref):
    first_x_ref[...] = jnp.zeros((16, CY), jnp.float32)
    first_y_ref[...] = jnp.zeros((16, CX), jnp.float32)
    row = lax.broadcasted_iota(jnp.int32, (8, CY), 0)
    col = lax.broadcasted_iota(jnp.int32, (8, CY), 1)
    pick = jnp.where(
        ((row == 0) & (col == 0)) | ((row == 1) & (col == CY - 1)), 1.0, 0.0
    ).astype(jnp.float32)
    for f in range(F):
        block = fields_ref[f]
        last_x_ref[f : f + 1] = block[CX - 1 : CX]
        first_x_ref[f : f + 1] = block[0:1]
        ends = dot(pick, block, ((1,), (1,)))
        first_y_ref[f : f + 1] = ends[0:1]
        last_y_ref[f : f + 1] = ends[1:2]
    first_x_ref[F : F + 1] = velocity_ref[0, 0:1]
    first_y_ref[F : F + 1] = dot(pick, velocity_ref[1], ((1,), (1,)))[0:1]


def step_kernel(
    fields_ref, velocity_ref, west_ref, east_ref, south_ref, north_ref, out_ref, *block_refs
):
    row = lax.broadcasted_iota(jnp.int32, (CX, CY), 0)
    col = lax.broadcasted_iota(jnp.int32, (CX, CY), 1)
    first_row, last_row = row == 0, row == CX - 1
    first_col, last_col = col == 0, col == CY - 1
    gx, gy = lax.axis_index("gx"), lax.axis_index("gy")
    is_open = [
        jnp.where(test, 1.0, 0.0) for test in (gx > 0, gx < GX - 1, gy > 0, gy < GY - 1)
    ]
    before = jnp.transpose(south_ref[...])
    after = jnp.transpose(north_ref[...])
    speed = velocity_ref[0]
    shut = jnp.where(first_row, is_open[0], 1.0)
    low_w = time_step * shut * (jnp.maximum(speed, 0.0) + diffusion)
    high_w = time_step * shut * (jnp.minimum(speed, 0.0) - diffusion)
    edge = east_ref[F : F + 1]
    low_edge = time_step * is_open[1] * (jnp.maximum(edge, 0.0) + diffusion)
    high_edge = time_step * is_open[1] * (jnp.minimum(edge, 0.0) - diffusion)
    low_e = jnp.where(last_row, low_edge, pltpu.roll(low_w, CX - 1, 0))
    high_e = jnp.where(last_row, high_edge, pltpu.roll(high_w, CX - 1, 0))
    speed = velocity_ref[1]
    shut = jnp.where(first_col, is_open[2], 1.0)
    low_s = time_step * shut * (jnp.maximum(speed, 0.0) + diffusion)
    high_s = time_step * shut * (jnp.minimum(speed, 0.0) - diffusion)
    edge = after[:, F : F + 1]
    low_edge = time_step * is_open[3] * (jnp.maximum(edge, 0.0) + diffusion)
    high_edge = time_step * is_open[3] * (jnp.minimum(edge, 0.0) - diffusion)
    low_n = jnp.where(last_col, low_edge, pltpu.roll(low_s, CY - 1, 1))
    high_n = jnp.where(last_col, high_edge, pltpu.roll(high_s, CY - 1, 1))
    own = 1.0 - low_e + high_w - low_n + high_s
    for f in range(F):
        block = fields_ref[f]
        west = jnp.where(first_row, west_ref[f : f + 1], pltpu.roll(block, 1, 0))
        east = jnp.where(last_row, east_ref[f : f + 1], pltpu.roll(block, CX - 1, 0))
        south = jnp.where(first_col, before[:, f : f + 1], pltpu.roll(block, 1, 1))
        north = jnp.where(last_col, after[:, f : f + 1], pltpu.roll(block, CY - 1, 1))
        out_ref[f] = (
            own * block + low_w * west - high_e * east + low_s * south - high_n * north
        )
    for k, ref in enumerate(block_refs):
        ref[...] = out_ref[lax.rem(lax.axis_index("gx") + k, GX)]


def quarter_turn(index, t):
    place = lax.rem(index * t, 4)
    cosine = jnp.where(place == 0, 1.0, jnp.where(place == 2, -1.0, 0.0))
    sine = jnp.where(place == 1, 1.0, jnp.where(place == 3, -1.0, 0.0))
    return cosine.astype(jnp.float32), sine.astype(jnp.float32)


def forward_kernel(*refs):
    *block_refs, fore_x_ref, period_ref, fore_y_ref, height_ref, weight_ref = refs[:-3]
    out_ref, columns_ref, parts_ref = refs[-3:]
    for k, ref in enumerate(block_refs):
        source = lax.rem(lax.axis_index("gx") + (GX - k), GX)
        columns_ref[pl.ds(pl.multiple_of(source * CX, CX), CX), :] = ref[...]
    q = lax.broadcasted_iota(jnp.int32, (HALF, CY), 0)
    real = jnp.zeros((HALF, CY), jnp.float32)
    imag = jnp.zeros((HALF, CY), jnp.float32)
    for t in range(4):
        piece = dot(fore_x_ref[...], columns_ref[t * MX : (t + 1) * MX])
        piece_r, piece_i = piece[:HALF], piece[HALF:]
        if t == 0:
            real, imag = piece_r, piece_i
        else:
            cosine, sine = quarter_turn(q, t)
            real = real + piece_r * cosine + piece_i * sine
            imag = imag + piece_i * cosine - piece_r * sine
    folded = jnp.sum(columns_ref[...].reshape(NX // 8, 8, CY), axis=0)
    last_r = jnp.sum(folded * period_ref[0], axis=0, keepdims=True)
    last_i = jnp.sum(folded * period_ref[1], axis=0, keepdims=True)
    row = lax.broadcasted_iota(jnp.int32, (HALF, HALF), 0)
    col = lax.broadcasted_iota(jnp.int32, (HALF, HALF), 1)
    mirror = jnp.where(row + col == HALF, 1.0, 0.0).astype(jnp.float32)
    parts_ref[0:HALF] = real
    parts_ref[HALF:MX] = jnp.where(q == 0, last_r, dot(mirror, real))
    parts_ref[MX : MX + HALF] = imag
    parts_ref[MX + HALF :] = -jnp.where(q == 0, last_i, dot(mirror, imag))
    mixed = dot(fore_y_ref[...], parts_ref[...], ((1,), (1,)))
    modes = (mixed[:MY, :MX] + mixed[MY:, MX:], mixed[:MY, MX:] - mixed[MY:, :MX])
    group = lax.broadcasted_iota(jnp.int32, (GY, 128), 1) // 32
    for low in range(4):
        for half in range(2):
            tiles = [
                modes[part][high * 128 + low * 32 : high * 128 + low * 32 + 32, half * 128 : half * 128 + 128]
                for part in range(2)
                for high in range(2)
            ]
            for s in range(4):
                gx = 4 * half + s
                value = None
                for k, tile in enumerate(tiles):
                    shift = (32 * (k - s)) % 128
                    moved = pltpu.roll(tile, shift, 1) if shift else tile
                    value = moved if value is None else jnp.where(group == k, moved, value)
                out_ref[gx * GY : (gx + 1) * GY, 0, low * 128 : (low + 1) * 128] = value
    out_ref[:, 0, 512:640] = height_ref[...]
    out_ref[:, 0, 640:768] = weight_ref[...]


def mix_kernel(got_ref, turn_ref, gain_ref, lift_ref, project_ref, out_ref):
    gy = lax.axis_index("gy")
    quarter = lax.rem(gy, 4)
    lane = lax.broadcasted_iota(jnp.int32, (F, 128), 1)
    is_real = lane < 64
    high_zero = (lane // 32) % 2 == 0
    for low in range(4):
        cosine = turn_ref[0, quarter, low]
        sine = turn_ref[1, quarter, low]
        straight, crossed = [], []
        for f in range(F):
            block = got_ref[f * GY : (f + 1) * GY, low * 128 : (low + 1) * 128]
            straight.append(jnp.sum(block * cosine, axis=0, keepdims=True))
            crossed.append(jnp.sum(block * sine, axis=0, keepdims=True))
        crossed = pltpu.roll(jnp.concatenate(crossed, axis=0), 64, 1)
        coeffs = jnp.concatenate(straight, axis=0) + jnp.where(is_real, crossed, -crossed)
        lifted = dot(jnp.transpose(coeffs * SCALE_IN), lift_ref[...])
        mixed_r, mixed_i = [], []
        for high in range(2):
            lift_r = lifted[high * 32 : high * 32 + 32]
            lift_i = lifted[64 + high * 32 : 96 + high * 32]
            gain_r = gain_ref[0, 4 * high + low]
            gain_i = gain_ref[1, 4 * high + low]
            mixed_r.append(gain_r * lift_r - gain_i * lift_i)
            mixed_i.append(gain_r * lift_i + gain_i * lift_r)
        mixed = jnp.concatenate(mixed_r + mixed_i, axis=0)
        outgoing = dot(project_ref[...], mixed, ((1,), (1,)))
        first = high_zero & (gy == 0) if low == 0 else None
        scale = 2.0 * SCALE_OUT if first is None else jnp.where(first, SCALE_OUT, 2.0 * SCALE_OUT)
        outgoing = outgoing * scale
        swapped = pltpu.roll(outgoing, 64, 1)
        swapped = jnp.where(is_real, -swapped, swapped)
        for f in range(F):
            out_ref[f * GY : (f + 1) * GY, 0, low * 128 : (low + 1) * 128] = (
                outgoing[f : f + 1] * cosine + swapped[f : f + 1] * sine
            )


def backward_kernel(got_ref, back_y_ref, back_x_ref, *refs):
    *out_refs, modes_ref, field_ref = refs
    group = lax.broadcasted_iota(jnp.int32, (GY, 128), 1) // 32
    for low in range(4):
        for half in range(2):
            tiles = [
                got_ref[gx * GY : (gx + 1) * GY, low * 128 : (low + 1) * 128]
                for gx in range(4 * half, 4 * half + 4)
            ]
            for part in range(2):
                for high in range(2):
                    k = 2 * part + high
                    value = None
                    for s, tile in enumerate(tiles):
                        shift = (32 * (s - k)) % 128
                        moved = pltpu.roll(tile, shift, 1) if shift else tile
                        value = moved if value is None else jnp.where(group == s, moved, value)
                    lanes = part * MX + half * 128
                    start = high * 128 + low * 32
                    modes_ref[start : start + 32, lanes : lanes + 128] = value
    mixed = dot(back_y_ref[...], modes_ref[...])
    real = mixed[:CY, :MX] - mixed[CY:, MX:]
    imag = mixed[:CY, MX:] + mixed[CY:, :MX]
    index = lax.broadcasted_iota(jnp.int32, (CY, MX), 1)
    for t in range(4):
        if t == 0:
            turned = jnp.concatenate((real, imag), axis=1)
        else:
            cosine, sine = quarter_turn(index, t)
            turned = jnp.concatenate(
                (real * cosine - imag * sine, imag * cosine + real * sine), axis=1
            )
        field_ref[t * MX : (t + 1) * MX] = dot(back_x_ref[...], turned, ((1,), (1,)))
    for k, ref in enumerate(out_refs):
        owner = lax.rem(lax.axis_index("gx") + k, GX)
        ref[...] = field_ref[pl.ds(pl.multiple_of(owner * CX, CX), CX), :]


def finish_kernel(*refs):
    stepped_ref, *block_refs, w_0, w_1, wh_0, wh_1, out_ref, gradient_ref = refs
    for k, ref in enumerate(block_refs):
        f = lax.rem(lax.axis_index("gx") + (GX - k), GX)
        out_ref[f] = stepped_ref[f] + ref[...]
    gradient_ref[...] = out_ref[0] * (w_0[...] + w_1[...]) - (wh_0[...] + wh_1[...])


def exchange(blocks):
    moved = {0: blocks[0]}
    for k in (4, 3, 5, 2, 6, 7, 1):
        moved[k] = lax.ppermute(blocks[k], "gx", [(i, (i + k) % GX) for i in range(GX)])
    return [moved[k] for k in range(GX)]


def advance(fields, velocity):
    up_x = [(i, i + 1) for i in range(GX - 1)]
    down_x = [(i + 1, i) for i in range(GX - 1)]
    up_y = [(i, i + 1) for i in range(GY - 1)]
    down_y = [(i + 1, i) for i in range(GY - 1)]
    last_x, first_x, last_y, first_y = local_kernel(
        edge_kernel, [shape(F, CY), shape(16, CY), shape(F, CX), shape(16, CX)], (fields, velocity)
    )
    west = lax.ppermute(last_x, "gx", up_x)
    east = lax.ppermute(first_x, "gx", down_x)
    south = lax.ppermute(last_y, "gy", up_y)
    north = lax.ppermute(first_y, "gy", down_y)
    stepped, *blocks = local_kernel(
        step_kernel,
        [shape(F, CX, CY)] + [shape(CX, CY)] * GX,
        (fields, velocity, west, east, south, north),
    )
    return stepped, blocks


CHUNK = 16
CPTS = CHUNK * 128


def scatter_kernel(rows_ref, cols_ref, weight_ref, height_ref, sum_w_ref, sum_wh_ref, a_ref, b_ref, acc_ref):
    step = pl.program_id(0)
    weight = weight_ref[...]
    product = weight * height_ref[...]
    pieces = []
    for value in (weight, product):
        for _ in range(3):
            piece = value.astype(jnp.bfloat16)
            pieces.append(piece)
            value = value - piece.astype(jnp.float32)
    rows = rows_ref[...].astype(jnp.float32).astype(jnp.bfloat16)
    cols = cols_ref[...].astype(jnp.float32).astype(jnp.bfloat16)
    spot_r = lax.broadcasted_iota(jnp.int32, (CX, 128), 0).astype(jnp.float32).astype(jnp.bfloat16)
    spot_c = lax.broadcasted_iota(jnp.int32, (CY, 128), 0).astype(jnp.float32).astype(jnp.bfloat16)
    zero = jnp.zeros((CX, 128), jnp.bfloat16)
    one_c = jnp.ones((CY, 128), jnp.bfloat16)
    zero_c = jnp.zeros((CY, 128), jnp.bfloat16)
    for s in range(CHUNK):
        lanes = pl.ds(s * 128, 128)
        hit = spot_r == jnp.broadcast_to(rows[s : s + 1], (CX, 128))
        for k, piece in enumerate(pieces):
            a_ref[pl.ds(k * CX, CX), lanes] = jnp.where(
                hit, jnp.broadcast_to(piece[s : s + 1], (CX, 128)), zero
            )
        hit = spot_c == jnp.broadcast_to(cols[s : s + 1], (CY, 128))
        b_ref[:, lanes] = jnp.where(hit, one_c, zero_c)
    part = lax.dot_general(
        a_ref[...], b_ref[...], (((1,), (1,)), ((), ())), preferred_element_type=jnp.float32
    )

    @pl.when(step == 0)
    def _():
        acc_ref[...] = part

    @pl.when(step > 0)
    def _():
        acc_ref[...] += part

    @pl.when(step == pl.num_programs(0) - 1)
    def _():
        sum_w_ref[...] = acc_ref[0:CX] + acc_ref[CX : 2 * CX] + acc_ref[2 * CX : 3 * CX]
        sum_wh_ref[...] = (
            acc_ref[3 * CX : 4 * CX] + acc_ref[4 * CX : 5 * CX] + acc_ref[5 * CX : 6 * CX]
        )


def scatter(rows, cols, weight, height):
    steps = rows.shape[0] // CHUNK
    block = pl.BlockSpec((CHUNK, 128), lambda i: (i, 0))
    whole = pl.BlockSpec((CX, CY), lambda i: (0, 0))
    return pl.pallas_call(
        scatter_kernel,
        grid=(steps,),
        in_specs=[block] * 4,
        out_specs=[whole, whole],
        out_shape=[jax.ShapeDtypeStruct((CX, CY), jnp.float32)] * 2,
        scratch_shapes=[
            pltpu.VMEM((6 * CX, CPTS), jnp.bfloat16),
            pltpu.VMEM((CY, CPTS), jnp.bfloat16),
            pltpu.VMEM((6 * CX, CY), jnp.float32),
        ],
        compiler_params=pltpu.CompilerParams(vmem_limit_bytes=24 * 1024 * 1024),
        cost_estimate=pl.CostEstimate(
            flops=2 * 6 * CX * CY * 128 * rows.shape[0],
            bytes_accessed=4 * 128 * 4 * rows.shape[0],
            transcendentals=0,
        ),
    )(rows, cols, weight, height)


def body(
    fields,
    velocity,
    mode_gain,
    lift_weight,
    project_weight,
    obs_height,
    obs_weight,
    cell_rows,
    cell_cols,
    counts,
):
    stepped, blocks = advance(fields, velocity)
    sent = local_kernel(
        forward_kernel,
        [shape(DEV, 1, 768)],
        (*exchange(blocks), *map(jnp.asarray, (FORE_X, PERIOD, FORE_Y)), obs_height[0], obs_weight[0]),
        flops=6 * 2 * (256 * NX * CY + 512 * 256 * 512),
        scratch=[pltpu.VMEM((NX, CY), jnp.float32), pltpu.VMEM((2 * MX, CY), jnp.float32)],
    )[0]
    got = all_to_all(sent, ("gx", "gy")).reshape(DEV, 768)
    sent = local_kernel(
        mix_kernel,
        [shape(DEV, 1, 512)],
        (
            got,
            jnp.asarray(TURN),
            mode_gain.transpose(2, 1, 0, 3),
            lift_weight,
            project_weight.T,
        ),
        flops=6 * 2 * 512 * 128 * 16,
    )[0]

    live = jnp.arange(128, dtype=jnp.int32)[None, :] < counts[0][:, None]
    weight = jnp.where(live, got[:, 640:], 0.0)
    height = got[:, 512:640]
    cut = 112
    w_0, wh_0 = scatter(cell_rows[0, :cut], cell_cols[0, :cut], weight[:cut], height[:cut])

    back = all_to_all(sent, ("gx", "gy")).reshape(DEV, 512)
    back, w_0, wh_0 = lax.optimization_barrier((back, w_0, wh_0))
    blocks = local_kernel(
        backward_kernel,
        [shape(CX, CY)] * GX,
        (back, jnp.asarray(BACK_Y), jnp.asarray(BACK_X)),
        flops=6 * 2 * (512 * NX * CY + 512 * 256 * 512),
        scratch=[pltpu.VMEM((MY, 2 * MX), jnp.float32), pltpu.VMEM((NX, CY), jnp.float32)],
    )
    weight, w_0 = lax.optimization_barrier((weight, w_0))
    w_1, wh_1 = scatter(cell_rows[0, cut:], cell_cols[0, cut:], weight[cut:], height[cut:])
    return tuple(
        local_kernel(
            finish_kernel,
            [shape(F, CX, CY), shape(CX, CY)],
            (stepped, *exchange(blocks), w_0, w_1, wh_0, wh_1),
        )
    )


def solution(mesh):
    return jax.shard_map(
        body,
        mesh=mesh,
        in_specs=(
            P(None, "gx", "gy"),
            P(None, "gx", "gy"),
            P("gx", "gy", None, None),
            P(),
            P(),
            P(("gx", "gy"), None, None),
            P(("gx", "gy"), None, None),
            P(("gx", "gy"), None, None),
            P(("gx", "gy"), None, None),
            P(("gx", "gy"), None),
        ),
        out_specs=(P(None, "gx", "gy"), P("gx", "gy")),
        check_vma=False,
    )
```

```python
import math

import jax
import jax.numpy as jnp
import numpy as np
from jax import lax
from jax.experimental import pallas as pl
from jax.experimental.pallas import tpu as pltpu
from jax.sharding import PartitionSpec as P

MX = 256
MY = 256
NX = 1024
NY = 8192
F = 8
CX = 128
CY = 256
GX = 8
GY = 32
DEV = GX * GY
HALF = MY // 2

time_step = 0.2
diffusion = 0.25
highest = lax.Precision.HIGHEST


ORDER = np.array(
    [GX * gy + 4 * high + low for high in range(2) for low in range(4) for gy in range(GY)]
)


def tables():
    x = np.arange(MX)
    q = np.arange(MX // 2)
    ang = 2.0 * np.pi * (q[:, None] * x[None, :]) / NX
    fore_x = np.concatenate((np.cos(ang), -np.sin(ang)))
    m = np.arange(MX)
    q = np.where(m < MX // 2, m, m - MX)
    ang = 2.0 * np.pi * (x[:, None] * q[None, :]) / NX
    back_x = np.concatenate((np.cos(ang), -np.sin(ang)), axis=1)
    ang = 2.0 * np.pi * np.arange(8) / 8.0
    period = np.stack([np.tile(row[:, None], (1, CY)) for row in (np.cos(ang), -np.sin(ang))])
    ang = 2.0 * np.pi * (ORDER[:, None] * np.arange(CY)[None, :]) / NY
    fore_y = np.concatenate((np.cos(ang), np.sin(ang)))
    back_y = np.concatenate((np.cos(ang.T), np.sin(ang.T)))
    turn = np.zeros((2, 4, 4, GY, 2, 2, 32))
    for quarter in range(4):
        for low in range(4):
            for high in range(2):
                n = 8 * quarter + 4 * high + low
                ang = 2.0 * np.pi * ((n * np.arange(GY)) % GY) / GY
                turn[0, quarter, low, :, :, high] = np.cos(ang)[:, None, None]
                turn[1, quarter, low, :, :, high] = np.sin(ang)[:, None, None]
    turn = turn.reshape(2, 4, 4, GY, 128)
    def pair(array):
        high = array.astype(np.float32).astype(jnp.bfloat16)
        return high, (array - high.astype(np.float64)).astype(np.float32).astype(jnp.bfloat16)

    return (
        *map(pair, (fore_x, back_x, fore_y, back_y)),
        period.astype(np.float32),
        turn.astype(np.float32),
    )


FORE_X, BACK_X, FORE_Y, BACK_Y, PERIOD, TURN = tables()
SCALE_IN = 1.0 / math.sqrt(NX * NY)
SCALE_OUT = 1.0 / math.sqrt(MX * MY)


def all_to_all(array, axis):
    return lax.all_to_all(array, axis, split_axis=0, concat_axis=0, tiled=True)


def dot(a, b, contract=((1,), (0,))):
    return lax.dot_general(
        a, b, (contract, ((), ())), precision=highest, preferred_element_type=jnp.float32
    )


def split_dot(table, b, contract=((1,), (0,))):
    table_high, table_low = table
    b_high = b.astype(jnp.bfloat16)
    b_low = (b - b_high.astype(jnp.float32)).astype(jnp.bfloat16)

    def one(left, right):
        return lax.dot_general(
            left, right, (contract, ((), ())), preferred_element_type=jnp.float32
        )

    return one(table_high, b_high) + (one(table_high, b_low) + one(table_low, b_high))


def shape(*dims):
    return jax.ShapeDtypeStruct(dims, jnp.float32)


def local_kernel(kernel, out_shape, operands, flops=0, scratch=(), in_place=False, limit=24):
    vmem = pl.BlockSpec(memory_space=pltpu.VMEM)
    place = pl.BlockSpec(memory_space=pl.ANY) if in_place else vmem
    size = sum(4 * math.prod(a.shape) for a in (*operands, *out_shape))
    return pl.pallas_call(
        kernel,
        in_specs=[place] * len(operands),
        out_specs=[vmem] * len(out_shape),
        out_shape=out_shape,
        scratch_shapes=scratch,
        compiler_params=pltpu.CompilerParams(vmem_limit_bytes=limit * 1024 * 1024),
        cost_estimate=pl.CostEstimate(flops=flops, bytes_accessed=size, transcendentals=0),
    )(*operands)


def face(speed):
    return (
        time_step * (jnp.maximum(speed, 0.0) + diffusion),
        time_step * (jnp.minimum(speed, 0.0) - diffusion),
    )


def step_kernel(fields_hbm, velocity_hbm, *refs):
    out_ref, last_x_ref, first_x_ref, last_y_ref, first_y_ref = refs[:5]
    block_refs = refs[5:-3]
    fields_ref, velocity_ref, sems = refs[-3:]
    copies = [pltpu.make_async_copy(velocity_hbm, velocity_ref, sems.at[F])]
    copies += [
        pltpu.make_async_copy(fields_hbm.at[f], fields_ref.at[f], sems.at[f]) for f in range(F)
    ]
    for copy in copies:
        copy.start()
    row = lax.broadcasted_iota(jnp.int32, (CX, CY), 0)
    col = lax.broadcasted_iota(jnp.int32, (CX, CY), 1)
    pick_row = lax.broadcasted_iota(jnp.int32, (8, CY), 0)
    pick_col = lax.broadcasted_iota(jnp.int32, (8, CY), 1)
    pick = jnp.where(pick_col == pick_row * (CY - 1), 1.0, 0.0).astype(jnp.float32)
    first_x_ref[...] = jnp.zeros((16, CY), jnp.float32)
    first_y_ref[...] = jnp.zeros((16, CX), jnp.float32)
    copies[0].wait()
    first_x_ref[F : F + 1] = velocity_ref[0, 0:1]
    first_y_ref[F : F + 1] = dot(pick, velocity_ref[1], ((1,), (1,)))[0:1]
    low_w, high_w = (jnp.where(row == 0, 0.0, value) for value in face(velocity_ref[0]))
    low_e, high_e = (
        jnp.where(row == CX - 1, 0.0, pltpu.roll(value, CX - 1, 0)) for value in (low_w, high_w)
    )
    low_s, high_s = (jnp.where(col == 0, 0.0, value) for value in face(velocity_ref[1]))
    low_n, high_n = (
        jnp.where(col == CY - 1, 0.0, pltpu.roll(value, CY - 1, 1)) for value in (low_s, high_s)
    )
    own = 1.0 - low_e + high_w - low_n + high_s
    for f in range(F):
        copies[f + 1].wait()
        block = fields_ref[f]
        ends = dot(pick, block, ((1,), (1,)))
        first_y_ref[f : f + 1] = ends[0:1]
        last_y_ref[f : f + 1] = ends[1:2]
        last_x_ref[f : f + 1] = block[CX - 1 : CX]
        first_x_ref[f : f + 1] = block[0:1]
        out_ref[f] = (
            own * block
            + low_w * pltpu.roll(block, 1, 0)
            - high_e * pltpu.roll(block, CX - 1, 0)
            + low_s * pltpu.roll(block, 1, 1)
            - high_n * pltpu.roll(block, CY - 1, 1)
        )
    for k, ref in enumerate(block_refs):
        f = lax.rem(lax.axis_index("gx") + k, GX)
        ref[0:CX] = out_ref[f]
        ref[CX : CX + 1] = fields_ref[f, 0:1]
        ref[CX + 1 : CX + 2] = fields_ref[f, CX - 1 : CX]
        ref[CX + 2 : CX + 3] = velocity_ref[0, 0:1]
        ref[CX + 3 :] = jnp.zeros((5, CY), jnp.float32)


def side_kernel(first_ref, last_ref, south_ref, north_ref, out_ref):
    gy = lax.axis_index("gy")
    first, second = face(first_ref[F : F + 1])
    low = (first * south_ref[...] + second * first_ref[0:F]) * jnp.where(gy > 0, 1.0, 0.0)
    first, second = face(north_ref[F : F + 1])
    high = (first * last_ref[...] + second * north_ref[0:F]) * jnp.where(gy < GY - 1, 1.0, 0.0)
    for f in range(F):
        out_ref[f, 0:1] = low[f : f + 1]
        out_ref[f, 1:2] = -high[f : f + 1]
        out_ref[f, 2:] = jnp.zeros((6, CX), jnp.float32)


def add_sides(block, sides):
    sides = jnp.transpose(sides)
    col = lax.broadcasted_iota(jnp.int32, (CX, CY), 1)
    return block + jnp.where(
        col == 0, sides[:, 0:1], jnp.where(col == CY - 1, sides[:, 1:2], 0.0)
    )


def quarter_turn(index, t):
    place = lax.rem(index * t, 4)
    cosine = jnp.where(place == 0, 1.0, jnp.where(place == 2, -1.0, 0.0))
    sine = jnp.where(place == 1, 1.0, jnp.where(place == 3, -1.0, 0.0))
    return cosine.astype(jnp.float32), sine.astype(jnp.float32)


def forward_kernel(*refs):
    *block_refs, sides_ref, fore_xh, fore_xl, period_ref, fore_yh, fore_yl, height_ref, weight_ref = (
        refs[:-4]
    )
    out_ref, columns_ref, parts_ref, edges_ref = refs[-4:]
    for k, ref in enumerate(block_refs):
        source = lax.rem(lax.axis_index("gx") + (GX - k), GX)
        columns_ref[pl.ds(pl.multiple_of(source * CX, CX), CX), :] = add_sides(
            ref[0:CX], sides_ref[source]
        )
        edges_ref[source] = ref[CX:]
    for t in range(1, GX):
        first, second = face(edges_ref[t, 2:3])
        flux = first * edges_ref[t - 1, 1:2] + second * edges_ref[t, 0:1]
        columns_ref[t * CX - 1 : t * CX] -= flux
        columns_ref[t * CX : t * CX + 1] += flux
    q = lax.broadcasted_iota(jnp.int32, (HALF, CY), 0)
    real = jnp.zeros((HALF, CY), jnp.float32)
    imag = jnp.zeros((HALF, CY), jnp.float32)
    for t in range(4):
        piece = split_dot((fore_xh[...], fore_xl[...]), columns_ref[t * MX : (t + 1) * MX])
        piece_r, piece_i = piece[:HALF], piece[HALF:]
        if t == 0:
            real, imag = piece_r, piece_i
        else:
            cosine, sine = quarter_turn(q, t)
            real = real + piece_r * cosine + piece_i * sine
            imag = imag + piece_i * cosine - piece_r * sine
    folded = jnp.sum(columns_ref[...].reshape(NX // 8, 8, CY), axis=0)
    last_r = jnp.sum(folded * period_ref[0], axis=0, keepdims=True)
    last_i = jnp.sum(folded * period_ref[1], axis=0, keepdims=True)
    row = lax.broadcasted_iota(jnp.int32, (HALF, HALF), 0)
    col = lax.broadcasted_iota(jnp.int32, (HALF, HALF), 1)
    mirror = jnp.where(row + col == HALF, 1.0, 0.0).astype(jnp.float32)
    parts_ref[0:HALF] = real
    parts_ref[HALF:MX] = jnp.where(q == 0, last_r, dot(mirror, real))
    parts_ref[MX : MX + HALF] = imag
    parts_ref[MX + HALF :] = -jnp.where(q == 0, last_i, dot(mirror, imag))
    mixed = split_dot((fore_yh[...], fore_yl[...]), parts_ref[...], ((1,), (1,)))
    modes = (mixed[:MY, :MX] + mixed[MY:, MX:], mixed[:MY, MX:] - mixed[MY:, :MX])
    group = lax.broadcasted_iota(jnp.int32, (GY, 128), 1) // 32
    for low in range(4):
        for half in range(2):
            tiles = [
                modes[part][high * 128 + low * 32 : high * 128 + low * 32 + 32, half * 128 : half * 128 + 128]
                for part in range(2)
                for high in range(2)
            ]
            for s in range(4):
                gx = 4 * half + s
                value = None
                for k, tile in enumerate(tiles):
                    shift = (32 * (k - s)) % 128
                    moved = pltpu.roll(tile, shift, 1) if shift else tile
                    value = moved if value is None else jnp.where(group == k, moved, value)
                out_ref[gx * GY : (gx + 1) * GY, 0, low * 128 : (low + 1) * 128] = value
    out_ref[:, 0, 512:640] = height_ref[...]
    out_ref[:, 0, 640:768] = weight_ref[...]


def mix_kernel(got_ref, turn_ref, gain_ref, lift_ref, project_ref, out_ref):
    gy = lax.axis_index("gy")
    quarter = lax.rem(gy, 4)
    lane = lax.broadcasted_iota(jnp.int32, (F, 128), 1)
    is_real = lane < 64
    high_zero = (lane // 32) % 2 == 0
    for low in range(4):
        cosine = turn_ref[0, quarter, low]
        sine = turn_ref[1, quarter, low]
        straight, crossed = [], []
        for f in range(F):
            block = got_ref[f * GY : (f + 1) * GY, 0, low * 128 : (low + 1) * 128]
            straight.append(jnp.sum(block * cosine, axis=0, keepdims=True))
            crossed.append(jnp.sum(block * sine, axis=0, keepdims=True))
        crossed = pltpu.roll(jnp.concatenate(crossed, axis=0), 64, 1)
        coeffs = jnp.concatenate(straight, axis=0) + jnp.where(is_real, crossed, -crossed)
        lifted = dot(jnp.transpose(coeffs * SCALE_IN), lift_ref[...])
        mixed_r, mixed_i = [], []
        for high in range(2):
            lift_r = lifted[high * 32 : high * 32 + 32]
            lift_i = lifted[64 + high * 32 : 96 + high * 32]
            gain_r = gain_ref[0, 4 * high + low]
            gain_i = gain_ref[1, 4 * high + low]
            mixed_r.append(gain_r * lift_r - gain_i * lift_i)
            mixed_i.append(gain_r * lift_i + gain_i * lift_r)
        mixed = jnp.concatenate(mixed_r + mixed_i, axis=0)
        outgoing = dot(project_ref[...], mixed, ((1,), (1,)))
        first = high_zero & (gy == 0) if low == 0 else None
        scale = 2.0 * SCALE_OUT if first is None else jnp.where(first, SCALE_OUT, 2.0 * SCALE_OUT)
        outgoing = outgoing * scale
        swapped = pltpu.roll(outgoing, 64, 1)
        swapped = jnp.where(is_real, -swapped, swapped)
        for f in range(F):
            out_ref[f * GY : (f + 1) * GY, 0, low * 128 : (low + 1) * 128] = (
                outgoing[f : f + 1] * cosine + swapped[f : f + 1] * sine
            )


def backward_kernel(got_ref, back_yh, back_yl, back_xh, back_xl, *refs):
    *out_refs, modes_ref, field_ref = refs
    group = lax.broadcasted_iota(jnp.int32, (GY, 128), 1) // 32
    for low in range(4):
        for half in range(2):
            tiles = [
                got_ref[gx * GY : (gx + 1) * GY, 0, low * 128 : (low + 1) * 128]
                for gx in range(4 * half, 4 * half + 4)
            ]
            for part in range(2):
                for high in range(2):
                    k = 2 * part + high
                    value = None
                    for s, tile in enumerate(tiles):
                        shift = (32 * (s - k)) % 128
                        moved = pltpu.roll(tile, shift, 1) if shift else tile
                        value = moved if value is None else jnp.where(group == s, moved, value)
                    lanes = part * MX + half * 128
                    start = high * 128 + low * 32
                    modes_ref[start : start + 32, lanes : lanes + 128] = value
    mixed = split_dot((back_yh[...], back_yl[...]), modes_ref[...])
    real = mixed[:CY, :MX] - mixed[CY:, MX:]
    imag = mixed[:CY, MX:] + mixed[CY:, :MX]
    index = lax.broadcasted_iota(jnp.int32, (CY, MX), 1)
    for t in range(4):
        if t == 0:
            turned = jnp.concatenate((real, imag), axis=1)
        else:
            cosine, sine = quarter_turn(index, t)
            turned = jnp.concatenate(
                (real * cosine - imag * sine, imag * cosine + real * sine), axis=1
            )
        field_ref[t * MX : (t + 1) * MX] = split_dot(
            (back_xh[...], back_xl[...]), turned, ((1,), (1,))
        )
    for k, ref in enumerate(out_refs):
        owner = lax.rem(lax.axis_index("gx") + k, GX)
        ref[...] = field_ref[pl.ds(pl.multiple_of(owner * CX, CX), CX), :]


def finish_kernel(*refs):
    stepped_ref, *block_refs, sides_ref, west_ref, east_ref, first_ref, last_ref = refs[:-6]
    w_0, w_1, wh_0, wh_1 = refs[-6:-2]
    out_ref, gradient_ref = refs[-2:]
    gx = lax.axis_index("gx")
    for k, ref in enumerate(block_refs):
        f = lax.rem(gx + (GX - k), GX)
        out_ref[f] = add_sides(stepped_ref[f] + ref[...], sides_ref[f])
    first, second = face(first_ref[F : F + 1])
    left = (first * west_ref[...] + second * first_ref[0:F]) * jnp.where(gx > 0, 1.0, 0.0)
    first, second = face(east_ref[F : F + 1])
    right = (first * last_ref[...] + second * east_ref[0:F]) * jnp.where(gx < GX - 1, 1.0, 0.0)
    for f in range(F):
        out_ref[f, 0:1] += left[f : f + 1]
        out_ref[f, CX - 1 : CX] -= right[f : f + 1]
    gradient_ref[...] = out_ref[0] * (w_0[...] + w_1[...]) - (wh_0[...] + wh_1[...])


def exchange(blocks):
    moved = {0: blocks[0]}
    for k in (4, 3, 5, 2, 6, 7, 1):
        moved[k] = lax.ppermute(blocks[k], "gx", [(i, (i + k) % GX) for i in range(GX)])
    return [moved[k] for k in range(GX)]


def scatter_kernel(
    rows_ref, cols_ref, live_ref, got_ref, sum_w_ref, sum_wh_ref, a_ref, b_ref, acc_ref
):
    step = pl.program_id(0)
    weight = got_ref[:, 0, 640:] * live_ref[...]
    product = weight * got_ref[:, 0, 512:640]
    pieces = []
    for value in (weight, product):
        for _ in range(3):
            piece = value.astype(jnp.bfloat16)
            pieces.append(piece)
            value = value - piece.astype(jnp.float32)
    rows = rows_ref[...].astype(jnp.float32).astype(jnp.bfloat16)
    cols = cols_ref[...].astype(jnp.float32).astype(jnp.bfloat16)
    spot_r = lax.broadcasted_iota(jnp.int32, (CX, 128), 0).astype(jnp.float32).astype(jnp.bfloat16)
    spot_c = lax.broadcasted_iota(jnp.int32, (CY, 128), 0).astype(jnp.float32).astype(jnp.bfloat16)
    zero = jnp.zeros((CX, 128), jnp.bfloat16)
    one_c = jnp.ones((CY, 128), jnp.bfloat16)
    zero_c = jnp.zeros((CY, 128), jnp.bfloat16)
    for s in range(rows.shape[0]):
        lanes = pl.ds(s * 128, 128)
        hit = spot_r == jnp.broadcast_to(rows[s : s + 1], (CX, 128))
        for k, piece in enumerate(pieces):
            a_ref[pl.ds(k * CX, CX), lanes] = jnp.where(
                hit, jnp.broadcast_to(piece[s : s + 1], (CX, 128)), zero
            )
        hit = spot_c == jnp.broadcast_to(cols[s : s + 1], (CY, 128))
        b_ref[:, lanes] = jnp.where(hit, one_c, zero_c)
    part = lax.dot_general(
        a_ref[...], b_ref[...], (((1,), (1,)), ((), ())), preferred_element_type=jnp.float32
    )

    @pl.when(step == 0)
    def _():
        acc_ref[...] = part

    @pl.when(step > 0)
    def _():
        acc_ref[...] += part

    @pl.when(step == pl.num_programs(0) - 1)
    def _():
        sum_w_ref[...] = acc_ref[0:CX] + acc_ref[CX : 2 * CX] + acc_ref[2 * CX : 3 * CX]
        sum_wh_ref[...] = (
            acc_ref[3 * CX : 4 * CX] + acc_ref[4 * CX : 5 * CX] + acc_ref[5 * CX : 6 * CX]
        )


def scatter(rows, cols, live, got, start, stop, chunk):
    steps = (stop - start) // chunk
    block = pl.BlockSpec((chunk, 128), lambda i: (start // chunk + i, 0))
    whole = pl.BlockSpec((CX, CY), lambda i: (0, 0))
    return pl.pallas_call(
        scatter_kernel,
        grid=(steps,),
        in_specs=[block] * 3 + [pl.BlockSpec((chunk, 1, 768), lambda i: (start // chunk + i, 0, 0))],
        out_specs=[whole, whole],
        out_shape=[shape(CX, CY)] * 2,
        scratch_shapes=[
            pltpu.VMEM((6 * CX, chunk * 128), jnp.bfloat16),
            pltpu.VMEM((CY, chunk * 128), jnp.bfloat16),
            pltpu.VMEM((6 * CX, CY), jnp.float32),
        ],
        compiler_params=pltpu.CompilerParams(vmem_limit_bytes=32 * 1024 * 1024),
        cost_estimate=pl.CostEstimate(
            flops=2 * 6 * CX * CY * 128 * (stop - start),
            bytes_accessed=4 * 128 * 4 * (stop - start),
            transcendentals=0,
        ),
    )(rows, cols, live, got)


def body(
    fields,
    velocity,
    mode_gain,
    lift_weight,
    project_weight,
    obs_height,
    obs_weight,
    cell_rows,
    cell_cols,
    counts,
):
    up_x = [(i, i + 1) for i in range(GX - 1)]
    down_x = [(i + 1, i) for i in range(GX - 1)]
    up_y = [(i, i + 1) for i in range(GY - 1)]
    down_y = [(i + 1, i) for i in range(GY - 1)]
    stepped, last_x, first_x, last_y, first_y, *blocks = local_kernel(
        step_kernel,
        [shape(F, CX, CY), shape(F, CY), shape(16, CY), shape(F, CX), shape(16, CX)]
        + [shape(CX + 8, CY)] * GX,
        (fields, velocity),
        scratch=[
            pltpu.VMEM((F, CX, CY), jnp.float32),
            pltpu.VMEM((2, CX, CY), jnp.float32),
            pltpu.SemaphoreType.DMA((F + 1,)),
        ],
        in_place=True,
        limit=56,
    )
    south = lax.ppermute(last_y, "gy", up_y)
    north = lax.ppermute(first_y, "gy", down_y)
    blocks = exchange(blocks)
    sides = local_kernel(side_kernel, [shape(F, 8, CX)], (first_y, last_y, south, north))[0]
    all_sides = all_to_all(sides, "gx")
    sent = local_kernel(
        forward_kernel,
        [shape(DEV, 1, 768)],
        (
            *blocks,
            all_sides,
            *map(jnp.asarray, (*FORE_X, PERIOD, *FORE_Y)),
            obs_height[0],
            obs_weight[0],
        ),
        flops=3 * 2 * (256 * NX * CY + 512 * 256 * 512),
        scratch=[
            pltpu.VMEM((NX, CY), jnp.float32),
            pltpu.VMEM((2 * MX, CY), jnp.float32),
            pltpu.VMEM((GX, 8, CY), jnp.float32),
        ],
    )[0]
    sent, last_x, first_x = lax.optimization_barrier((sent, last_x, first_x))
    west = lax.ppermute(last_x, "gx", up_x)
    east = lax.ppermute(first_x, "gx", down_x)
    got = all_to_all(sent, ("gx", "gy"))
    got, west, east = lax.optimization_barrier((got, west, east))
    sent = local_kernel(
        mix_kernel,
        [shape(DEV, 1, 512)],
        (
            got,
            jnp.asarray(TURN),
            mode_gain.transpose(2, 1, 0, 3),
            lift_weight,
            project_weight.T,
        ),
        flops=6 * 2 * 512 * 128 * 16,
    )[0]

    live = (jnp.arange(128, dtype=jnp.int32)[None, :] < counts[0][:, None]).astype(jnp.float32)
    points = (cell_rows[0], cell_cols[0], live)
    w_0, wh_0 = scatter(*points, got, 0, 224, 56)

    back = all_to_all(sent, ("gx", "gy"))
    back, w_0, wh_0 = lax.optimization_barrier((back, w_0, wh_0))
    blocks = local_kernel(
        backward_kernel,
        [shape(CX, CY)] * GX,
        (back, *map(jnp.asarray, (*BACK_Y, *BACK_X))),
        flops=3 * 2 * (512 * NX * CY + 512 * 256 * 512),
        scratch=[pltpu.VMEM((MY, 2 * MX), jnp.float32), pltpu.VMEM((NX, CY), jnp.float32)],
    )
    got, w_0 = lax.optimization_barrier((got, w_0))
    w_1, wh_1 = scatter(*points, got, 224, 256, 32)
    return tuple(
        local_kernel(
            finish_kernel,
            [shape(F, CX, CY), shape(CX, CY)],
            (
                stepped,
                *exchange(blocks),
                sides,
                west,
                east,
                first_x,
                last_x,
                w_0,
                w_1,
                wh_0,
                wh_1,
            ),
        )
    )


def solution(mesh):
    return jax.shard_map(
        body,
        mesh=mesh,
        in_specs=(
            P(None, "gx", "gy"),
            P(None, "gx", "gy"),
            P("gx", "gy", None, None),
            P(),
            P(),
            P(("gx", "gy"), None, None),
            P(("gx", "gy"), None, None),
            P(("gx", "gy"), None, None),
            P(("gx", "gy"), None, None),
            P(("gx", "gy"), None),
        ),
        out_specs=(P(None, "gx", "gy"), P("gx", "gy")),
        check_vma=False,
    )
```

```python
import math

import jax
import jax.numpy as jnp
import numpy as np
from jax import lax
from jax.experimental import pallas as pl
from jax.experimental.pallas import tpu as pltpu
from jax.sharding import PartitionSpec as P

MX = 256
MY = 256
NX = 1024
NY = 8192
F = 8
CX = 128
CY = 256
GX = 8
GY = 32
DEV = GX * GY
HALF = MY // 2
PARTNERS = (0, 2, 6, 3, 7, 4, 5, 1)

time_step = 0.2
diffusion = 0.25
highest = lax.Precision.HIGHEST


ORDER = np.array(
    [GX * gy + 4 * high + low for high in range(2) for low in range(4) for gy in range(GY)]
)


def tables():
    x = np.arange(MX)
    q = np.arange(MX // 2)
    ang = 2.0 * np.pi * (q[:, None] * x[None, :]) / NX
    fore_x = np.concatenate((np.cos(ang), -np.sin(ang)))
    m = np.arange(MX)
    q = np.where(m < MX // 2, m, m - MX)
    ang = 2.0 * np.pi * (x[:, None] * q[None, :]) / NX
    back_x = np.concatenate((np.cos(ang), -np.sin(ang)))
    ang = 2.0 * np.pi * np.arange(8) / 8.0
    period = np.stack([np.tile(row[:, None], (1, CY)) for row in (np.cos(ang), -np.sin(ang))])
    ang = 2.0 * np.pi * (ORDER[:, None] * np.arange(CY)[None, :]) / NY
    fore_y = np.concatenate((np.cos(ang), np.sin(ang)))
    back_y = np.concatenate((np.cos(ang.T), np.sin(ang.T)))
    turn = np.zeros((2, 4, 4, GY, 2, 2, 32))
    for quarter in range(4):
        for low in range(4):
            for high in range(2):
                n = 8 * quarter + 4 * high + low
                ang = 2.0 * np.pi * ((n * np.arange(GY)) % GY) / GY
                turn[0, quarter, low, :, :, high] = np.cos(ang)[:, None, None]
                turn[1, quarter, low, :, :, high] = np.sin(ang)[:, None, None]
    turn = turn.reshape(2, 4, 4, GY, 128)
    def pair(array):
        high = array.astype(np.float32).astype(jnp.bfloat16)
        return high, (array - high.astype(np.float64)).astype(np.float32).astype(jnp.bfloat16)

    fore = np.concatenate((*pair(fore_x), *pair(fore_y)))
    back = np.concatenate((*pair(back_y), *pair(back_x)))
    return (
        fore,
        back,
        period.astype(np.float32),
        turn.astype(np.float32),
    )


FORE, BACK, PERIOD, TURN = tables()
SCALE_IN = 1.0 / math.sqrt(NX * NY)
SCALE_OUT = 1.0 / math.sqrt(MX * MY)


def all_to_all(array, axis):
    return lax.all_to_all(array, axis, split_axis=0, concat_axis=0, tiled=True)


def dot(a, b, contract=((1,), (0,))):
    return lax.dot_general(
        a, b, (contract, ((), ())), precision=highest, preferred_element_type=jnp.float32
    )


def split_dot(table, b, contract=((1,), (0,))):
    table_high, table_low = table
    b_high = b.astype(jnp.bfloat16)
    b_low = (b - b_high.astype(jnp.float32)).astype(jnp.bfloat16)

    def one(left, right):
        return lax.dot_general(
            left, right, (contract, ((), ())), preferred_element_type=jnp.float32
        )

    return one(table_high, b_high) + (one(table_high, b_low) + one(table_low, b_high))


def shape(*dims):
    return jax.ShapeDtypeStruct(dims, jnp.float32)


def local_kernel(kernel, out_shape, operands, flops=0, scratch=(), in_place=False, limit=24):
    vmem = pl.BlockSpec(memory_space=pltpu.VMEM)
    place = pl.BlockSpec(memory_space=pl.ANY) if in_place else vmem
    size = sum(4 * math.prod(a.shape) for a in (*operands, *out_shape))
    return pl.pallas_call(
        kernel,
        in_specs=[place] * len(operands),
        out_specs=[vmem] * len(out_shape),
        out_shape=out_shape,
        scratch_shapes=scratch,
        compiler_params=pltpu.CompilerParams(vmem_limit_bytes=limit * 1024 * 1024),
        cost_estimate=pl.CostEstimate(flops=flops, bytes_accessed=size, transcendentals=0),
    )(*operands)


def face(speed):
    return (
        time_step * (jnp.maximum(speed, 0.0) + diffusion),
        time_step * (jnp.minimum(speed, 0.0) - diffusion),
    )


def edge_kernel(
    fields_hbm, velocity_hbm, last_x_ref, first_x_ref, last_y_ref, first_y_ref, block_ref, row_ref, sems
):
    copies = [
        pltpu.make_async_copy(fields_hbm.at[f], block_ref.at[f], sems.at[f]) for f in range(F)
    ]
    copies += [
        pltpu.make_async_copy(velocity_hbm.at[1], block_ref.at[F], sems.at[F]),
        pltpu.make_async_copy(velocity_hbm.at[0, pl.ds(0, 8)], row_ref, sems.at[F + 1]),
    ]
    for copy in copies:
        copy.start()
    first_x_ref[F + 1 :] = jnp.zeros((7, CY), jnp.float32)
    lane = lax.broadcasted_iota(jnp.int32, (CX, 128), 1)
    sides = jnp.zeros((CX, 128), jnp.float32)
    for f in range(F + 1):
        copies[f].wait()
        tile = block_ref[f, :, 0:128]
        sides = jnp.where(lane == f, pltpu.roll(tile, f, 1) if f else tile, sides)
        if f < F:
            sides = jnp.where(
                lane == 16 + f, pltpu.roll(block_ref[f, :, 128:256], 17 + f, 1), sides
            )
            last_x_ref[f : f + 1] = block_ref[f, CX - 1 : CX]
            first_x_ref[f : f + 1] = block_ref[f, 0:1]
    sides = jnp.transpose(sides)
    first_y_ref[...] = sides[0:16]
    last_y_ref[...] = sides[16 : 16 + F]
    copies[F + 1].wait()
    first_x_ref[F : F + 1] = row_ref[0:1]


def step_kernel(fields_ref, velocity_ref, south_ref, north_ref, *refs):
    *block_refs, held_ref = refs
    row = lax.broadcasted_iota(jnp.int32, (CX, CY), 0)
    col = lax.broadcasted_iota(jnp.int32, (CX, CY), 1)
    first_col, last_col = col == 0, col == CY - 1
    gx, gy = lax.axis_index("gx"), lax.axis_index("gy")
    open_s = jnp.where(gy > 0, 1.0, 0.0)
    open_n = jnp.where(gy < GY - 1, 1.0, 0.0)
    before = jnp.transpose(south_ref[...])
    after = jnp.transpose(north_ref[...])
    low_w, high_w = (jnp.where(row == 0, 0.0, value) for value in face(velocity_ref[0]))
    low_e, high_e = (
        jnp.where(row == CX - 1, 0.0, pltpu.roll(value, CX - 1, 0)) for value in (low_w, high_w)
    )
    low_s, high_s = (
        jnp.where(first_col, value * open_s, value) for value in face(velocity_ref[1])
    )
    low_n, high_n = (
        jnp.where(last_col, edge * open_n, pltpu.roll(value, CY - 1, 1))
        for value, edge in zip((low_s, high_s), face(after[:, F : F + 1]))
    )
    own = 1.0 - low_e + high_w - low_n + high_s
    for f in range(F):
        block = fields_ref[f]
        south = jnp.where(first_col, before[:, f : f + 1], pltpu.roll(block, 1, 1))
        north = jnp.where(last_col, after[:, f : f + 1], pltpu.roll(block, CY - 1, 1))
        value = (
            own * block
            + low_w * pltpu.roll(block, 1, 0)
            - high_e * pltpu.roll(block, CX - 1, 0)
            + low_s * south
            - high_n * north
        )
        extra = jnp.concatenate(
            (
                block[0:1],
                block[CX - 1 : CX],
                velocity_ref[0, 0:1],
                jnp.zeros((5, CY), jnp.float32),
            ),
            axis=0,
        )
        held_ref[f, 0:CX] = value
        held_ref[f, CX:] = extra
    for k, ref in zip(PARTNERS, block_refs):
        ref[...] = held_ref[lax.bitwise_xor(gx, k)]


def quarter_turn(index, t):
    place = lax.rem(index * t, 4)
    cosine = jnp.where(place == 0, 1.0, jnp.where(place == 2, -1.0, 0.0))
    sine = jnp.where(place == 1, 1.0, jnp.where(place == 3, -1.0, 0.0))
    return cosine.astype(jnp.float32), sine.astype(jnp.float32)


def forward_kernel(*refs):
    *block_refs, table_ref, period_ref, height_ref, weight_ref = refs[:-4]
    out_ref, columns_ref, parts_ref, edges_ref = refs[-4:]
    for k, ref in zip(PARTNERS, block_refs):
        source = lax.bitwise_xor(lax.axis_index("gx"), k)
        columns_ref[pl.ds(pl.multiple_of(source * CX, CX), CX), :] = ref[0:CX]
        edges_ref[source] = ref[CX:]
    for t in range(1, GX):
        first, second = face(edges_ref[t, 2:3])
        flux = first * edges_ref[t - 1, 1:2] + second * edges_ref[t, 0:1]
        columns_ref[t * CX - 1 : t * CX] -= flux
        columns_ref[t * CX : t * CX + 1] += flux
    q = lax.broadcasted_iota(jnp.int32, (HALF, CY), 0)
    real = jnp.zeros((HALF, CY), jnp.float32)
    imag = jnp.zeros((HALF, CY), jnp.float32)
    for t in range(4):
        piece = split_dot(
            (table_ref[0:256], table_ref[256:512]), columns_ref[t * MX : (t + 1) * MX]
        )
        piece_r, piece_i = piece[:HALF], piece[HALF:]
        if t == 0:
            real, imag = piece_r, piece_i
        else:
            cosine, sine = quarter_turn(q, t)
            real = real + piece_r * cosine + piece_i * sine
            imag = imag + piece_i * cosine - piece_r * sine
    folded = jnp.sum(columns_ref[...].reshape(NX // 8, 8, CY), axis=0)
    last_r = jnp.sum(folded * period_ref[0], axis=0, keepdims=True)
    last_i = jnp.sum(folded * period_ref[1], axis=0, keepdims=True)
    row = lax.broadcasted_iota(jnp.int32, (HALF, HALF), 0)
    col = lax.broadcasted_iota(jnp.int32, (HALF, HALF), 1)
    mirror = jnp.where(row + col == HALF, 1.0, 0.0).astype(jnp.float32)
    parts_ref[0:HALF] = real
    parts_ref[HALF:MX] = jnp.where(q == 0, last_r, dot(mirror, real))
    parts_ref[MX : MX + HALF] = imag
    parts_ref[MX + HALF :] = -jnp.where(q == 0, last_i, dot(mirror, imag))
    mixed = split_dot((table_ref[512:1024], table_ref[1024:]), parts_ref[...], ((1,), (1,)))
    modes = (mixed[:MY, :MX] + mixed[MY:, MX:], mixed[:MY, MX:] - mixed[MY:, :MX])
    group = lax.broadcasted_iota(jnp.int32, (GY, 128), 1) // 32
    for low in range(4):
        for half in range(2):
            tiles = [
                modes[part][high * 128 + low * 32 : high * 128 + low * 32 + 32, half * 128 : half * 128 + 128]
                for part in range(2)
                for high in range(2)
            ]
            for s in range(4):
                gx = 4 * half + s
                value = None
                for k, tile in enumerate(tiles):
                    shift = (32 * (k - s)) % 128
                    moved = pltpu.roll(tile, shift, 1) if shift else tile
                    value = moved if value is None else jnp.where(group == k, moved, value)
                out_ref[gx * GY : (gx + 1) * GY, 0, low * 128 : (low + 1) * 128] = value
    out_ref[:, 0, 512:640] = height_ref[...]
    out_ref[:, 0, 640:768] = weight_ref[...]


def mix_kernel(got_ref, turn_ref, gain_ref, lift_ref, project_ref, out_ref):
    gy = lax.axis_index("gy")
    quarter = lax.rem(gy, 4)
    lane = lax.broadcasted_iota(jnp.int32, (F, 128), 1)
    is_real = lane < 64
    high_zero = (lane // 32) % 2 == 0
    for low in range(4):
        cosine = turn_ref[0, quarter, low]
        sine = turn_ref[1, quarter, low]
        straight, crossed = [], []
        for f in range(F):
            block = got_ref[f * GY : (f + 1) * GY, 0, low * 128 : (low + 1) * 128]
            straight.append(jnp.sum(block * cosine, axis=0, keepdims=True))
            crossed.append(jnp.sum(block * sine, axis=0, keepdims=True))
        crossed = pltpu.roll(jnp.concatenate(crossed, axis=0), 64, 1)
        coeffs = jnp.concatenate(straight, axis=0) + jnp.where(is_real, crossed, -crossed)
        lifted = dot(jnp.transpose(coeffs * SCALE_IN), lift_ref[...])
        mixed_r, mixed_i = [], []
        for high in range(2):
            lift_r = lifted[high * 32 : high * 32 + 32]
            lift_i = lifted[64 + high * 32 : 96 + high * 32]
            gain_r = gain_ref[0, 4 * high + low]
            gain_i = gain_ref[1, 4 * high + low]
            mixed_r.append(gain_r * lift_r - gain_i * lift_i)
            mixed_i.append(gain_r * lift_i + gain_i * lift_r)
        mixed = jnp.concatenate(mixed_r + mixed_i, axis=0)
        outgoing = dot(project_ref[...], mixed, ((1,), (1,)))
        first = high_zero & (gy == 0) if low == 0 else None
        scale = 2.0 * SCALE_OUT if first is None else jnp.where(first, SCALE_OUT, 2.0 * SCALE_OUT)
        outgoing = outgoing * scale
        swapped = pltpu.roll(outgoing, 64, 1)
        swapped = jnp.where(is_real, -swapped, swapped)
        for f in range(F):
            out_ref[f * GY : (f + 1) * GY, 0, low * 128 : (low + 1) * 128] = (
                outgoing[f : f + 1] * cosine + swapped[f : f + 1] * sine
            )


def backward_kernel(got_ref, table_ref, *refs):
    *out_refs, modes_ref, field_ref = refs
    group = lax.broadcasted_iota(jnp.int32, (GY, 128), 1) // 32
    for low in range(4):
        for half in range(2):
            tiles = [
                got_ref[gx * GY : (gx + 1) * GY, 0, low * 128 : (low + 1) * 128]
                for gx in range(4 * half, 4 * half + 4)
            ]
            for part in range(2):
                for high in range(2):
                    k = 2 * part + high
                    value = None
                    for s, tile in enumerate(tiles):
                        shift = (32 * (s - k)) % 128
                        moved = pltpu.roll(tile, shift, 1) if shift else tile
                        value = moved if value is None else jnp.where(group == s, moved, value)
                    lanes = part * MX + half * 128
                    start = high * 128 + low * 32
                    modes_ref[start : start + 32, lanes : lanes + 128] = value
    mixed = split_dot((table_ref[0:512], table_ref[512:1024]), modes_ref[...])
    real = mixed[:CY, :MX] - mixed[CY:, MX:]
    imag = mixed[:CY, MX:] + mixed[CY:, :MX]
    index = lax.broadcasted_iota(jnp.int32, (CY, MX), 1)
    for t in range(4):
        turned_r, turned_i = real, imag
        if t:
            cosine, sine = quarter_turn(index, t)
            turned_r = real * cosine - imag * sine
            turned_i = imag * cosine + real * sine
        field_ref[t * MX : (t + 1) * MX] = split_dot(
            (table_ref[1024:1280], table_ref[1536:1792]), turned_r, ((1,), (1,))
        ) + split_dot((table_ref[1280:1536], table_ref[1792:]), turned_i, ((1,), (1,)))
    for k, ref in zip(PARTNERS, out_refs):
        owner = lax.bitwise_xor(lax.axis_index("gx"), k)
        ref[...] = field_ref[pl.ds(pl.multiple_of(owner * CX, CX), CX), :]


def finish_kernel(*refs):
    step_refs, block_refs, refs = refs[:GX], refs[GX : 2 * GX], refs[2 * GX :]
    west_ref, east_ref, first_ref, last_ref, w_0, w_1, wh_0, wh_1, out_ref, gradient_ref = refs
    gx = lax.axis_index("gx")
    for k, step_ref, block_ref in zip(PARTNERS, step_refs, block_refs):
        out_ref[lax.bitwise_xor(gx, k)] = step_ref[0:CX] + block_ref[...]
    first, second = face(first_ref[F : F + 1])
    left = (first * west_ref[...] + second * first_ref[0:F]) * jnp.where(gx > 0, 1.0, 0.0)
    first, second = face(east_ref[F : F + 1])
    right = (first * last_ref[...] + second * east_ref[0:F]) * jnp.where(gx < GX - 1, 1.0, 0.0)
    for f in range(F):
        out_ref[f, 0:1] += left[f : f + 1]
        out_ref[f, CX - 1 : CX] -= right[f : f + 1]
    gradient_ref[...] = out_ref[0] * (w_0[...] + w_1[...]) - (wh_0[...] + wh_1[...])


def exchange(blocks):
    return [blocks[0]] + [
        lax.ppermute(block, "gx", [(i, i ^ k) for i in range(GX)])
        for k, block in zip(PARTNERS[1:], blocks[1:])
    ]


def scatter_kernel(
    rows_ref, cols_ref, live_ref, got_ref, sum_w_ref, sum_wh_ref, a_ref, b_ref, acc_ref
):
    step = pl.program_id(0)
    weight = got_ref[:, 0, 640:] * live_ref[...]
    product = weight * got_ref[:, 0, 512:640]
    pieces = []
    for value in (weight, product):
        for _ in range(3):
            piece = value.astype(jnp.bfloat16)
            pieces.append(piece)
            value = value - piece.astype(jnp.float32)
    rows = rows_ref[...].astype(jnp.float32).astype(jnp.bfloat16)
    cols = cols_ref[...].astype(jnp.float32).astype(jnp.bfloat16)
    spot_r = lax.broadcasted_iota(jnp.int32, (CX, 128), 0).astype(jnp.float32).astype(jnp.bfloat16)
    spot_c = lax.broadcasted_iota(jnp.int32, (CY, 128), 0).astype(jnp.float32).astype(jnp.bfloat16)
    zero = jnp.zeros((CX, 128), jnp.bfloat16)
    one_c = jnp.ones((CY, 128), jnp.bfloat16)
    zero_c = jnp.zeros((CY, 128), jnp.bfloat16)
    for s in range(rows.shape[0]):
        lanes = pl.ds(s * 128, 128)
        hit = spot_r == jnp.broadcast_to(rows[s : s + 1], (CX, 128))
        for k, piece in enumerate(pieces):
            a_ref[pl.ds(k * CX, CX), lanes] = jnp.where(
                hit, jnp.broadcast_to(piece[s : s + 1], (CX, 128)), zero
            )
        hit = spot_c == jnp.broadcast_to(cols[s : s + 1], (CY, 128))
        b_ref[:, lanes] = jnp.where(hit, one_c, zero_c)
    part = lax.dot_general(
        a_ref[...], b_ref[...], (((1,), (1,)), ((), ())), preferred_element_type=jnp.float32
    )

    @pl.when(step == 0)
    def _():
        acc_ref[...] = part

    @pl.when(step > 0)
    def _():
        acc_ref[...] += part

    @pl.when(step == pl.num_programs(0) - 1)
    def _():
        sum_w_ref[...] = acc_ref[0:CX] + acc_ref[CX : 2 * CX] + acc_ref[2 * CX : 3 * CX]
        sum_wh_ref[...] = (
            acc_ref[3 * CX : 4 * CX] + acc_ref[4 * CX : 5 * CX] + acc_ref[5 * CX : 6 * CX]
        )


def scatter(rows, cols, live, got, start, stop, chunk):
    steps = (stop - start) // chunk
    block = pl.BlockSpec((chunk, 128), lambda i: (start // chunk + i, 0))
    whole = pl.BlockSpec((CX, CY), lambda i: (0, 0))
    return pl.pallas_call(
        scatter_kernel,
        grid=(steps,),
        in_specs=[block] * 3 + [pl.BlockSpec((chunk, 1, 768), lambda i: (start // chunk + i, 0, 0))],
        out_specs=[whole, whole],
        out_shape=[shape(CX, CY)] * 2,
        scratch_shapes=[
            pltpu.VMEM((6 * CX, chunk * 128), jnp.bfloat16),
            pltpu.VMEM((CY, chunk * 128), jnp.bfloat16),
            pltpu.VMEM((6 * CX, CY), jnp.float32),
        ],
        compiler_params=pltpu.CompilerParams(vmem_limit_bytes=32 * 1024 * 1024),
        cost_estimate=pl.CostEstimate(
            flops=2 * 6 * CX * CY * 128 * (stop - start),
            bytes_accessed=4 * 128 * 4 * (stop - start),
            transcendentals=0,
        ),
    )(rows, cols, live, got)


def body(
    fields,
    velocity,
    mode_gain,
    lift_weight,
    project_weight,
    obs_height,
    obs_weight,
    cell_rows,
    cell_cols,
    counts,
):
    up_x = [(i, i + 1) for i in range(GX - 1)]
    down_x = [(i + 1, i) for i in range(GX - 1)]
    up_y = [(i, i + 1) for i in range(GY - 1)]
    down_y = [(i + 1, i) for i in range(GY - 1)]
    last_x, first_x, last_y, first_y = local_kernel(
        edge_kernel,
        [shape(F, CY), shape(16, CY), shape(F, CX), shape(16, CX)],
        (fields, velocity),
        scratch=[
            pltpu.VMEM((F + 1, CX, CY), jnp.float32),
            pltpu.VMEM((8, CY), jnp.float32),
            pltpu.SemaphoreType.DMA((F + 2,)),
        ],
        in_place=True,
        limit=56,
    )
    south = lax.ppermute(last_y, "gy", up_y)
    north = lax.ppermute(first_y, "gy", down_y)
    stepped = local_kernel(
        step_kernel,
        [shape(CX + 8, CY)] * GX,
        (fields, velocity, south, north),
        scratch=[pltpu.VMEM((F, CX + 8, CY), jnp.float32)],
    )
    blocks = exchange(stepped)
    sent = local_kernel(
        forward_kernel,
        [shape(DEV, 1, 768)],
        (
            *blocks,
            jnp.asarray(FORE),
            jnp.asarray(PERIOD),
            obs_height[0],
            obs_weight[0],
        ),
        flops=3 * 2 * (256 * NX * CY + 512 * 256 * 512),
        scratch=[
            pltpu.VMEM((NX, CY), jnp.float32),
            pltpu.VMEM((2 * MX, CY), jnp.float32),
            pltpu.VMEM((GX, 8, CY), jnp.float32),
        ],
    )[0]
    sent, last_x, first_x = lax.optimization_barrier((sent, last_x, first_x))
    west = lax.ppermute(last_x, "gx", up_x)
    east = lax.ppermute(first_x, "gx", down_x)
    got = all_to_all(sent, ("gx", "gy"))
    got, west, east = lax.optimization_barrier((got, west, east))
    sent = local_kernel(
        mix_kernel,
        [shape(DEV, 1, 512)],
        (
            got,
            jnp.asarray(TURN),
            mode_gain.transpose(2, 1, 0, 3),
            lift_weight,
            project_weight.T,
        ),
        flops=6 * 2 * 512 * 128 * 16,
    )[0]

    live = (jnp.arange(128, dtype=jnp.int32)[None, :] < counts[0][:, None]).astype(jnp.float32)
    points = (cell_rows[0], cell_cols[0], live)
    w_0, wh_0 = scatter(*points, got, 0, 224, 56)

    back = all_to_all(sent, ("gx", "gy"))
    back, w_0, wh_0 = lax.optimization_barrier((back, w_0, wh_0))
    blocks = local_kernel(
        backward_kernel,
        [shape(CX, CY)] * GX,
        (back, jnp.asarray(BACK)),
        flops=3 * 2 * (512 * NX * CY + 512 * 256 * 512),
        scratch=[pltpu.VMEM((MY, 2 * MX), jnp.float32), pltpu.VMEM((NX, CY), jnp.float32)],
    )
    got, w_0 = lax.optimization_barrier((got, w_0))
    w_1, wh_1 = scatter(*points, got, 224, 256, 32)
    return tuple(
        local_kernel(
            finish_kernel,
            [shape(F, CX, CY), shape(CX, CY)],
            (
                *stepped,
                *exchange(blocks),
                west,
                east,
                first_x,
                last_x,
                w_0,
                w_1,
                wh_0,
                wh_1,
            ),
        )
    )


def solution(mesh):
    return jax.shard_map(
        body,
        mesh=mesh,
        in_specs=(
            P(None, "gx", "gy"),
            P(None, "gx", "gy"),
            P("gx", "gy", None, None),
            P(),
            P(),
            P(("gx", "gy"), None, None),
            P(("gx", "gy"), None, None),
            P(("gx", "gy"), None, None),
            P(("gx", "gy"), None, None),
            P(("gx", "gy"), None),
        ),
        out_specs=(P(None, "gx", "gy"), P("gx", "gy")),
        check_vma=False,
    )
```

```python
import math

import jax
import jax.numpy as jnp
import numpy as np
from jax import lax
from jax.experimental import pallas as pl
from jax.experimental.pallas import tpu as pltpu
from jax.sharding import PartitionSpec as P

MX = 256
MY = 256
NX = 1024
NY = 8192
F = 8
CX = 128
CY = 256
GX = 8
GY = 32
DEV = GX * GY
HALF = MY // 2
PARTNERS = (0, 2, 6, 3, 7, 4, 5, 1)

time_step = 0.2
diffusion = 0.25
highest = lax.Precision.HIGHEST


ORDER = np.array(
    [GX * gy + 4 * high + low for high in range(2) for low in range(4) for gy in range(GY)]
)


def tables():
    x = np.arange(MX)
    q = np.arange(MX // 2)
    ang = 2.0 * np.pi * (q[:, None] * x[None, :]) / NX
    fore_x = np.concatenate((np.cos(ang), -np.sin(ang)))
    m = np.arange(MX)
    q = np.where(m < MX // 2, m, m - MX)
    ang = 2.0 * np.pi * (x[:, None] * q[None, :]) / NX
    back_x = np.concatenate((np.cos(ang), -np.sin(ang)))
    ang = 2.0 * np.pi * np.arange(8) / 8.0
    period = np.stack([np.tile(row[:, None], (1, CY)) for row in (np.cos(ang), -np.sin(ang))])
    ang = 2.0 * np.pi * (ORDER[:, None] * np.arange(CY)[None, :]) / NY
    fore_y = np.concatenate((np.cos(ang), np.sin(ang)))
    back_y = np.concatenate((np.cos(ang.T), np.sin(ang.T)))
    turn = np.zeros((2, 4, 4, GY, 2, 2, 32))
    for quarter in range(4):
        for low in range(4):
            for high in range(2):
                n = 8 * quarter + 4 * high + low
                ang = 2.0 * np.pi * ((n * np.arange(GY)) % GY) / GY
                turn[0, quarter, low, :, :, high] = np.cos(ang)[:, None, None]
                turn[1, quarter, low, :, :, high] = np.sin(ang)[:, None, None]
    turn = turn.reshape(2, 4, 4, GY, 128)
    def pair(array):
        high = array.astype(np.float32).astype(jnp.bfloat16)
        return high, (array - high.astype(np.float64)).astype(np.float32).astype(jnp.bfloat16)

    fore = np.concatenate((*pair(fore_x), *pair(fore_y)))
    back = np.concatenate((*pair(back_y), *pair(back_x)))
    return (
        fore,
        back,
        period.astype(np.float32),
        turn.astype(np.float32),
    )


FORE, BACK, PERIOD, TURN = tables()
SCALE_IN = 1.0 / math.sqrt(NX * NY)
SCALE_OUT = 1.0 / math.sqrt(MX * MY)


def all_to_all(array, axis):
    return lax.all_to_all(array, axis, split_axis=0, concat_axis=0, tiled=True)


def dot(a, b, contract=((1,), (0,))):
    return lax.dot_general(
        a, b, (contract, ((), ())), precision=highest, preferred_element_type=jnp.float32
    )


def split_dot(table, b, contract=((1,), (0,))):
    table_high, table_low = table
    b_high = b.astype(jnp.bfloat16)
    b_low = (b - b_high.astype(jnp.float32)).astype(jnp.bfloat16)

    def one(left, right):
        return lax.dot_general(
            left, right, (contract, ((), ())), preferred_element_type=jnp.float32
        )

    return one(table_high, b_high) + (one(table_high, b_low) + one(table_low, b_high))


def shape(*dims):
    return jax.ShapeDtypeStruct(dims, jnp.float32)


def local_kernel(kernel, out_shape, operands, flops=0, scratch=(), in_place=False, limit=24):
    vmem = pl.BlockSpec(memory_space=pltpu.VMEM)
    place = pl.BlockSpec(memory_space=pl.ANY) if in_place else vmem
    size = sum(4 * math.prod(a.shape) for a in (*operands, *out_shape))
    return pl.pallas_call(
        kernel,
        in_specs=[place] * len(operands),
        out_specs=[vmem] * len(out_shape),
        out_shape=out_shape,
        scratch_shapes=scratch,
        compiler_params=pltpu.CompilerParams(vmem_limit_bytes=limit * 1024 * 1024),
        cost_estimate=pl.CostEstimate(flops=flops, bytes_accessed=size, transcendentals=0),
    )(*operands)


def face(speed):
    return (
        time_step * (jnp.maximum(speed, 0.0) + diffusion),
        time_step * (jnp.minimum(speed, 0.0) - diffusion),
    )


def edge_kernel(
    fields_hbm, velocity_hbm, last_x_ref, first_x_ref, even_ref, odd_ref, block_ref, row_ref, sems
):
    copies = [
        pltpu.make_async_copy(fields_hbm.at[f], block_ref.at[f], sems.at[f]) for f in range(F)
    ]
    copies += [
        pltpu.make_async_copy(velocity_hbm.at[1], block_ref.at[F], sems.at[F]),
        pltpu.make_async_copy(velocity_hbm.at[0, pl.ds(0, 8)], row_ref, sems.at[F + 1]),
    ]
    for copy in copies:
        copy.start()
    first_x_ref[F + 1 :] = jnp.zeros((7, CY), jnp.float32)
    lane = lax.broadcasted_iota(jnp.int32, (CX, 128), 1)
    sides = jnp.zeros((CX, 128), jnp.float32)
    for f in range(F + 1):
        copies[f].wait()
        tile = block_ref[f, :, 0:128]
        sides = jnp.where(lane == f, pltpu.roll(tile, f, 1) if f else tile, sides)
        if f < F:
            sides = jnp.where(
                lane == 16 + f, pltpu.roll(block_ref[f, :, 128:256], 17 + f, 1), sides
            )
            last_x_ref[f : f + 1] = block_ref[f, CX - 1 : CX]
            first_x_ref[f : f + 1] = block_ref[f, 0:1]
    sides = jnp.transpose(sides)
    is_even = lax.rem(lax.axis_index("gy"), 2) == 0
    first, last = sides[0:16], sides[16:32]
    even_ref[...] = jnp.where(is_even, last, first)
    odd_ref[...] = jnp.where(is_even, first, last)
    copies[F + 1].wait()
    first_x_ref[F : F + 1] = row_ref[0:1]


def step_kernel(fields_ref, velocity_ref, even_ref, odd_ref, *refs):
    *block_refs, held_ref = refs
    row = lax.broadcasted_iota(jnp.int32, (CX, CY), 0)
    col = lax.broadcasted_iota(jnp.int32, (CX, CY), 1)
    first_col, last_col = col == 0, col == CY - 1
    gx, gy = lax.axis_index("gx"), lax.axis_index("gy")
    open_s = jnp.where(gy > 0, 1.0, 0.0)
    open_n = jnp.where(gy < GY - 1, 1.0, 0.0)
    is_even = lax.rem(gy, 2) == 0
    before = jnp.transpose(jnp.where(is_even, odd_ref[...], even_ref[...]))
    after = jnp.transpose(jnp.where(is_even, even_ref[...], odd_ref[...]))
    low_w, high_w = (jnp.where(row == 0, 0.0, value) for value in face(velocity_ref[0]))
    low_e, high_e = (
        jnp.where(row == CX - 1, 0.0, pltpu.roll(value, CX - 1, 0)) for value in (low_w, high_w)
    )
    low_s, high_s = (
        jnp.where(first_col, value * open_s, value) for value in face(velocity_ref[1])
    )
    low_n, high_n = (
        jnp.where(last_col, edge * open_n, pltpu.roll(value, CY - 1, 1))
        for value, edge in zip((low_s, high_s), face(after[:, F : F + 1]))
    )
    own = 1.0 - low_e + high_w - low_n + high_s
    for f in range(F):
        block = fields_ref[f]
        south = jnp.where(first_col, before[:, f : f + 1], pltpu.roll(block, 1, 1))
        north = jnp.where(last_col, after[:, f : f + 1], pltpu.roll(block, CY - 1, 1))
        value = (
            own * block
            + low_w * pltpu.roll(block, 1, 0)
            - high_e * pltpu.roll(block, CX - 1, 0)
            + low_s * south
            - high_n * north
        )
        extra = jnp.concatenate(
            (
                block[0:1],
                block[CX - 1 : CX],
                velocity_ref[0, 0:1],
                jnp.zeros((5, CY), jnp.float32),
            ),
            axis=0,
        )
        held_ref[f, 0:CX] = value
        held_ref[f, CX:] = extra
    for k, ref in zip(PARTNERS, block_refs):
        ref[...] = held_ref[lax.bitwise_xor(gx, k)]


def quarter_turn(index, t):
    place = lax.rem(index * t, 4)
    cosine = jnp.where(place == 0, 1.0, jnp.where(place == 2, -1.0, 0.0))
    sine = jnp.where(place == 1, 1.0, jnp.where(place == 3, -1.0, 0.0))
    return cosine.astype(jnp.float32), sine.astype(jnp.float32)


def forward_kernel(*refs):
    *block_refs, table_ref, period_ref, height_ref, weight_ref = refs[:-4]
    out_ref, columns_ref, parts_ref, edges_ref = refs[-4:]
    for k, ref in zip(PARTNERS, block_refs):
        source = lax.bitwise_xor(lax.axis_index("gx"), k)
        columns_ref[pl.ds(pl.multiple_of(source * CX, CX), CX), :] = ref[0:CX]
        edges_ref[source] = ref[CX:]
    for t in range(1, GX):
        first, second = face(edges_ref[t, 2:3])
        flux = first * edges_ref[t - 1, 1:2] + second * edges_ref[t, 0:1]
        columns_ref[t * CX - 1 : t * CX] -= flux
        columns_ref[t * CX : t * CX + 1] += flux
    q = lax.broadcasted_iota(jnp.int32, (HALF, CY), 0)
    real = jnp.zeros((HALF, CY), jnp.float32)
    imag = jnp.zeros((HALF, CY), jnp.float32)
    for t in range(4):
        piece = split_dot(
            (table_ref[0:256], table_ref[256:512]), columns_ref[t * MX : (t + 1) * MX]
        )
        piece_r, piece_i = piece[:HALF], piece[HALF:]
        if t == 0:
            real, imag = piece_r, piece_i
        else:
            cosine, sine = quarter_turn(q, t)
            real = real + piece_r * cosine + piece_i * sine
            imag = imag + piece_i * cosine - piece_r * sine
    folded = jnp.sum(columns_ref[...].reshape(NX // 8, 8, CY), axis=0)
    last_r = jnp.sum(folded * period_ref[0], axis=0, keepdims=True)
    last_i = jnp.sum(folded * period_ref[1], axis=0, keepdims=True)
    row = lax.broadcasted_iota(jnp.int32, (HALF, HALF), 0)
    col = lax.broadcasted_iota(jnp.int32, (HALF, HALF), 1)
    mirror = jnp.where(row + col == HALF, 1.0, 0.0).astype(jnp.float32)
    parts_ref[0:HALF] = real
    parts_ref[HALF:MX] = jnp.where(q == 0, last_r, dot(mirror, real))
    parts_ref[MX : MX + HALF] = imag
    parts_ref[MX + HALF :] = -jnp.where(q == 0, last_i, dot(mirror, imag))
    mixed = split_dot((table_ref[512:1024], table_ref[1024:]), parts_ref[...], ((1,), (1,)))
    modes = (mixed[:MY, :MX] + mixed[MY:, MX:], mixed[:MY, MX:] - mixed[MY:, :MX])
    group = lax.broadcasted_iota(jnp.int32, (GY, 128), 1) // 32
    for low in range(4):
        for half in range(2):
            tiles = [
                modes[part][high * 128 + low * 32 : high * 128 + low * 32 + 32, half * 128 : half * 128 + 128]
                for part in range(2)
                for high in range(2)
            ]
            for s in range(4):
                gx = 4 * half + s
                value = None
                for k, tile in enumerate(tiles):
                    shift = (32 * (k - s)) % 128
                    moved = pltpu.roll(tile, shift, 1) if shift else tile
                    value = moved if value is None else jnp.where(group == k, moved, value)
                out_ref[gx * GY : (gx + 1) * GY, 0, low * 128 : (low + 1) * 128] = value
    out_ref[:, 0, 512:640] = height_ref[...]
    out_ref[:, 0, 640:768] = weight_ref[...]


def mix_kernel(got_ref, turn_ref, gain_ref, lift_ref, project_ref, out_ref):
    gy = lax.axis_index("gy")
    quarter = lax.rem(gy, 4)
    lane = lax.broadcasted_iota(jnp.int32, (F, 128), 1)
    is_real = lane < 64
    high_zero = (lane // 32) % 2 == 0
    for low in range(4):
        cosine = turn_ref[0, quarter, low]
        sine = turn_ref[1, quarter, low]
        straight, crossed = [], []
        for f in range(F):
            block = got_ref[f * GY : (f + 1) * GY, 0, low * 128 : (low + 1) * 128]
            straight.append(jnp.sum(block * cosine, axis=0, keepdims=True))
            crossed.append(jnp.sum(block * sine, axis=0, keepdims=True))
        crossed = pltpu.roll(jnp.concatenate(crossed, axis=0), 64, 1)
        coeffs = jnp.concatenate(straight, axis=0) + jnp.where(is_real, crossed, -crossed)
        lifted = dot(jnp.transpose(coeffs * SCALE_IN), lift_ref[...])
        mixed_r, mixed_i = [], []
        for high in range(2):
            lift_r = lifted[high * 32 : high * 32 + 32]
            lift_i = lifted[64 + high * 32 : 96 + high * 32]
            gain_r = gain_ref[0, 4 * high + low]
            gain_i = gain_ref[1, 4 * high + low]
            mixed_r.append(gain_r * lift_r - gain_i * lift_i)
            mixed_i.append(gain_r * lift_i + gain_i * lift_r)
        mixed = jnp.concatenate(mixed_r + mixed_i, axis=0)
        outgoing = dot(project_ref[...], mixed, ((1,), (1,)))
        first = high_zero & (gy == 0) if low == 0 else None
        scale = 2.0 * SCALE_OUT if first is None else jnp.where(first, SCALE_OUT, 2.0 * SCALE_OUT)
        outgoing = outgoing * scale
        swapped = pltpu.roll(outgoing, 64, 1)
        swapped = jnp.where(is_real, -swapped, swapped)
        for f in range(F):
            out_ref[f * GY : (f + 1) * GY, 0, low * 128 : (low + 1) * 128] = (
                outgoing[f : f + 1] * cosine + swapped[f : f + 1] * sine
            )


def backward_kernel(got_ref, table_ref, *refs):
    *out_refs, modes_ref, field_ref = refs
    group = lax.broadcasted_iota(jnp.int32, (GY, 128), 1) // 32
    for low in range(4):
        for half in range(2):
            tiles = [
                got_ref[gx * GY : (gx + 1) * GY, 0, low * 128 : (low + 1) * 128]
                for gx in range(4 * half, 4 * half + 4)
            ]
            for part in range(2):
                for high in range(2):
                    k = 2 * part + high
                    value = None
                    for s, tile in enumerate(tiles):
                        shift = (32 * (s - k)) % 128
                        moved = pltpu.roll(tile, shift, 1) if shift else tile
                        value = moved if value is None else jnp.where(group == s, moved, value)
                    lanes = part * MX + half * 128
                    start = high * 128 + low * 32
                    modes_ref[start : start + 32, lanes : lanes + 128] = value
    mixed = split_dot((table_ref[0:512], table_ref[512:1024]), modes_ref[...])
    real = mixed[:CY, :MX] - mixed[CY:, MX:]
    imag = mixed[:CY, MX:] + mixed[CY:, :MX]
    index = lax.broadcasted_iota(jnp.int32, (CY, MX), 1)
    for t in range(4):
        turned_r, turned_i = real, imag
        if t:
            cosine, sine = quarter_turn(index, t)
            turned_r = real * cosine - imag * sine
            turned_i = imag * cosine + real * sine
        field_ref[t * MX : (t + 1) * MX] = split_dot(
            (table_ref[1024:1280], table_ref[1536:1792]), turned_r, ((1,), (1,))
        ) + split_dot((table_ref[1280:1536], table_ref[1792:]), turned_i, ((1,), (1,)))
    for k, ref in zip(PARTNERS, out_refs):
        owner = lax.bitwise_xor(lax.axis_index("gx"), k)
        ref[...] = field_ref[pl.ds(pl.multiple_of(owner * CX, CX), CX), :]


def finish_kernel(*refs):
    step_refs, block_refs, refs = refs[:GX], refs[GX : 2 * GX], refs[2 * GX :]
    west_ref, east_ref, first_ref, last_ref, w_0, w_1, wh_0, wh_1, out_ref, gradient_ref = refs
    gx = lax.axis_index("gx")
    for k, step_ref, block_ref in zip(PARTNERS, step_refs, block_refs):
        out_ref[lax.bitwise_xor(gx, k)] = step_ref[0:CX] + block_ref[...]
    first, second = face(first_ref[F : F + 1])
    left = (first * west_ref[...] + second * first_ref[0:F]) * jnp.where(gx > 0, 1.0, 0.0)
    first, second = face(east_ref[F : F + 1])
    right = (first * last_ref[...] + second * east_ref[0:F]) * jnp.where(gx < GX - 1, 1.0, 0.0)
    for f in range(F):
        out_ref[f, 0:1] += left[f : f + 1]
        out_ref[f, CX - 1 : CX] -= right[f : f + 1]
    gradient_ref[...] = out_ref[0] * (w_0[...] + w_1[...]) - (wh_0[...] + wh_1[...])


def exchange(blocks):
    return [blocks[0]] + [
        lax.ppermute(block, "gx", [(i, i ^ k) for i in range(GX)])
        for k, block in zip(PARTNERS[1:], blocks[1:])
    ]


def scatter_kernel(
    rows_ref, cols_ref, live_ref, got_ref, sum_w_ref, sum_wh_ref, a_ref, b_ref, acc_ref
):
    step = pl.program_id(0)
    weight = got_ref[:, 0, 640:] * live_ref[...]
    product = weight * got_ref[:, 0, 512:640]
    pieces = []
    for value in (weight, product):
        for _ in range(3):
            piece = value.astype(jnp.bfloat16)
            pieces.append(piece)
            value = value - piece.astype(jnp.float32)
    rows = rows_ref[...].astype(jnp.float32).astype(jnp.bfloat16)
    cols = cols_ref[...].astype(jnp.float32).astype(jnp.bfloat16)
    spot_r = lax.broadcasted_iota(jnp.int32, (CX, 128), 0).astype(jnp.float32).astype(jnp.bfloat16)
    spot_c = lax.broadcasted_iota(jnp.int32, (CY, 128), 0).astype(jnp.float32).astype(jnp.bfloat16)
    zero = jnp.zeros((CX, 128), jnp.bfloat16)
    one_c = jnp.ones((CY, 128), jnp.bfloat16)
    zero_c = jnp.zeros((CY, 128), jnp.bfloat16)
    for s in range(rows.shape[0]):
        lanes = pl.ds(s * 128, 128)
        hit = spot_r == jnp.broadcast_to(rows[s : s + 1], (CX, 128))
        for k, piece in enumerate(pieces):
            a_ref[pl.ds(k * CX, CX), lanes] = jnp.where(
                hit, jnp.broadcast_to(piece[s : s + 1], (CX, 128)), zero
            )
        hit = spot_c == jnp.broadcast_to(cols[s : s + 1], (CY, 128))
        b_ref[:, lanes] = jnp.where(hit, one_c, zero_c)
    part = lax.dot_general(
        a_ref[...], b_ref[...], (((1,), (1,)), ((), ())), preferred_element_type=jnp.float32
    )

    @pl.when(step == 0)
    def _():
        acc_ref[...] = part

    @pl.when(step > 0)
    def _():
        acc_ref[...] += part

    @pl.when(step == pl.num_programs(0) - 1)
    def _():
        sum_w_ref[...] = acc_ref[0:CX] + acc_ref[CX : 2 * CX] + acc_ref[2 * CX : 3 * CX]
        sum_wh_ref[...] = (
            acc_ref[3 * CX : 4 * CX] + acc_ref[4 * CX : 5 * CX] + acc_ref[5 * CX : 6 * CX]
        )


def scatter(rows, cols, live, got, start, stop, chunk):
    steps = (stop - start) // chunk
    block = pl.BlockSpec((chunk, 128), lambda i: (start // chunk + i, 0))
    whole = pl.BlockSpec((CX, CY), lambda i: (0, 0))
    return pl.pallas_call(
        scatter_kernel,
        grid=(steps,),
        in_specs=[block] * 3 + [pl.BlockSpec((chunk, 1, 768), lambda i: (start // chunk + i, 0, 0))],
        out_specs=[whole, whole],
        out_shape=[shape(CX, CY)] * 2,
        scratch_shapes=[
            pltpu.VMEM((6 * CX, chunk * 128), jnp.bfloat16),
            pltpu.VMEM((CY, chunk * 128), jnp.bfloat16),
            pltpu.VMEM((6 * CX, CY), jnp.float32),
        ],
        compiler_params=pltpu.CompilerParams(vmem_limit_bytes=32 * 1024 * 1024),
        cost_estimate=pl.CostEstimate(
            flops=2 * 6 * CX * CY * 128 * (stop - start),
            bytes_accessed=4 * 128 * 4 * (stop - start),
            transcendentals=0,
        ),
    )(rows, cols, live, got)


def body(
    fields,
    velocity,
    mode_gain,
    lift_weight,
    project_weight,
    obs_height,
    obs_weight,
    cell_rows,
    cell_cols,
    counts,
):
    up_x = [(i, i + 1) for i in range(GX - 1)]
    down_x = [(i + 1, i) for i in range(GX - 1)]
    even_pairs = [(i, i ^ 1) for i in range(GY)]
    odd_pairs = [(i, (i + 1) % GY if i % 2 else (i - 1) % GY) for i in range(GY)]
    last_x, first_x, even, odd = local_kernel(
        edge_kernel,
        [shape(F, CY), shape(16, CY), shape(16, CX), shape(16, CX)],
        (fields, velocity),
        scratch=[
            pltpu.VMEM((F + 1, CX, CY), jnp.float32),
            pltpu.VMEM((8, CY), jnp.float32),
            pltpu.SemaphoreType.DMA((F + 2,)),
        ],
        in_place=True,
        limit=56,
    )
    even = lax.ppermute(even, "gy", even_pairs)
    odd = lax.ppermute(odd, "gy", odd_pairs)
    stepped = local_kernel(
        step_kernel,
        [shape(CX + 8, CY)] * GX,
        (fields, velocity, even, odd),
        scratch=[pltpu.VMEM((F, CX + 8, CY), jnp.float32)],
    )
    blocks = exchange(stepped)
    sent = local_kernel(
        forward_kernel,
        [shape(DEV, 1, 768)],
        (
            *blocks,
            jnp.asarray(FORE),
            jnp.asarray(PERIOD),
            obs_height[0],
            obs_weight[0],
        ),
        flops=3 * 2 * (256 * NX * CY + 512 * 256 * 512),
        scratch=[
            pltpu.VMEM((NX, CY), jnp.float32),
            pltpu.VMEM((2 * MX, CY), jnp.float32),
            pltpu.VMEM((GX, 8, CY), jnp.float32),
        ],
    )[0]
    sent, last_x, first_x = lax.optimization_barrier((sent, last_x, first_x))
    west = lax.ppermute(last_x, "gx", up_x)
    east = lax.ppermute(first_x, "gx", down_x)
    got = all_to_all(sent, ("gx", "gy"))
    got, west, east = lax.optimization_barrier((got, west, east))
    sent = local_kernel(
        mix_kernel,
        [shape(DEV, 1, 512)],
        (
            got,
            jnp.asarray(TURN),
            mode_gain.transpose(2, 1, 0, 3),
            lift_weight,
            project_weight.T,
        ),
        flops=6 * 2 * 512 * 128 * 16,
    )[0]

    live = (jnp.arange(128, dtype=jnp.int32)[None, :] < counts[0][:, None]).astype(jnp.float32)
    points = (cell_rows[0], cell_cols[0], live)
    w_0, wh_0 = scatter(*points, got, 0, 224, 56)

    back = all_to_all(sent, ("gx", "gy"))
    back, w_0, wh_0 = lax.optimization_barrier((back, w_0, wh_0))
    blocks = local_kernel(
        backward_kernel,
        [shape(CX, CY)] * GX,
        (back, jnp.asarray(BACK)),
        flops=3 * 2 * (512 * NX * CY + 512 * 256 * 512),
        scratch=[pltpu.VMEM((MY, 2 * MX), jnp.float32), pltpu.VMEM((NX, CY), jnp.float32)],
    )
    got, w_0 = lax.optimization_barrier((got, w_0))
    w_1, wh_1 = scatter(*points, got, 224, 256, 32)
    return tuple(
        local_kernel(
            finish_kernel,
            [shape(F, CX, CY), shape(CX, CY)],
            (
                *stepped,
                *exchange(blocks),
                west,
                east,
                first_x,
                last_x,
                w_0,
                w_1,
                wh_0,
                wh_1,
            ),
        )
    )


def solution(mesh):
    return jax.shard_map(
        body,
        mesh=mesh,
        in_specs=(
            P(None, "gx", "gy"),
            P(None, "gx", "gy"),
            P("gx", "gy", None, None),
            P(),
            P(),
            P(("gx", "gy"), None, None),
            P(("gx", "gy"), None, None),
            P(("gx", "gy"), None, None),
            P(("gx", "gy"), None, None),
            P(("gx", "gy"), None),
        ),
        out_specs=(P(None, "gx", "gy"), P("gx", "gy")),
        check_vma=False,
    )
```

```python
import math

import jax
import jax.numpy as jnp
import numpy as np
from jax import lax
from jax.experimental import pallas as pl
from jax.experimental.pallas import tpu as pltpu
from jax.sharding import PartitionSpec as P

MX = 256
MY = 256
NX = 1024
NY = 8192
F = 8
CX = 128
CY = 256
GX = 8
GY = 32
DEV = GX * GY
HALF = MY // 2
PARTNERS = (0, 2, 6, 3, 7, 4, 5, 1)
SIDE = 48

time_step = 0.2
diffusion = 0.25
highest = lax.Precision.HIGHEST


ORDER = np.array(
    [GX * gy + 4 * high + low for high in range(2) for low in range(4) for gy in range(GY)]
)


def tables():
    x = np.arange(MX)
    q = np.arange(MX // 2)
    ang = 2.0 * np.pi * (q[:, None] * x[None, :]) / NX
    fore_x = np.concatenate((np.cos(ang), -np.sin(ang)))
    m = np.arange(MX)
    q = np.where(m < MX // 2, m, m - MX)
    ang = 2.0 * np.pi * (x[:, None] * q[None, :]) / NX
    back_x = np.concatenate((np.cos(ang), -np.sin(ang)))
    ang = 2.0 * np.pi * np.arange(8) / 8.0
    period = np.stack([np.tile(row[:, None], (1, CY)) for row in (np.cos(ang), -np.sin(ang))])
    ang = 2.0 * np.pi * (ORDER[:, None] * np.arange(CY)[None, :]) / NY
    fore_y = np.concatenate((np.cos(ang), np.sin(ang)))
    back_y = np.concatenate((np.cos(ang.T), np.sin(ang.T)))
    turn = np.zeros((2, 4, 4, GY, 2, 2, 32))
    for quarter in range(4):
        for low in range(4):
            for high in range(2):
                n = 8 * quarter + 4 * high + low
                ang = 2.0 * np.pi * ((n * np.arange(GY)) % GY) / GY
                turn[0, quarter, low, :, :, high] = np.cos(ang)[:, None, None]
                turn[1, quarter, low, :, :, high] = np.sin(ang)[:, None, None]
    turn = turn.reshape(2, 4, 4, GY, 128)
    def pair(array):
        high = array.astype(np.float32).astype(jnp.bfloat16)
        return high, (array - high.astype(np.float64)).astype(np.float32).astype(jnp.bfloat16)

    fore = np.concatenate((*pair(fore_x), *pair(fore_y)))
    back = np.concatenate((*pair(back_y), *pair(back_x)))
    return (
        fore,
        back,
        period.astype(np.float32),
        turn.astype(np.float32),
    )


FORE, BACK, PERIOD, TURN = tables()
SCALE_IN = 1.0 / math.sqrt(NX * NY)
SCALE_OUT = 1.0 / math.sqrt(MX * MY)


def all_to_all(array, axis):
    return lax.all_to_all(array, axis, split_axis=0, concat_axis=0, tiled=True)


def dot(a, b, contract=((1,), (0,))):
    return lax.dot_general(
        a, b, (contract, ((), ())), precision=highest, preferred_element_type=jnp.float32
    )


def pieces(array):
    high = array.astype(jnp.bfloat16)
    return high, (array - high.astype(jnp.float32)).astype(jnp.bfloat16)


def split_dot(table, b, contract=((1,), (0,))):
    table_high, table_low = table
    b_high, b_low = pieces(b)

    def one(left, right):
        return lax.dot_general(
            left, right, (contract, ((), ())), preferred_element_type=jnp.float32
        )

    return one(table_high, b_high) + (one(table_high, b_low) + one(table_low, b_high))


def shape(*dims):
    return jax.ShapeDtypeStruct(dims, jnp.float32)


def local_kernel(kernel, out_shape, operands, flops=0, scratch=(), in_place=False, limit=16):
    vmem = pl.BlockSpec(memory_space=pltpu.VMEM)
    place = pl.BlockSpec(memory_space=pl.ANY) if in_place else vmem
    size = sum(4 * math.prod(a.shape) for a in (*operands, *out_shape))
    return pl.pallas_call(
        kernel,
        in_specs=[place] * len(operands),
        out_specs=[vmem] * len(out_shape),
        out_shape=out_shape,
        scratch_shapes=scratch,
        compiler_params=pltpu.CompilerParams(vmem_limit_bytes=limit * 1024 * 1024),
        cost_estimate=pl.CostEstimate(flops=flops, bytes_accessed=size, transcendentals=0),
    )(*operands)


def face(speed):
    return (
        time_step * (jnp.maximum(speed, 0.0) + diffusion),
        time_step * (jnp.minimum(speed, 0.0) - diffusion),
    )


def edge_kernel(
    fields_hbm, velocity_hbm, even_x_ref, odd_x_ref, even_ref, odd_ref, block_ref, row_ref, sems
):
    copies = [
        pltpu.make_async_copy(fields_hbm.at[f], block_ref.at[f], sems.at[f]) for f in range(F)
    ]
    copies += [
        pltpu.make_async_copy(velocity_hbm.at[1], block_ref.at[F], sems.at[F]),
        pltpu.make_async_copy(velocity_hbm.at[0, pl.ds(0, 8)], row_ref, sems.at[F + 1]),
    ]
    for copy in copies:
        copy.start()
    lane = lax.broadcasted_iota(jnp.int32, (CX, 128), 1)
    sides = jnp.zeros((CX, 128), jnp.float32)
    for f in range(F + 1):
        copies[f].wait()
        tile = block_ref[f, :, 0:128]
        sides = jnp.where(lane == f, pltpu.roll(tile, f, 1) if f else tile, sides)
        if f < F:
            sides = jnp.where(
                lane == 16 + f, pltpu.roll(block_ref[f, :, 128:256], 17 + f, 1), sides
            )
    sides = jnp.transpose(sides)
    is_even = lax.rem(lax.axis_index("gy"), 2) == 0
    first, last = sides[0:16], sides[16:32]
    even_ref[0:16] = jnp.where(is_even, last, first)
    odd_ref[0:16] = jnp.where(is_even, first, last)
    for ref in (even_ref, odd_ref):
        ref[16:] = jnp.zeros((SIDE - 16, CX), jnp.float32)
    copies[F + 1].wait()
    rest = jnp.zeros((7, CY), jnp.float32)
    first = [block_ref[f, 0:1] for f in range(F)] + [row_ref[0:1], rest]
    last = [block_ref[f, CX - 1 : CX] for f in range(F)] + [row_ref[0:1], rest]
    first, last = jnp.concatenate(first, axis=0), jnp.concatenate(last, axis=0)
    is_even = lax.rem(lax.axis_index("gx"), 2) == 0
    even_x_ref[...] = jnp.where(is_even, last, first)
    odd_x_ref[...] = jnp.where(is_even, first, last)


def step_kernel(fields_ref, velocity_ref, odd_ref, even_ref, odd_x_ref, even_x_ref, *block_refs):
    *block_refs, held_ref = block_refs
    row = lax.broadcasted_iota(jnp.int32, (CX, CY), 0)
    col = lax.broadcasted_iota(jnp.int32, (CX, CY), 1)
    first_row, last_row = row == 0, row == CX - 1
    first_col, last_col = col == 0, col == CY - 1
    gx, gy = lax.axis_index("gx"), lax.axis_index("gy")
    open_w = jnp.where(gx > 0, 1.0, 0.0)
    open_e = jnp.where(gx < GX - 1, 1.0, 0.0)
    open_s = jnp.where(gy > 0, 1.0, 0.0)
    open_n = jnp.where(gy < GY - 1, 1.0, 0.0)
    is_even = lax.rem(gx, 2) == 0
    above = jnp.where(is_even, odd_x_ref[...], even_x_ref[...])
    below = jnp.where(is_even, even_x_ref[...], odd_x_ref[...])
    is_even = lax.rem(gy, 2) == 0
    before = jnp.transpose(jnp.where(is_even, odd_ref[0:16], even_ref[0:16]))
    after = jnp.transpose(jnp.where(is_even, even_ref[0:16], odd_ref[0:16]))
    low_w, high_w = (
        jnp.where(first_row, value * open_w, value) for value in face(velocity_ref[0])
    )
    low_e, high_e = (
        jnp.where(last_row, edge * open_e, pltpu.roll(value, CX - 1, 0))
        for value, edge in zip((low_w, high_w), face(below[F : F + 1]))
    )
    low_s, high_s = (
        jnp.where(first_col, value * open_s, value) for value in face(velocity_ref[1])
    )
    low_n, high_n = (
        jnp.where(last_col, edge * open_n, pltpu.roll(value, CY - 1, 1))
        for value, edge in zip((low_s, high_s), face(after[:, F : F + 1]))
    )
    own = 1.0 - low_e + high_w - low_n + high_s
    for f in range(F):
        block = fields_ref[f]
        west = jnp.where(first_row, above[f : f + 1], pltpu.roll(block, 1, 0))
        east = jnp.where(last_row, below[f : f + 1], pltpu.roll(block, CX - 1, 0))
        south = jnp.where(first_col, before[:, f : f + 1], pltpu.roll(block, 1, 1))
        north = jnp.where(last_col, after[:, f : f + 1], pltpu.roll(block, CY - 1, 1))
        held_ref[f] = (
            own * block + low_w * west - high_e * east + low_s * south - high_n * north
        )
    for k, ref in zip(PARTNERS, block_refs):
        ref[...] = held_ref[lax.bitwise_xor(gx, k)]


def quarter_turn(index, t):
    place = lax.rem(index * t, 4)
    cosine = jnp.where(place == 0, 1.0, jnp.where(place == 2, -1.0, 0.0))
    sine = jnp.where(place == 1, 1.0, jnp.where(place == 3, -1.0, 0.0))
    return cosine.astype(jnp.float32), sine.astype(jnp.float32)


def forward_kernel(*refs):
    *block_refs, table_ref, period_ref, height_ref, weight_ref = refs[:-3]
    out_ref, columns_ref, parts_ref = refs[-3:]
    for k, ref in zip(PARTNERS, block_refs):
        source = lax.bitwise_xor(lax.axis_index("gx"), k)
        columns_ref[pl.ds(pl.multiple_of(source * CX, CX), CX), :] = ref[...]
    q = lax.broadcasted_iota(jnp.int32, (HALF, CY), 0)
    real = jnp.zeros((HALF, CY), jnp.float32)
    imag = jnp.zeros((HALF, CY), jnp.float32)
    for t in range(4):
        piece = split_dot(
            (table_ref[0:256], table_ref[256:512]), columns_ref[t * MX : (t + 1) * MX]
        )
        piece_r, piece_i = piece[:HALF], piece[HALF:]
        if t == 0:
            real, imag = piece_r, piece_i
        else:
            cosine, sine = quarter_turn(q, t)
            real = real + piece_r * cosine + piece_i * sine
            imag = imag + piece_i * cosine - piece_r * sine
    folded = jnp.sum(columns_ref[...].reshape(NX // 8, 8, CY), axis=0)
    last_r = jnp.sum(folded * period_ref[0], axis=0, keepdims=True)
    last_i = jnp.sum(folded * period_ref[1], axis=0, keepdims=True)
    row = lax.broadcasted_iota(jnp.int32, (HALF, HALF), 0)
    col = lax.broadcasted_iota(jnp.int32, (HALF, HALF), 1)
    mirror = jnp.where(row + col == HALF, 1.0, 0.0).astype(jnp.bfloat16)

    def reflect(block):
        high, low = pieces(block)
        return jnp.dot(mirror, high, preferred_element_type=jnp.float32) + jnp.dot(
            mirror, low, preferred_element_type=jnp.float32
        )

    parts_ref[0:HALF] = real
    parts_ref[HALF:MX] = jnp.where(q == 0, last_r, reflect(real))
    parts_ref[MX : MX + HALF] = imag
    parts_ref[MX + HALF :] = -jnp.where(q == 0, last_i, reflect(imag))
    mixed = split_dot((table_ref[512:1024], table_ref[1024:]), parts_ref[...], ((1,), (1,)))
    modes = (mixed[:MY, :MX] + mixed[MY:, MX:], mixed[:MY, MX:] - mixed[MY:, :MX])
    group = lax.broadcasted_iota(jnp.int32, (GY, 128), 1) // 32
    for low in range(4):
        for half in range(2):
            tiles = [
                modes[part][high * 128 + low * 32 : high * 128 + low * 32 + 32, half * 128 : half * 128 + 128]
                for part in range(2)
                for high in range(2)
            ]
            for s in range(4):
                gx = 4 * half + s
                value = None
                for k, tile in enumerate(tiles):
                    shift = (32 * (k - s)) % 128
                    moved = pltpu.roll(tile, shift, 1) if shift else tile
                    value = moved if value is None else jnp.where(group == k, moved, value)
                out_ref[gx * GY : (gx + 1) * GY, 0, low * 128 : (low + 1) * 128] = value
    out_ref[:, 0, 512:640] = height_ref[...]
    out_ref[:, 0, 640:768] = weight_ref[...]


def mix_kernel(got_ref, turn_ref, gain_ref, lift_ref, project_ref, out_ref):
    gy = lax.axis_index("gy")
    quarter = lax.rem(gy, 4)
    lane = lax.broadcasted_iota(jnp.int32, (F, 128), 1)
    is_real = lane < 64
    high_zero = (lane // 32) % 2 == 0
    coeffs = []
    for low in range(4):
        cosine = turn_ref[0, quarter, low]
        sine = turn_ref[1, quarter, low]
        straight, crossed = [], []
        for f in range(F):
            block = got_ref[f * GY : (f + 1) * GY, 0, low * 128 : (low + 1) * 128]
            straight.append(jnp.sum(block * cosine, axis=0, keepdims=True))
            crossed.append(jnp.sum(block * sine, axis=0, keepdims=True))
        crossed = pltpu.roll(jnp.concatenate(crossed, axis=0), 64, 1)
        total = jnp.concatenate(straight, axis=0) + jnp.where(is_real, crossed, -crossed)
        coeffs.append(jnp.transpose(total * SCALE_IN))
    lift_high, lift_low = pieces(lift_ref[...])
    high, low = pieces(jnp.concatenate(coeffs, axis=0))
    lifted = jnp.dot(
        jnp.concatenate((high, high, low), axis=1),
        jnp.concatenate((lift_high, lift_low, lift_high), axis=0),
        preferred_element_type=jnp.float32,
    )
    mixed = []
    for low in range(4):
        part = lifted[low * 128 : (low + 1) * 128]
        mixed_r, mixed_i = [], []
        for high in range(2):
            lift_r = part[high * 32 : high * 32 + 32]
            lift_i = part[64 + high * 32 : 96 + high * 32]
            gain_r = gain_ref[0, 4 * high + low]
            gain_i = gain_ref[1, 4 * high + low]
            mixed_r.append(gain_r * lift_r - gain_i * lift_i)
            mixed_i.append(gain_r * lift_i + gain_i * lift_r)
        mixed += mixed_r + mixed_i
    mixed = jnp.concatenate(mixed, axis=0)
    result = split_dot(pieces(project_ref[...]), mixed, ((1,), (1,)))
    for low in range(4):
        cosine = turn_ref[0, quarter, low]
        sine = turn_ref[1, quarter, low]
        outgoing = result[:, low * 128 : (low + 1) * 128]
        if low == 0:
            first = high_zero & (gy == 0)
            outgoing = outgoing * jnp.where(first, SCALE_OUT, 2.0 * SCALE_OUT)
        else:
            outgoing = outgoing * (2.0 * SCALE_OUT)
        swapped = pltpu.roll(outgoing, 64, 1)
        swapped = jnp.where(is_real, -swapped, swapped)
        for f in range(F):
            out_ref[f * GY : (f + 1) * GY, 0, low * 128 : (low + 1) * 128] = (
                outgoing[f : f + 1] * cosine + swapped[f : f + 1] * sine
            )


def backward_kernel(got_ref, table_ref, *refs):
    *out_refs, modes_ref, field_ref = refs
    group = lax.broadcasted_iota(jnp.int32, (GY, 128), 1) // 32
    for low in range(4):
        for half in range(2):
            tiles = [
                got_ref[gx * GY : (gx + 1) * GY, 0, low * 128 : (low + 1) * 128]
                for gx in range(4 * half, 4 * half + 4)
            ]
            for part in range(2):
                for high in range(2):
                    k = 2 * part + high
                    value = None
                    for s, tile in enumerate(tiles):
                        shift = (32 * (s - k)) % 128
                        moved = pltpu.roll(tile, shift, 1) if shift else tile
                        value = moved if value is None else jnp.where(group == s, moved, value)
                    lanes = part * MX + half * 128
                    start = high * 128 + low * 32
                    modes_ref[start : start + 32, lanes : lanes + 128] = value
    mixed = split_dot((table_ref[0:512], table_ref[512:1024]), modes_ref[...])
    real = mixed[:CY, :MX] - mixed[CY:, MX:]
    imag = mixed[:CY, MX:] + mixed[CY:, :MX]
    index = lax.broadcasted_iota(jnp.int32, (CY, MX), 1)
    for t in range(4):
        turned_r, turned_i = real, imag
        if t:
            cosine, sine = quarter_turn(index, t)
            turned_r = real * cosine - imag * sine
            turned_i = imag * cosine + real * sine
        field_ref[t * MX : (t + 1) * MX] = split_dot(
            (table_ref[1024:1280], table_ref[1536:1792]), turned_r, ((1,), (1,))
        ) + split_dot((table_ref[1280:1536], table_ref[1792:]), turned_i, ((1,), (1,)))
    for k, ref in zip(PARTNERS, out_refs):
        owner = lax.bitwise_xor(lax.axis_index("gx"), k)
        ref[...] = field_ref[pl.ds(pl.multiple_of(owner * CX, CX), CX), :]


def finish_kernel(*refs):
    step_refs, block_refs, refs = refs[:GX], refs[GX : 2 * GX], refs[2 * GX :]
    w_0, w_1, wh_0, wh_1, out_ref, gradient_ref = refs
    gx = lax.axis_index("gx")
    for k, step_ref, block_ref in zip(PARTNERS, step_refs, block_refs):
        out_ref[lax.bitwise_xor(gx, k)] = step_ref[...] + block_ref[...]
    gradient_ref[...] = out_ref[0] * (w_0[...] + w_1[...]) - (wh_0[...] + wh_1[...])


def exchange(blocks):
    return [blocks[0]] + [
        lax.ppermute(block, "gx", [(i, i ^ k) for i in range(GX)])
        for k, block in zip(PARTNERS[1:], blocks[1:])
    ]


def scatter_kernel(
    rows_ref, cols_ref, live_ref, got_ref, sum_w_ref, sum_wh_ref, a_ref, b_ref, acc_ref
):
    step = pl.program_id(0)
    weight = got_ref[:, 0, 640:] * live_ref[...]
    product = weight * got_ref[:, 0, 512:640]
    pieces = []
    for value in (weight, product):
        for _ in range(3):
            piece = value.astype(jnp.bfloat16)
            pieces.append(piece)
            value = value - piece.astype(jnp.float32)
    rows = rows_ref[...].astype(jnp.float32).astype(jnp.bfloat16)
    cols = cols_ref[...].astype(jnp.float32).astype(jnp.bfloat16)
    spot_r = lax.broadcasted_iota(jnp.int32, (CX, 128), 0).astype(jnp.float32).astype(jnp.bfloat16)
    spot_c = lax.broadcasted_iota(jnp.int32, (CY, 128), 0).astype(jnp.float32).astype(jnp.bfloat16)
    zero = jnp.zeros((CX, 128), jnp.bfloat16)
    one_c = jnp.ones((CY, 128), jnp.bfloat16)
    zero_c = jnp.zeros((CY, 128), jnp.bfloat16)
    for s in range(rows.shape[0]):
        lanes = pl.ds(s * 128, 128)
        hit = spot_r == jnp.broadcast_to(rows[s : s + 1], (CX, 128))
        for k, piece in enumerate(pieces):
            a_ref[pl.ds(k * CX, CX), lanes] = jnp.where(
                hit, jnp.broadcast_to(piece[s : s + 1], (CX, 128)), zero
            )
        hit = spot_c == jnp.broadcast_to(cols[s : s + 1], (CY, 128))
        b_ref[:, lanes] = jnp.where(hit, one_c, zero_c)
    part = lax.dot_general(
        a_ref[...], b_ref[...], (((1,), (1,)), ((), ())), preferred_element_type=jnp.float32
    )

    @pl.when(step == 0)
    def _():
        acc_ref[...] = part

    @pl.when(step > 0)
    def _():
        acc_ref[...] += part

    @pl.when(step == pl.num_programs(0) - 1)
    def _():
        sum_w_ref[...] = acc_ref[0:CX] + acc_ref[CX : 2 * CX] + acc_ref[2 * CX : 3 * CX]
        sum_wh_ref[...] = (
            acc_ref[3 * CX : 4 * CX] + acc_ref[4 * CX : 5 * CX] + acc_ref[5 * CX : 6 * CX]
        )


def scatter(rows, cols, live, got, start, stop, chunk):
    steps = (stop - start) // chunk
    block = pl.BlockSpec((chunk, 128), lambda i: (start // chunk + i, 0))
    whole = pl.BlockSpec((CX, CY), lambda i: (0, 0))
    return pl.pallas_call(
        scatter_kernel,
        grid=(steps,),
        in_specs=[block] * 3 + [pl.BlockSpec((chunk, 1, 768), lambda i: (start // chunk + i, 0, 0))],
        out_specs=[whole, whole],
        out_shape=[shape(CX, CY)] * 2,
        scratch_shapes=[
            pltpu.VMEM((6 * CX, chunk * 128), jnp.bfloat16),
            pltpu.VMEM((CY, chunk * 128), jnp.bfloat16),
            pltpu.VMEM((6 * CX, CY), jnp.float32),
        ],
        compiler_params=pltpu.CompilerParams(vmem_limit_bytes=20 * 1024 * 1024),
        cost_estimate=pl.CostEstimate(
            flops=2 * 6 * CX * CY * 128 * (stop - start),
            bytes_accessed=4 * 128 * 4 * (stop - start),
            transcendentals=0,
        ),
    )(rows, cols, live, got)


def body(
    fields,
    velocity,
    mode_gain,
    lift_weight,
    project_weight,
    obs_height,
    obs_weight,
    cell_rows,
    cell_cols,
    counts,
):
    even_pairs_x = [(i, i ^ 1) for i in range(GX)]
    odd_pairs_x = [(i, (i + 1) % GX if i % 2 else (i - 1) % GX) for i in range(GX)]
    even_pairs = [(i, i ^ 1) for i in range(GY)]
    odd_pairs = [(i, (i + 1) % GY if i % 2 else (i - 1) % GY) for i in range(GY)]
    even_x, odd_x, even, odd = local_kernel(
        edge_kernel,
        [shape(16, CY), shape(16, CY), shape(SIDE, CX), shape(SIDE, CX)],
        (fields, velocity),
        scratch=[
            pltpu.VMEM((F + 1, CX, CY), jnp.float32),
            pltpu.VMEM((8, CY), jnp.float32),
            pltpu.SemaphoreType.DMA((F + 2,)),
        ],
        in_place=True,
        limit=56,
    )
    odd = lax.ppermute(odd, "gy", odd_pairs)
    even = lax.ppermute(even, "gy", even_pairs)
    odd_x = lax.ppermute(odd_x, "gx", odd_pairs_x)
    even_x = lax.ppermute(even_x, "gx", even_pairs_x)
    stepped = local_kernel(
        step_kernel,
        [shape(CX, CY)] * GX,
        (fields, velocity, odd, even, odd_x, even_x),
        scratch=[pltpu.VMEM((F, CX, CY), jnp.float32)],
    )
    blocks = exchange(stepped)
    sent = local_kernel(
        forward_kernel,
        [shape(DEV, 1, 768)],
        (
            *blocks,
            jnp.asarray(FORE),
            jnp.asarray(PERIOD),
            obs_height[0],
            obs_weight[0],
        ),
        flops=3 * 2 * (256 * NX * CY + 512 * 256 * 512),
        scratch=[
            pltpu.VMEM((NX, CY), jnp.float32),
            pltpu.VMEM((2 * MX, CY), jnp.float32),
        ],
    )[0]
    got = all_to_all(sent, ("gx", "gy"))
    sent = local_kernel(
        mix_kernel,
        [shape(DEV, 1, 512)],
        (
            got,
            jnp.asarray(TURN),
            mode_gain.transpose(2, 1, 0, 3),
            lift_weight,
            project_weight.T,
        ),
        flops=6 * 2 * 512 * 128 * 16,
    )[0]

    live = (jnp.arange(128, dtype=jnp.int32)[None, :] < counts[0][:, None]).astype(jnp.float32)
    points = (cell_rows[0], cell_cols[0], live)
    w_0, wh_0 = scatter(*points, got, 0, 224, 56)

    back = all_to_all(sent, ("gx", "gy"))
    back, w_0, wh_0 = lax.optimization_barrier((back, w_0, wh_0))
    blocks = local_kernel(
        backward_kernel,
        [shape(CX, CY)] * GX,
        (back, jnp.asarray(BACK)),
        flops=3 * 2 * (512 * NX * CY + 512 * 256 * 512),
        scratch=[pltpu.VMEM((MY, 2 * MX), jnp.float32), pltpu.VMEM((NX, CY), jnp.float32)],
    )
    got, w_0 = lax.optimization_barrier((got, w_0))
    w_1, wh_1 = scatter(*points, got, 224, 256, 32)
    return tuple(
        local_kernel(
            finish_kernel,
            [shape(F, CX, CY), shape(CX, CY)],
            (
                *stepped,
                *exchange(blocks),
                w_0,
                w_1,
                wh_0,
                wh_1,
            ),
        )
    )


def solution(mesh):
    return jax.shard_map(
        body,
        mesh=mesh,
        in_specs=(
            P(None, "gx", "gy"),
            P(None, "gx", "gy"),
            P("gx", "gy", None, None),
            P(),
            P(),
            P(("gx", "gy"), None, None),
            P(("gx", "gy"), None, None),
            P(("gx", "gy"), None, None),
            P(("gx", "gy"), None, None),
            P(("gx", "gy"), None),
        ),
        out_specs=(P(None, "gx", "gy"), P("gx", "gy")),
        check_vma=False,
    )
```

```python
import math

import jax
import jax.numpy as jnp
import numpy as np
from jax import lax
from jax.experimental import pallas as pl
from jax.experimental.pallas import tpu as pltpu
from jax.sharding import PartitionSpec as P

MX = 256
MY = 256
NX = 1024
NY = 8192
F = 8
CX = 128
CY = 256
GX = 8
GY = 32
DEV = GX * GY
HALF = MY // 2
PARTNERS = (0, 2, 6, 3, 7, 4, 5, 1)
SIDE = 48

time_step = 0.2
diffusion = 0.25
highest = lax.Precision.HIGHEST


ORDER = np.array(
    [GX * gy + 4 * high + low for high in range(2) for low in range(4) for gy in range(GY)]
)


def tables():
    x = np.arange(MX)
    q = np.arange(MX // 2)
    ang = 2.0 * np.pi * (q[:, None] * x[None, :]) / NX
    fore_x = np.concatenate((np.cos(ang), -np.sin(ang)))
    m = np.arange(MX)
    q = np.where(m < MX // 2, m, m - MX)
    ang = 2.0 * np.pi * (x[:, None] * q[None, :]) / NX
    back_x = np.concatenate((np.cos(ang), -np.sin(ang)))
    ang = 2.0 * np.pi * np.arange(8) / 8.0
    period = np.stack([np.tile(row[:, None], (1, CY)) for row in (np.cos(ang), -np.sin(ang))])
    ang = 2.0 * np.pi * (ORDER[:, None] * np.arange(CY)[None, :]) / NY
    fore_y = np.concatenate((np.cos(ang), np.sin(ang)))
    back_y = np.concatenate((np.cos(ang.T), np.sin(ang.T)))
    turn = np.zeros((2, 4, 4, GY, 2, 2, 32))
    for quarter in range(4):
        for low in range(4):
            for high in range(2):
                n = 8 * quarter + 4 * high + low
                ang = 2.0 * np.pi * ((n * np.arange(GY)) % GY) / GY
                turn[0, quarter, low, :, :, high] = np.cos(ang)[:, None, None]
                turn[1, quarter, low, :, :, high] = np.sin(ang)[:, None, None]
    turn = turn.reshape(2, 4, 4, GY, 128)
    def pair(array):
        high = array.astype(np.float32).astype(jnp.bfloat16)
        return high, (array - high.astype(np.float64)).astype(np.float32).astype(jnp.bfloat16)

    fore = np.concatenate((*pair(fore_x), *pair(fore_y)))
    back = np.concatenate((*pair(back_y), *pair(back_x)))
    return (
        fore,
        back,
        period.astype(np.float32),
        turn.astype(np.float32),
    )


FORE, BACK, PERIOD, TURN = tables()
SCALE_IN = 1.0 / math.sqrt(NX * NY)
SCALE_OUT = 1.0 / math.sqrt(MX * MY)


def all_to_all(array, axis):
    return lax.all_to_all(array, axis, split_axis=0, concat_axis=0, tiled=True)


def dot(a, b, contract=((1,), (0,))):
    return lax.dot_general(
        a, b, (contract, ((), ())), precision=highest, preferred_element_type=jnp.float32
    )


def pieces(array):
    high = array.astype(jnp.bfloat16)
    return high, (array - high.astype(jnp.float32)).astype(jnp.bfloat16)


def split_dot(table, b, contract=((1,), (0,))):
    table_high, table_low = table
    b_high, b_low = pieces(b)

    def one(left, right):
        return lax.dot_general(
            left, right, (contract, ((), ())), preferred_element_type=jnp.float32
        )

    return one(table_high, b_high) + (one(table_high, b_low) + one(table_low, b_high))


def shape(*dims):
    return jax.ShapeDtypeStruct(dims, jnp.float32)


def local_kernel(kernel, out_shape, operands, flops=0, scratch=(), in_place=False, limit=16):
    vmem = pl.BlockSpec(memory_space=pltpu.VMEM)
    place = pl.BlockSpec(memory_space=pl.ANY) if in_place else vmem
    size = sum(4 * math.prod(a.shape) for a in (*operands, *out_shape))
    return pl.pallas_call(
        kernel,
        in_specs=[place] * len(operands),
        out_specs=[vmem] * len(out_shape),
        out_shape=out_shape,
        scratch_shapes=scratch,
        compiler_params=pltpu.CompilerParams(vmem_limit_bytes=limit * 1024 * 1024),
        cost_estimate=pl.CostEstimate(flops=flops, bytes_accessed=size, transcendentals=0),
    )(*operands)


def face(speed):
    return (
        time_step * (jnp.maximum(speed, 0.0) + diffusion),
        time_step * (jnp.minimum(speed, 0.0) - diffusion),
    )


def edge_kernel(
    fields_hbm, velocity_hbm, even_x_ref, odd_x_ref, even_ref, odd_ref, block_ref, row_ref, sems
):
    copies = [
        pltpu.make_async_copy(fields_hbm.at[f], block_ref.at[f], sems.at[f]) for f in range(F)
    ]
    copies += [
        pltpu.make_async_copy(velocity_hbm.at[1], block_ref.at[F], sems.at[F]),
        pltpu.make_async_copy(velocity_hbm.at[0, pl.ds(0, 8)], row_ref, sems.at[F + 1]),
    ]
    for copy in copies:
        copy.start()
    lane = lax.broadcasted_iota(jnp.int32, (CX, 128), 1)
    sides = jnp.zeros((CX, 128), jnp.float32)
    for f in range(F + 1):
        copies[f].wait()
        tile = block_ref[f, :, 0:128]
        sides = jnp.where(lane == f, pltpu.roll(tile, f, 1) if f else tile, sides)
        if f < F:
            sides = jnp.where(
                lane == 16 + f, pltpu.roll(block_ref[f, :, 128:256], 17 + f, 1), sides
            )
    sides = jnp.transpose(sides)
    is_even = lax.rem(lax.axis_index("gy"), 2) == 0
    first, last = sides[0:16], sides[16:32]
    even_ref[0:16] = jnp.where(is_even, last, first)
    odd_ref[0:16] = jnp.where(is_even, first, last)
    for ref in (even_ref, odd_ref):
        ref[16:] = jnp.zeros((SIDE - 16, CX), jnp.float32)
    copies[F + 1].wait()
    rest = jnp.zeros((7, CY), jnp.float32)
    first = [block_ref[f, 0:1] for f in range(F)] + [row_ref[0:1], rest]
    last = [block_ref[f, CX - 1 : CX] for f in range(F)] + [row_ref[0:1], rest]
    first, last = jnp.concatenate(first, axis=0), jnp.concatenate(last, axis=0)
    is_even = lax.rem(lax.axis_index("gx"), 2) == 0
    even_x_ref[...] = jnp.where(is_even, last, first)
    odd_x_ref[...] = jnp.where(is_even, first, last)


def step_kernel(fields_ref, velocity_ref, odd_ref, even_ref, odd_x_ref, even_x_ref, *block_refs):
    *block_refs, held_ref = block_refs
    row = lax.broadcasted_iota(jnp.int32, (CX, CY), 0)
    col = lax.broadcasted_iota(jnp.int32, (CX, CY), 1)
    first_row, last_row = row == 0, row == CX - 1
    first_col, last_col = col == 0, col == CY - 1
    gx, gy = lax.axis_index("gx"), lax.axis_index("gy")
    open_w = jnp.where(gx > 0, 1.0, 0.0)
    open_e = jnp.where(gx < GX - 1, 1.0, 0.0)
    open_s = jnp.where(gy > 0, 1.0, 0.0)
    open_n = jnp.where(gy < GY - 1, 1.0, 0.0)
    is_even = lax.rem(gx, 2) == 0
    above = jnp.where(is_even, odd_x_ref[...], even_x_ref[...])
    below = jnp.where(is_even, even_x_ref[...], odd_x_ref[...])
    is_even = lax.rem(gy, 2) == 0
    before = jnp.transpose(jnp.where(is_even, odd_ref[0:16], even_ref[0:16]))
    after = jnp.transpose(jnp.where(is_even, even_ref[0:16], odd_ref[0:16]))
    low_w, high_w = (
        jnp.where(first_row, value * open_w, value) for value in face(velocity_ref[0])
    )
    low_e, high_e = (
        jnp.where(last_row, edge * open_e, pltpu.roll(value, CX - 1, 0))
        for value, edge in zip((low_w, high_w), face(below[F : F + 1]))
    )
    low_s, high_s = (
        jnp.where(first_col, value * open_s, value) for value in face(velocity_ref[1])
    )
    low_n, high_n = (
        jnp.where(last_col, edge * open_n, pltpu.roll(value, CY - 1, 1))
        for value, edge in zip((low_s, high_s), face(after[:, F : F + 1]))
    )
    own = 1.0 - low_e + high_w - low_n + high_s
    for f in range(F):
        block = fields_ref[f]
        west = jnp.where(first_row, above[f : f + 1], pltpu.roll(block, 1, 0))
        east = jnp.where(last_row, below[f : f + 1], pltpu.roll(block, CX - 1, 0))
        south = jnp.where(first_col, before[:, f : f + 1], pltpu.roll(block, 1, 1))
        north = jnp.where(last_col, after[:, f : f + 1], pltpu.roll(block, CY - 1, 1))
        held_ref[f] = (
            own * block + low_w * west - high_e * east + low_s * south - high_n * north
        )
    for k, ref in zip(PARTNERS, block_refs):
        ref[...] = held_ref[lax.bitwise_xor(gx, k)]


def quarter_turn(index, t):
    place = lax.rem(index * t, 4)
    cosine = jnp.where(place == 0, 1.0, jnp.where(place == 2, -1.0, 0.0))
    sine = jnp.where(place == 1, 1.0, jnp.where(place == 3, -1.0, 0.0))
    return cosine.astype(jnp.float32), sine.astype(jnp.float32)


def forward_kernel(*refs):
    *block_refs, table_ref, period_ref, height_ref, weight_ref = refs[:-3]
    out_ref, columns_ref, parts_ref = refs[-3:]
    for k, ref in zip(PARTNERS, block_refs):
        source = lax.bitwise_xor(lax.axis_index("gx"), k)
        columns_ref[pl.ds(pl.multiple_of(source * CX, CX), CX), :] = ref[...]
    q = lax.broadcasted_iota(jnp.int32, (HALF, CY), 0)
    real = jnp.zeros((HALF, CY), jnp.float32)
    imag = jnp.zeros((HALF, CY), jnp.float32)
    for t in range(4):
        piece = split_dot(
            (table_ref[0:256], table_ref[256:512]), columns_ref[t * MX : (t + 1) * MX]
        )
        piece_r, piece_i = piece[:HALF], piece[HALF:]
        if t == 0:
            real, imag = piece_r, piece_i
        else:
            cosine, sine = quarter_turn(q, t)
            real = real + piece_r * cosine + piece_i * sine
            imag = imag + piece_i * cosine - piece_r * sine
    folded = jnp.sum(columns_ref[...].reshape(NX // 8, 8, CY), axis=0)
    last_r = jnp.sum(folded * period_ref[0], axis=0, keepdims=True)
    last_i = jnp.sum(folded * period_ref[1], axis=0, keepdims=True)
    row = lax.broadcasted_iota(jnp.int32, (HALF, HALF), 0)
    col = lax.broadcasted_iota(jnp.int32, (HALF, HALF), 1)
    mirror = jnp.where(row + col == HALF, 1.0, 0.0).astype(jnp.bfloat16)

    def reflect(block):
        high, low = pieces(block)
        return jnp.dot(mirror, high, preferred_element_type=jnp.float32) + jnp.dot(
            mirror, low, preferred_element_type=jnp.float32
        )

    parts_ref[0:HALF] = real
    parts_ref[HALF:MX] = jnp.where(q == 0, last_r, reflect(real))
    parts_ref[MX : MX + HALF] = imag
    parts_ref[MX + HALF :] = -jnp.where(q == 0, last_i, reflect(imag))
    mixed = split_dot((table_ref[512:1024], table_ref[1024:]), parts_ref[...], ((1,), (1,)))
    modes = (mixed[:MY, :MX] + mixed[MY:, MX:], mixed[:MY, MX:] - mixed[MY:, :MX])
    group = lax.broadcasted_iota(jnp.int32, (GY, 128), 1) // 32
    for low in range(4):
        for half in range(2):
            tiles = [
                modes[part][high * 128 + low * 32 : high * 128 + low * 32 + 32, half * 128 : half * 128 + 128]
                for part in range(2)
                for high in range(2)
            ]
            for s in range(4):
                gx = 4 * half + s
                value = None
                for k, tile in enumerate(tiles):
                    shift = (32 * (k - s)) % 128
                    moved = pltpu.roll(tile, shift, 1) if shift else tile
                    value = moved if value is None else jnp.where(group == k, moved, value)
                out_ref[gx * GY : (gx + 1) * GY, 0, low * 128 : (low + 1) * 128] = value
    out_ref[:, 0, 512:640] = height_ref[...]
    out_ref[:, 0, 640:768] = weight_ref[...]


def mix_kernel(got_ref, turn_ref, gain_ref, lift_ref, project_ref, out_ref):
    gy = lax.axis_index("gy")
    quarter = lax.rem(gy, 4)
    lane = lax.broadcasted_iota(jnp.int32, (F, 128), 1)
    is_real = lane < 64
    high_zero = (lane // 32) % 2 == 0
    coeffs = []
    for low in range(4):
        cosine = turn_ref[0, quarter, low]
        sine = turn_ref[1, quarter, low]
        straight, crossed = [], []
        for f in range(F):
            block = got_ref[f * GY : (f + 1) * GY, 0, low * 128 : (low + 1) * 128]
            straight.append(jnp.sum(block * cosine, axis=0, keepdims=True))
            crossed.append(jnp.sum(block * sine, axis=0, keepdims=True))
        crossed = pltpu.roll(jnp.concatenate(crossed, axis=0), 64, 1)
        total = jnp.concatenate(straight, axis=0) + jnp.where(is_real, crossed, -crossed)
        coeffs.append(jnp.transpose(total * SCALE_IN))
    lift_high, lift_low = pieces(lift_ref[...])
    high, low = pieces(jnp.concatenate(coeffs, axis=0))
    lifted = jnp.dot(
        jnp.concatenate((high, high, low), axis=1),
        jnp.concatenate((lift_high, lift_low, lift_high), axis=0),
        preferred_element_type=jnp.float32,
    )
    mixed = []
    for low in range(4):
        part = lifted[low * 128 : (low + 1) * 128]
        mixed_r, mixed_i = [], []
        for high in range(2):
            lift_r = part[high * 32 : high * 32 + 32]
            lift_i = part[64 + high * 32 : 96 + high * 32]
            gain_r = gain_ref[0, 4 * high + low]
            gain_i = gain_ref[1, 4 * high + low]
            mixed_r.append(gain_r * lift_r - gain_i * lift_i)
            mixed_i.append(gain_r * lift_i + gain_i * lift_r)
        mixed += mixed_r + mixed_i
    mixed = jnp.concatenate(mixed, axis=0)
    result = split_dot(pieces(project_ref[...]), mixed, ((1,), (1,)))
    for low in range(4):
        cosine = turn_ref[0, quarter, low]
        sine = turn_ref[1, quarter, low]
        outgoing = result[:, low * 128 : (low + 1) * 128]
        if low == 0:
            first = high_zero & (gy == 0)
            outgoing = outgoing * jnp.where(first, SCALE_OUT, 2.0 * SCALE_OUT)
        else:
            outgoing = outgoing * (2.0 * SCALE_OUT)
        swapped = pltpu.roll(outgoing, 64, 1)
        swapped = jnp.where(is_real, -swapped, swapped)
        for f in range(F):
            out_ref[f * GY : (f + 1) * GY, 0, low * 128 : (low + 1) * 128] = (
                outgoing[f : f + 1] * cosine + swapped[f : f + 1] * sine
            )


def backward_kernel(got_ref, table_ref, *refs):
    *out_refs, modes_ref, field_ref = refs
    group = lax.broadcasted_iota(jnp.int32, (GY, 128), 1) // 32
    for low in range(4):
        for half in range(2):
            tiles = [
                got_ref[gx * GY : (gx + 1) * GY, 0, low * 128 : (low + 1) * 128]
                for gx in range(4 * half, 4 * half + 4)
            ]
            for part in range(2):
                for high in range(2):
                    k = 2 * part + high
                    value = None
                    for s, tile in enumerate(tiles):
                        shift = (32 * (s - k)) % 128
                        moved = pltpu.roll(tile, shift, 1) if shift else tile
                        value = moved if value is None else jnp.where(group == s, moved, value)
                    lanes = part * MX + half * 128
                    start = high * 128 + low * 32
                    modes_ref[start : start + 32, lanes : lanes + 128] = value
    mixed = split_dot((table_ref[0:512], table_ref[512:1024]), modes_ref[...])
    real = mixed[:CY, :MX] - mixed[CY:, MX:]
    imag = mixed[:CY, MX:] + mixed[CY:, :MX]
    index = lax.broadcasted_iota(jnp.int32, (CY, MX), 1)
    for t in range(4):
        turned_r, turned_i = real, imag
        if t:
            cosine, sine = quarter_turn(index, t)
            turned_r = real * cosine - imag * sine
            turned_i = imag * cosine + real * sine
        field_ref[t * MX : (t + 1) * MX] = split_dot(
            (table_ref[1024:1280], table_ref[1536:1792]), turned_r, ((1,), (1,))
        ) + split_dot((table_ref[1280:1536], table_ref[1792:]), turned_i, ((1,), (1,)))
    for k, ref in zip(PARTNERS, out_refs):
        owner = lax.bitwise_xor(lax.axis_index("gx"), k)
        ref[...] = field_ref[pl.ds(pl.multiple_of(owner * CX, CX), CX), :]


def finish_kernel(*refs):
    step_refs, block_refs, refs = refs[:GX], refs[GX : 2 * GX], refs[2 * GX :]
    w_0, w_1, wh_0, wh_1, out_ref, gradient_ref = refs
    gx = lax.axis_index("gx")
    for k, step_ref, block_ref in zip(PARTNERS, step_refs, block_refs):
        out_ref[lax.bitwise_xor(gx, k)] = step_ref[...] + block_ref[...]
    gradient_ref[...] = out_ref[0] * (w_0[...] + w_1[...]) - (wh_0[...] + wh_1[...])


def exchange(blocks):
    return [blocks[0]] + [
        lax.ppermute(block, "gx", [(i, i ^ k) for i in range(GX)])
        for k, block in zip(PARTNERS[1:], blocks[1:])
    ]


def scatter_kernel(
    rows_ref, cols_ref, live_ref, got_ref, sum_w_ref, sum_wh_ref, a_ref, b_ref, acc_ref
):
    step = pl.program_id(0)
    weight = got_ref[:, 0, 640:] * live_ref[...]
    product = weight * got_ref[:, 0, 512:640]
    pieces = []
    for value in (weight, product):
        for _ in range(3):
            piece = value.astype(jnp.bfloat16)
            pieces.append(piece)
            value = value - piece.astype(jnp.float32)
    rows = rows_ref[...].astype(jnp.float32).astype(jnp.bfloat16)
    cols = cols_ref[...].astype(jnp.float32).astype(jnp.bfloat16)
    spot_r = lax.broadcasted_iota(jnp.int32, (CX, 128), 0).astype(jnp.float32).astype(jnp.bfloat16)
    spot_c = lax.broadcasted_iota(jnp.int32, (CY, 128), 0).astype(jnp.float32).astype(jnp.bfloat16)
    zero = jnp.zeros((CX, 128), jnp.bfloat16)
    one_c = jnp.ones((CY, 128), jnp.bfloat16)
    zero_c = jnp.zeros((CY, 128), jnp.bfloat16)
    for s in range(rows.shape[0]):
        lanes = pl.ds(s * 128, 128)
        hit = spot_r == jnp.broadcast_to(rows[s : s + 1], (CX, 128))
        for k, piece in enumerate(pieces):
            a_ref[pl.ds(k * CX, CX), lanes] = jnp.where(
                hit, jnp.broadcast_to(piece[s : s + 1], (CX, 128)), zero
            )
        hit = spot_c == jnp.broadcast_to(cols[s : s + 1], (CY, 128))
        b_ref[:, lanes] = jnp.where(hit, one_c, zero_c)
    part = lax.dot_general(
        a_ref[...], b_ref[...], (((1,), (1,)), ((), ())), preferred_element_type=jnp.float32
    )

    @pl.when(step == 0)
    def _():
        acc_ref[...] = part

    @pl.when(step > 0)
    def _():
        acc_ref[...] += part

    @pl.when(step == pl.num_programs(0) - 1)
    def _():
        sum_w_ref[...] = acc_ref[0:CX] + acc_ref[CX : 2 * CX] + acc_ref[2 * CX : 3 * CX]
        sum_wh_ref[...] = (
            acc_ref[3 * CX : 4 * CX] + acc_ref[4 * CX : 5 * CX] + acc_ref[5 * CX : 6 * CX]
        )


def scatter(rows, cols, live, got, start, stop, chunk):
    steps = (stop - start) // chunk
    block = pl.BlockSpec((chunk, 128), lambda i: (start // chunk + i, 0))
    whole = pl.BlockSpec((CX, CY), lambda i: (0, 0))
    return pl.pallas_call(
        scatter_kernel,
        grid=(steps,),
        in_specs=[block] * 3 + [pl.BlockSpec((chunk, 1, 768), lambda i: (start // chunk + i, 0, 0))],
        out_specs=[whole, whole],
        out_shape=[shape(CX, CY)] * 2,
        scratch_shapes=[
            pltpu.VMEM((6 * CX, chunk * 128), jnp.bfloat16),
            pltpu.VMEM((CY, chunk * 128), jnp.bfloat16),
            pltpu.VMEM((6 * CX, CY), jnp.float32),
        ],
        compiler_params=pltpu.CompilerParams(vmem_limit_bytes=20 * 1024 * 1024),
        cost_estimate=pl.CostEstimate(
            flops=2 * 6 * CX * CY * 128 * (stop - start),
            bytes_accessed=4 * 128 * 4 * (stop - start),
            transcendentals=0,
        ),
    )(rows, cols, live, got)


def body(
    fields,
    velocity,
    mode_gain,
    lift_weight,
    project_weight,
    obs_height,
    obs_weight,
    cell_rows,
    cell_cols,
    counts,
):
    even_pairs_x = [(i, i ^ 1) for i in range(GX)]
    odd_pairs_x = [(i, (i + 1) % GX if i % 2 else (i - 1) % GX) for i in range(GX)]
    even_pairs = [(i, i ^ 1) for i in range(GY)]
    odd_pairs = [(i, (i + 1) % GY if i % 2 else (i - 1) % GY) for i in range(GY)]
    even_x, odd_x, even, odd = local_kernel(
        edge_kernel,
        [shape(16, CY), shape(16, CY), shape(SIDE, CX), shape(SIDE, CX)],
        (fields, velocity),
        scratch=[
            pltpu.VMEM((F + 1, CX, CY), jnp.float32),
            pltpu.VMEM((8, CY), jnp.float32),
            pltpu.SemaphoreType.DMA((F + 2,)),
        ],
        in_place=True,
        limit=56,
    )
    odd = lax.ppermute(odd, "gy", odd_pairs)
    even = lax.ppermute(even, "gy", even_pairs)
    odd_x = lax.ppermute(odd_x, "gx", odd_pairs_x)
    even_x = lax.ppermute(even_x, "gx", even_pairs_x)
    stepped = local_kernel(
        step_kernel,
        [shape(CX, CY)] * GX,
        (fields, velocity, odd, even, odd_x, even_x),
        scratch=[pltpu.VMEM((F, CX, CY), jnp.float32)],
    )
    live = (jnp.arange(128, dtype=jnp.int32)[None, :] < counts[0][:, None]).astype(jnp.float32)
    gains = mode_gain.transpose(2, 1, 0, 3)
    project = project_weight.T
    *blocks, live, gains, project = lax.optimization_barrier(
        (*exchange(stepped), live, gains, project)
    )
    sent = local_kernel(
        forward_kernel,
        [shape(DEV, 1, 768)],
        (
            *blocks,
            jnp.asarray(FORE),
            jnp.asarray(PERIOD),
            obs_height[0],
            obs_weight[0],
        ),
        flops=3 * 2 * (256 * NX * CY + 512 * 256 * 512),
        scratch=[
            pltpu.VMEM((NX, CY), jnp.float32),
            pltpu.VMEM((2 * MX, CY), jnp.float32),
        ],
    )[0]
    got = all_to_all(sent, ("gx", "gy"))
    sent = local_kernel(
        mix_kernel,
        [shape(DEV, 1, 512)],
        (
            got,
            jnp.asarray(TURN),
            gains,
            lift_weight,
            project,
        ),
        flops=6 * 2 * 512 * 128 * 16,
    )[0]

    points = (cell_rows[0], cell_cols[0], live)
    w_0, wh_0 = scatter(*points, got, 0, 224, 56)

    back = all_to_all(sent, ("gx", "gy"))
    back, w_0, wh_0 = lax.optimization_barrier((back, w_0, wh_0))
    blocks = local_kernel(
        backward_kernel,
        [shape(CX, CY)] * GX,
        (back, jnp.asarray(BACK)),
        flops=3 * 2 * (512 * NX * CY + 512 * 256 * 512),
        scratch=[pltpu.VMEM((MY, 2 * MX), jnp.float32), pltpu.VMEM((NX, CY), jnp.float32)],
    )
    got, w_0 = lax.optimization_barrier((got, w_0))
    w_1, wh_1 = scatter(*points, got, 224, 256, 32)
    return tuple(
        local_kernel(
            finish_kernel,
            [shape(F, CX, CY), shape(CX, CY)],
            (
                *stepped,
                *exchange(blocks),
                w_0,
                w_1,
                wh_0,
                wh_1,
            ),
        )
    )


def solution(mesh):
    return jax.shard_map(
        body,
        mesh=mesh,
        in_specs=(
            P(None, "gx", "gy"),
            P(None, "gx", "gy"),
            P("gx", "gy", None, None),
            P(),
            P(),
            P(("gx", "gy"), None, None),
            P(("gx", "gy"), None, None),
            P(("gx", "gy"), None, None),
            P(("gx", "gy"), None, None),
            P(("gx", "gy"), None),
        ),
        out_specs=(P(None, "gx", "gy"), P("gx", "gy")),
        check_vma=False,
    )
```

```python
import math

import jax
import jax.numpy as jnp
import numpy as np
from jax import lax
from jax.experimental import pallas as pl
from jax.experimental.pallas import tpu as pltpu
from jax.sharding import PartitionSpec as P

MX = 256
MY = 256
NX = 1024
NY = 8192
F = 8
CX = 128
CY = 256
GX = 8
GY = 32
DEV = GX * GY
HALF = MY // 2
PARTNERS = (0, 2, 6, 3, 7, 4, 5, 1)
SIDE = 48

time_step = 0.2
diffusion = 0.25
highest = lax.Precision.HIGHEST


ORDER = np.array(
    [GX * gy + 4 * high + low for high in range(2) for low in range(4) for gy in range(GY)]
)


def tables():
    x = np.arange(MX)
    q = np.arange(MX // 2)
    ang = 2.0 * np.pi * (q[:, None] * x[None, :]) / NX
    fore_x = np.concatenate((np.cos(ang), -np.sin(ang)))
    back_x = np.concatenate((np.cos(ang.T), -np.sin(ang.T)), axis=1)
    back_x[:, MX // 2] = np.cos(2.0 * np.pi * x / 8.0)
    ang = 2.0 * np.pi * np.arange(8) / 8.0
    period = np.stack([np.tile(row[:, None], (1, CY)) for row in (np.cos(ang), -np.sin(ang))])
    ang = 2.0 * np.pi * (ORDER[:, None] * np.arange(CY)[None, :]) / NY
    fore_y = np.concatenate((np.cos(ang), np.sin(ang)))
    back_y = np.concatenate((np.cos(ang.T), np.sin(ang.T)))
    turn = np.zeros((2, 4, 4, GY, 2, 2, 32))
    for quarter in range(4):
        for low in range(4):
            for high in range(2):
                n = 8 * quarter + 4 * high + low
                ang = 2.0 * np.pi * ((n * np.arange(GY)) % GY) / GY
                turn[0, quarter, low, :, :, high] = np.cos(ang)[:, None, None]
                turn[1, quarter, low, :, :, high] = np.sin(ang)[:, None, None]
    turn = turn.reshape(2, 4, 4, GY, 128)
    def pair(array):
        high = array.astype(np.float32).astype(jnp.bfloat16)
        return high, (array - high.astype(np.float64)).astype(np.float32).astype(jnp.bfloat16)

    fore = np.concatenate((*pair(fore_x), *pair(fore_y)))
    back = np.concatenate((*pair(back_y), *pair(back_x)))
    return (
        fore,
        back,
        period.astype(np.float32),
        turn.astype(np.float32),
    )


FORE, BACK, PERIOD, TURN = tables()
SCALE_IN = 1.0 / math.sqrt(NX * NY)
SCALE_OUT = 1.0 / math.sqrt(MX * MY)


def all_to_all(array, axis):
    return lax.all_to_all(array, axis, split_axis=0, concat_axis=0, tiled=True)


def dot(a, b, contract=((1,), (0,))):
    return lax.dot_general(
        a, b, (contract, ((), ())), precision=highest, preferred_element_type=jnp.float32
    )


def pieces(array):
    high = array.astype(jnp.bfloat16)
    return high, (array - high.astype(jnp.float32)).astype(jnp.bfloat16)


def split_dot(table, b, contract=((1,), (0,))):
    table_high, table_low = table
    b_high, b_low = pieces(b)

    def one(left, right):
        return lax.dot_general(
            left, right, (contract, ((), ())), preferred_element_type=jnp.float32
        )

    return one(table_high, b_high) + (one(table_high, b_low) + one(table_low, b_high))


def shape(*dims):
    return jax.ShapeDtypeStruct(dims, jnp.float32)


def local_kernel(kernel, out_shape, operands, flops=0, scratch=(), in_place=False, limit=16):
    vmem = pl.BlockSpec(memory_space=pltpu.VMEM)
    place = pl.BlockSpec(memory_space=pl.ANY) if in_place else vmem
    size = sum(4 * math.prod(a.shape) for a in (*operands, *out_shape))
    return pl.pallas_call(
        kernel,
        in_specs=[place] * len(operands),
        out_specs=[vmem] * len(out_shape),
        out_shape=out_shape,
        scratch_shapes=scratch,
        compiler_params=pltpu.CompilerParams(vmem_limit_bytes=limit * 1024 * 1024),
        cost_estimate=pl.CostEstimate(flops=flops, bytes_accessed=size, transcendentals=0),
    )(*operands)


def face(speed):
    return (
        time_step * (jnp.maximum(speed, 0.0) + diffusion),
        time_step * (jnp.minimum(speed, 0.0) - diffusion),
    )


def edge_kernel(
    fields_hbm, velocity_hbm, even_x_ref, odd_x_ref, even_ref, odd_ref, block_ref, row_ref, sems
):
    copies = [
        pltpu.make_async_copy(fields_hbm.at[f], block_ref.at[f], sems.at[f]) for f in range(F)
    ]
    copies += [
        pltpu.make_async_copy(velocity_hbm.at[1], block_ref.at[F], sems.at[F]),
        pltpu.make_async_copy(velocity_hbm.at[0, pl.ds(0, 8)], row_ref, sems.at[F + 1]),
    ]
    for copy in copies:
        copy.start()
    lane = lax.broadcasted_iota(jnp.int32, (CX, 128), 1)
    sides = jnp.zeros((CX, 128), jnp.float32)
    for f in range(F + 1):
        copies[f].wait()
        tile = block_ref[f, :, 0:128]
        sides = jnp.where(lane == f, pltpu.roll(tile, f, 1) if f else tile, sides)
        if f < F:
            sides = jnp.where(
                lane == 16 + f, pltpu.roll(block_ref[f, :, 128:256], 17 + f, 1), sides
            )
    sides = jnp.transpose(sides)
    is_even = lax.rem(lax.axis_index("gy"), 2) == 0
    first, last = sides[0:16], sides[16:32]
    even_ref[0:16] = jnp.where(is_even, last, first)
    odd_ref[0:16] = jnp.where(is_even, first, last)
    for ref in (even_ref, odd_ref):
        ref[16:] = jnp.zeros((SIDE - 16, CX), jnp.float32)
    copies[F + 1].wait()
    rest = jnp.zeros((7, CY), jnp.float32)
    first = [block_ref[f, 0:1] for f in range(F)] + [row_ref[0:1], rest]
    last = [block_ref[f, CX - 1 : CX] for f in range(F)] + [row_ref[0:1], rest]
    first, last = jnp.concatenate(first, axis=0), jnp.concatenate(last, axis=0)
    is_even = lax.rem(lax.axis_index("gx"), 2) == 0
    even_x_ref[...] = jnp.where(is_even, last, first)
    odd_x_ref[...] = jnp.where(is_even, first, last)


def step_kernel(fields_ref, velocity_ref, odd_ref, even_ref, odd_x_ref, even_x_ref, *block_refs):
    *block_refs, held_ref = block_refs
    row = lax.broadcasted_iota(jnp.int32, (CX, CY), 0)
    col = lax.broadcasted_iota(jnp.int32, (CX, CY), 1)
    first_row, last_row = row == 0, row == CX - 1
    first_col, last_col = col == 0, col == CY - 1
    gx, gy = lax.axis_index("gx"), lax.axis_index("gy")
    open_w = jnp.where(gx > 0, 1.0, 0.0)
    open_e = jnp.where(gx < GX - 1, 1.0, 0.0)
    open_s = jnp.where(gy > 0, 1.0, 0.0)
    open_n = jnp.where(gy < GY - 1, 1.0, 0.0)
    is_even = lax.rem(gx, 2) == 0
    above = jnp.where(is_even, odd_x_ref[...], even_x_ref[...])
    below = jnp.where(is_even, even_x_ref[...], odd_x_ref[...])
    is_even = lax.rem(gy, 2) == 0
    before = jnp.transpose(jnp.where(is_even, odd_ref[0:16], even_ref[0:16]))
    after = jnp.transpose(jnp.where(is_even, even_ref[0:16], odd_ref[0:16]))
    low_w, high_w = (
        jnp.where(first_row, value * open_w, value) for value in face(velocity_ref[0])
    )
    low_e, high_e = (
        jnp.where(last_row, edge * open_e, pltpu.roll(value, CX - 1, 0))
        for value, edge in zip((low_w, high_w), face(below[F : F + 1]))
    )
    low_s, high_s = (
        jnp.where(first_col, value * open_s, value) for value in face(velocity_ref[1])
    )
    low_n, high_n = (
        jnp.where(last_col, edge * open_n, pltpu.roll(value, CY - 1, 1))
        for value, edge in zip((low_s, high_s), face(after[:, F : F + 1]))
    )
    own = 1.0 - low_e + high_w - low_n + high_s
    for f in range(F):
        block = fields_ref[f]
        west = jnp.where(first_row, above[f : f + 1], pltpu.roll(block, 1, 0))
        east = jnp.where(last_row, below[f : f + 1], pltpu.roll(block, CX - 1, 0))
        south = jnp.where(first_col, before[:, f : f + 1], pltpu.roll(block, 1, 1))
        north = jnp.where(last_col, after[:, f : f + 1], pltpu.roll(block, CY - 1, 1))
        held_ref[f] = (
            own * block + low_w * west - high_e * east + low_s * south - high_n * north
        )
    for k, ref in zip(PARTNERS, block_refs):
        ref[...] = held_ref[lax.bitwise_xor(gx, k)]


def quarter_turn(index, t):
    place = lax.rem(index * t, 4)
    cosine = jnp.where(place == 0, 1.0, jnp.where(place == 2, -1.0, 0.0))
    sine = jnp.where(place == 1, 1.0, jnp.where(place == 3, -1.0, 0.0))
    return cosine.astype(jnp.float32), sine.astype(jnp.float32)


def forward_kernel(*refs):
    *block_refs, table_ref, period_ref, height_ref, weight_ref = refs[:-3]
    out_ref, columns_ref, parts_ref = refs[-3:]
    for k, ref in zip(PARTNERS, block_refs):
        source = lax.bitwise_xor(lax.axis_index("gx"), k)
        columns_ref[pl.ds(pl.multiple_of(source * CX, CX), CX), :] = ref[...]
    q = lax.broadcasted_iota(jnp.int32, (HALF, CY), 0)
    real = jnp.zeros((HALF, CY), jnp.float32)
    imag = jnp.zeros((HALF, CY), jnp.float32)
    for t in range(4):
        piece = split_dot(
            (table_ref[0:256], table_ref[256:512]), columns_ref[t * MX : (t + 1) * MX]
        )
        piece_r, piece_i = piece[:HALF], piece[HALF:]
        if t == 0:
            real, imag = piece_r, piece_i
        else:
            cosine, sine = quarter_turn(q, t)
            real = real + piece_r * cosine + piece_i * sine
            imag = imag + piece_i * cosine - piece_r * sine
    folded = jnp.sum(columns_ref[...].reshape(NX // 8, 8, CY), axis=0)
    last_r = jnp.sum(folded * period_ref[0], axis=0, keepdims=True)
    last_i = jnp.sum(folded * period_ref[1], axis=0, keepdims=True)
    row = lax.broadcasted_iota(jnp.int32, (HALF, HALF), 0)
    col = lax.broadcasted_iota(jnp.int32, (HALF, HALF), 1)
    mirror = jnp.where(row + col == HALF, 1.0, 0.0).astype(jnp.bfloat16)

    def reflect(block):
        high, low = pieces(block)
        return jnp.dot(mirror, high, preferred_element_type=jnp.float32) + jnp.dot(
            mirror, low, preferred_element_type=jnp.float32
        )

    parts_ref[0:HALF] = real
    parts_ref[HALF:MX] = jnp.where(q == 0, last_r, reflect(real))
    parts_ref[MX : MX + HALF] = imag
    parts_ref[MX + HALF :] = -jnp.where(q == 0, last_i, reflect(imag))
    mixed = split_dot((table_ref[512:1024], table_ref[1024:]), parts_ref[...], ((1,), (1,)))
    modes = (mixed[:MY, :MX] + mixed[MY:, MX:], mixed[:MY, MX:] - mixed[MY:, :MX])
    group = lax.broadcasted_iota(jnp.int32, (GY, 128), 1) // 32
    for low in range(4):
        for half in range(2):
            tiles = [
                modes[part][high * 128 + low * 32 : high * 128 + low * 32 + 32, half * 128 : half * 128 + 128]
                for part in range(2)
                for high in range(2)
            ]
            for s in range(4):
                gx = 4 * half + s
                value = None
                for k, tile in enumerate(tiles):
                    shift = (32 * (k - s)) % 128
                    moved = pltpu.roll(tile, shift, 1) if shift else tile
                    value = moved if value is None else jnp.where(group == k, moved, value)
                out_ref[gx * GY : (gx + 1) * GY, 0, low * 128 : (low + 1) * 128] = value
    out_ref[:, 0, 512:640] = height_ref[...]
    out_ref[:, 0, 640:768] = weight_ref[...]


def mix_kernel(got_ref, turn_ref, gain_ref, lift_ref, project_ref, out_ref):
    gy = lax.axis_index("gy")
    quarter = lax.rem(gy, 4)
    lane = lax.broadcasted_iota(jnp.int32, (F, 128), 1)
    is_real = lane < 64
    high_zero = (lane // 32) % 2 == 0
    coeffs = []
    for low in range(4):
        cosine = turn_ref[0, quarter, low]
        sine = turn_ref[1, quarter, low]
        straight, crossed = [], []
        for f in range(F):
            block = got_ref[f * GY : (f + 1) * GY, 0, low * 128 : (low + 1) * 128]
            straight.append(jnp.sum(block * cosine, axis=0, keepdims=True))
            crossed.append(jnp.sum(block * sine, axis=0, keepdims=True))
        crossed = pltpu.roll(jnp.concatenate(crossed, axis=0), 64, 1)
        total = jnp.concatenate(straight, axis=0) + jnp.where(is_real, crossed, -crossed)
        coeffs.append(jnp.transpose(total * SCALE_IN))
    lift_high, lift_low = pieces(lift_ref[...])
    high, low = pieces(jnp.concatenate(coeffs, axis=0))
    lifted = jnp.dot(
        jnp.concatenate((high, high, low), axis=1),
        jnp.concatenate((lift_high, lift_low, lift_high), axis=0),
        preferred_element_type=jnp.float32,
    )
    mixed = []
    for low in range(4):
        part = lifted[low * 128 : (low + 1) * 128]
        mixed_r, mixed_i = [], []
        for high in range(2):
            lift_r = part[high * 32 : high * 32 + 32]
            lift_i = part[64 + high * 32 : 96 + high * 32]
            gain_r = gain_ref[0, 4 * high + low]
            gain_i = gain_ref[1, 4 * high + low]
            mixed_r.append(gain_r * lift_r - gain_i * lift_i)
            mixed_i.append(gain_r * lift_i + gain_i * lift_r)
        mixed += mixed_r + mixed_i
    mixed = jnp.concatenate(mixed, axis=0)
    result = split_dot(pieces(project_ref[...]), mixed, ((1,), (1,)))
    for low in range(4):
        cosine = turn_ref[0, quarter, low]
        sine = turn_ref[1, quarter, low]
        outgoing = result[:, low * 128 : (low + 1) * 128]
        if low == 0:
            first = high_zero & (gy == 0)
            outgoing = outgoing * jnp.where(first, SCALE_OUT, 2.0 * SCALE_OUT)
        else:
            outgoing = outgoing * (2.0 * SCALE_OUT)
        swapped = pltpu.roll(outgoing, 64, 1)
        swapped = jnp.where(is_real, -swapped, swapped)
        for f in range(F):
            out_ref[f * GY : (f + 1) * GY, 0, low * 128 : (low + 1) * 128] = (
                outgoing[f : f + 1] * cosine + swapped[f : f + 1] * sine
            )


def backward_kernel(got_ref, table_ref, *refs):
    *out_refs, modes_ref, field_ref = refs
    group = lax.broadcasted_iota(jnp.int32, (GY, 128), 1) // 32
    for low in range(4):
        for half in range(2):
            tiles = [
                got_ref[gx * GY : (gx + 1) * GY, 0, low * 128 : (low + 1) * 128]
                for gx in range(4 * half, 4 * half + 4)
            ]
            for part in range(2):
                for high in range(2):
                    k = 2 * part + high
                    value = None
                    for s, tile in enumerate(tiles):
                        shift = (32 * (s - k)) % 128
                        moved = pltpu.roll(tile, shift, 1) if shift else tile
                        value = moved if value is None else jnp.where(group == s, moved, value)
                    lanes = part * MX + half * 128
                    start = high * 128 + low * 32
                    modes_ref[start : start + 32, lanes : lanes + 128] = value
    mixed = split_dot((table_ref[0:512], table_ref[512:1024]), modes_ref[...])
    real = mixed[:CY, :MX] - mixed[CY:, MX:]
    imag = mixed[:CY, MX:] + mixed[CY:, :MX]
    row = lax.broadcasted_iota(jnp.int32, (HALF, HALF), 0)
    col = lax.broadcasted_iota(jnp.int32, (HALF, HALF), 1)
    mirror = jnp.where(row + col == HALF, 1.0, 0.0).astype(jnp.bfloat16)

    def reflect(block):
        high, low = pieces(block)
        return jnp.dot(high, mirror, preferred_element_type=jnp.float32) + jnp.dot(
            low, mirror, preferred_element_type=jnp.float32
        )

    index = lax.broadcasted_iota(jnp.int32, (CY, HALF), 1)
    even = real[:, :HALF] + reflect(real[:, HALF:])
    odd = imag[:, :HALF] - reflect(imag[:, HALF:])
    odd = jnp.where(index == 0, real[:, HALF:], odd)
    pick = jnp.where(
        lax.broadcasted_iota(jnp.int32, (16, HALF), 1) == 0, 1.0, 0.0
    ).astype(jnp.bfloat16)
    last = split_dot((pick, jnp.zeros_like(pick)), imag[:, HALF:], ((1,), (1,)))[:8]
    place = lax.broadcasted_iota(jnp.int32, (8, CY), 0)
    sine = jnp.where(place % 4 == 0, 0.0, jnp.where(place % 2 == 0, 1.0, math.sqrt(0.5)))
    last = last * jnp.where(place < 4, sine, -sine)
    for t in range(4):
        turned = (even, odd)
        if t:
            cosine, sine = quarter_turn(index, t)
            turned = (even * cosine - odd * sine, odd * cosine + even * sine)
        block = split_dot(
            (table_ref[1024:1280], table_ref[1280:]),
            jnp.concatenate(turned, axis=1),
            ((1,), (1,)),
        )
        field_ref[t * MX : (t + 1) * MX] = (
            block.reshape(MX // 8, 8, CY) + last[None]
        ).reshape(MX, CY)
    for k, ref in zip(PARTNERS, out_refs):
        owner = lax.bitwise_xor(lax.axis_index("gx"), k)
        ref[...] = field_ref[pl.ds(pl.multiple_of(owner * CX, CX), CX), :]


def finish_kernel(*refs):
    step_refs, block_refs, refs = refs[:GX], refs[GX : 2 * GX], refs[2 * GX :]
    w_0, w_1, wh_0, wh_1, out_ref, gradient_ref = refs
    gx = lax.axis_index("gx")
    for k, step_ref, block_ref in zip(PARTNERS, step_refs, block_refs):
        out_ref[lax.bitwise_xor(gx, k)] = step_ref[...] + block_ref[...]
    gradient_ref[...] = out_ref[0] * (w_0[...] + w_1[...]) - (wh_0[...] + wh_1[...])


def exchange(blocks):
    return [blocks[0]] + [
        lax.ppermute(block, "gx", [(i, i ^ k) for i in range(GX)])
        for k, block in zip(PARTNERS[1:], blocks[1:])
    ]


def scatter_kernel(
    rows_ref, cols_ref, live_ref, got_ref, sum_w_ref, sum_wh_ref, a_ref, b_ref, acc_ref
):
    step = pl.program_id(0)
    weight = got_ref[:, 0, 640:] * live_ref[...]
    product = weight * got_ref[:, 0, 512:640]
    pieces = []
    for value in (weight, product):
        for _ in range(3):
            piece = value.astype(jnp.bfloat16)
            pieces.append(piece)
            value = value - piece.astype(jnp.float32)
    rows = rows_ref[...].astype(jnp.float32).astype(jnp.bfloat16)
    cols = cols_ref[...].astype(jnp.float32).astype(jnp.bfloat16)
    spot_r = lax.broadcasted_iota(jnp.int32, (CX, 128), 0).astype(jnp.float32).astype(jnp.bfloat16)
    spot_c = lax.broadcasted_iota(jnp.int32, (CY, 128), 0).astype(jnp.float32).astype(jnp.bfloat16)
    zero = jnp.zeros((CX, 128), jnp.bfloat16)
    one_c = jnp.ones((CY, 128), jnp.bfloat16)
    zero_c = jnp.zeros((CY, 128), jnp.bfloat16)
    for s in range(rows.shape[0]):
        lanes = pl.ds(s * 128, 128)
        hit = spot_r == jnp.broadcast_to(rows[s : s + 1], (CX, 128))
        for k, piece in enumerate(pieces):
            a_ref[pl.ds(k * CX, CX), lanes] = jnp.where(
                hit, jnp.broadcast_to(piece[s : s + 1], (CX, 128)), zero
            )
        hit = spot_c == jnp.broadcast_to(cols[s : s + 1], (CY, 128))
        b_ref[:, lanes] = jnp.where(hit, one_c, zero_c)
    part = lax.dot_general(
        a_ref[...], b_ref[...], (((1,), (1,)), ((), ())), preferred_element_type=jnp.float32
    )

    @pl.when(step == 0)
    def _():
        acc_ref[...] = part

    @pl.when(step > 0)
    def _():
        acc_ref[...] += part

    @pl.when(step == pl.num_programs(0) - 1)
    def _():
        sum_w_ref[...] = acc_ref[0:CX] + acc_ref[CX : 2 * CX] + acc_ref[2 * CX : 3 * CX]
        sum_wh_ref[...] = (
            acc_ref[3 * CX : 4 * CX] + acc_ref[4 * CX : 5 * CX] + acc_ref[5 * CX : 6 * CX]
        )


def scatter(rows, cols, live, got, start, stop, chunk):
    steps = (stop - start) // chunk
    block = pl.BlockSpec((chunk, 128), lambda i: (start // chunk + i, 0))
    whole = pl.BlockSpec((CX, CY), lambda i: (0, 0))
    return pl.pallas_call(
        scatter_kernel,
        grid=(steps,),
        in_specs=[block] * 3 + [pl.BlockSpec((chunk, 1, 768), lambda i: (start // chunk + i, 0, 0))],
        out_specs=[whole, whole],
        out_shape=[shape(CX, CY)] * 2,
        scratch_shapes=[
            pltpu.VMEM((6 * CX, chunk * 128), jnp.bfloat16),
            pltpu.VMEM((CY, chunk * 128), jnp.bfloat16),
            pltpu.VMEM((6 * CX, CY), jnp.float32),
        ],
        compiler_params=pltpu.CompilerParams(vmem_limit_bytes=20 * 1024 * 1024),
        cost_estimate=pl.CostEstimate(
            flops=2 * 6 * CX * CY * 128 * (stop - start),
            bytes_accessed=4 * 128 * 4 * (stop - start),
            transcendentals=0,
        ),
    )(rows, cols, live, got)


def body(
    fields,
    velocity,
    mode_gain,
    lift_weight,
    project_weight,
    obs_height,
    obs_weight,
    cell_rows,
    cell_cols,
    counts,
):
    even_pairs_x = [(i, i ^ 1) for i in range(GX)]
    odd_pairs_x = [(i, (i + 1) % GX if i % 2 else (i - 1) % GX) for i in range(GX)]
    even_pairs = [(i, i ^ 1) for i in range(GY)]
    odd_pairs = [(i, (i + 1) % GY if i % 2 else (i - 1) % GY) for i in range(GY)]
    even_x, odd_x, even, odd = local_kernel(
        edge_kernel,
        [shape(16, CY), shape(16, CY), shape(SIDE, CX), shape(SIDE, CX)],
        (fields, velocity),
        scratch=[
            pltpu.VMEM((F + 1, CX, CY), jnp.float32),
            pltpu.VMEM((8, CY), jnp.float32),
            pltpu.SemaphoreType.DMA((F + 2,)),
        ],
        in_place=True,
        limit=56,
    )
    odd = lax.ppermute(odd, "gy", odd_pairs)
    even = lax.ppermute(even, "gy", even_pairs)
    odd_x = lax.ppermute(odd_x, "gx", odd_pairs_x)
    even_x = lax.ppermute(even_x, "gx", even_pairs_x)
    stepped = local_kernel(
        step_kernel,
        [shape(CX, CY)] * GX,
        (fields, velocity, odd, even, odd_x, even_x),
        scratch=[pltpu.VMEM((F, CX, CY), jnp.float32)],
    )
    live = (jnp.arange(128, dtype=jnp.int32)[None, :] < counts[0][:, None]).astype(jnp.float32)
    gains = mode_gain.transpose(2, 1, 0, 3)
    project = project_weight.T
    *blocks, live, gains, project = lax.optimization_barrier(
        (*exchange(stepped), live, gains, project)
    )
    sent = local_kernel(
        forward_kernel,
        [shape(DEV, 1, 768)],
        (
            *blocks,
            jnp.asarray(FORE),
            jnp.asarray(PERIOD),
            obs_height[0],
            obs_weight[0],
        ),
        flops=3 * 2 * (256 * NX * CY + 512 * 256 * 512),
        scratch=[
            pltpu.VMEM((NX, CY), jnp.float32),
            pltpu.VMEM((2 * MX, CY), jnp.float32),
        ],
    )[0]
    got = all_to_all(sent, ("gx", "gy"))
    sent = local_kernel(
        mix_kernel,
        [shape(DEV, 1, 512)],
        (
            got,
            jnp.asarray(TURN),
            gains,
            lift_weight,
            project,
        ),
        flops=6 * 2 * 512 * 128 * 16,
    )[0]

    points = (cell_rows[0], cell_cols[0], live)
    w_0, wh_0 = scatter(*points, got, 0, 224, 56)

    back = all_to_all(sent, ("gx", "gy"))
    back, w_0, wh_0 = lax.optimization_barrier((back, w_0, wh_0))
    blocks = local_kernel(
        backward_kernel,
        [shape(CX, CY)] * GX,
        (back, jnp.asarray(BACK)),
        flops=3 * 2 * (512 * NX * CY + 512 * 256 * 512),
        scratch=[pltpu.VMEM((MY, 2 * MX), jnp.float32), pltpu.VMEM((NX, CY), jnp.float32)],
    )
    got, w_0 = lax.optimization_barrier((got, w_0))
    w_1, wh_1 = scatter(*points, got, 224, 256, 32)
    return tuple(
        local_kernel(
            finish_kernel,
            [shape(F, CX, CY), shape(CX, CY)],
            (
                *stepped,
                *exchange(blocks),
                w_0,
                w_1,
                wh_0,
                wh_1,
            ),
        )
    )


def solution(mesh):
    return jax.shard_map(
        body,
        mesh=mesh,
        in_specs=(
            P(None, "gx", "gy"),
            P(None, "gx", "gy"),
            P("gx", "gy", None, None),
            P(),
            P(),
            P(("gx", "gy"), None, None),
            P(("gx", "gy"), None, None),
            P(("gx", "gy"), None, None),
            P(("gx", "gy"), None, None),
            P(("gx", "gy"), None),
        ),
        out_specs=(P(None, "gx", "gy"), P("gx", "gy")),
        check_vma=False,
    )
```

```python
import math

import jax
import jax.numpy as jnp
import numpy as np
from jax import lax
from jax.experimental import pallas as pl
from jax.experimental.pallas import tpu as pltpu
from jax.sharding import PartitionSpec as P

MX = 256
MY = 256
NX = 1024
NY = 8192
F = 8
CX = 128
CY = 256
GX = 8
GY = 32
DEV = GX * GY
HALF = MY // 2
PARTNERS = (0, 2, 6, 3, 7, 4, 5, 1)
SIDE = 48

time_step = 0.2
diffusion = 0.25
highest = lax.Precision.HIGHEST


ORDER = np.array(
    [GX * gy + 4 * high + low for high in range(2) for low in range(4) for gy in range(GY)]
)


def tables():
    x = np.arange(MX)
    q = np.arange(MX // 2)
    ang = 2.0 * np.pi * (q[:, None] * x[None, :]) / NX
    fore_x = np.concatenate((np.cos(ang), -np.sin(ang)))
    back_x = np.concatenate((np.cos(ang.T), -np.sin(ang.T)), axis=1)
    back_x[:, MX // 2] = np.cos(2.0 * np.pi * x / 8.0)
    ang = 2.0 * np.pi * np.arange(8) / 8.0
    period = np.stack([np.tile(row[:, None], (1, CY)) for row in (np.cos(ang), -np.sin(ang))])
    ang = 2.0 * np.pi * (ORDER[:, None] * np.arange(CY)[None, :]) / NY
    fore_y = np.concatenate((np.cos(ang), np.sin(ang)))
    back_y = np.concatenate((np.cos(ang.T), np.sin(ang.T)))
    turn = np.zeros((2, 4, 4, GY, 2, 2, 32))
    for quarter in range(4):
        for low in range(4):
            for high in range(2):
                n = 8 * quarter + 4 * high + low
                ang = 2.0 * np.pi * ((n * np.arange(GY)) % GY) / GY
                turn[0, quarter, low, :, :, high] = np.cos(ang)[:, None, None]
                turn[1, quarter, low, :, :, high] = np.sin(ang)[:, None, None]
    turn = turn.reshape(2, 4, 4, GY, 128)
    def pair(array):
        high = array.astype(np.float32).astype(jnp.bfloat16)
        return high, (array - high.astype(np.float64)).astype(np.float32).astype(jnp.bfloat16)

    fore = np.concatenate((*pair(fore_x), *pair(fore_y)))
    back = np.concatenate((*pair(back_y), *pair(back_x)))
    return (
        fore,
        back,
        period.astype(np.float32),
        turn.astype(np.float32),
    )


FORE, BACK, PERIOD, TURN = tables()
SCALE_IN = 1.0 / math.sqrt(NX * NY)
SCALE_OUT = 1.0 / math.sqrt(MX * MY)


def all_to_all(array, axis):
    return lax.all_to_all(array, axis, split_axis=0, concat_axis=0, tiled=True)


def dot(a, b, contract=((1,), (0,))):
    return lax.dot_general(
        a, b, (contract, ((), ())), precision=highest, preferred_element_type=jnp.float32
    )


def pieces(array):
    high = array.astype(jnp.bfloat16)
    return high, (array - high.astype(jnp.float32)).astype(jnp.bfloat16)


def split_dot(table, b, contract=((1,), (0,))):
    table_high, table_low = table
    b_high, b_low = pieces(b)

    def one(left, right):
        return lax.dot_general(
            left, right, (contract, ((), ())), preferred_element_type=jnp.float32
        )

    return one(table_high, b_high) + (one(table_high, b_low) + one(table_low, b_high))


def shape(*dims):
    return jax.ShapeDtypeStruct(dims, jnp.float32)


def local_kernel(kernel, out_shape, operands, flops=0, scratch=(), in_place=False, limit=16):
    vmem = pl.BlockSpec(memory_space=pltpu.VMEM)
    place = pl.BlockSpec(memory_space=pl.ANY) if in_place else vmem
    size = sum(4 * math.prod(a.shape) for a in (*operands, *out_shape))
    return pl.pallas_call(
        kernel,
        in_specs=[place] * len(operands),
        out_specs=[vmem] * len(out_shape),
        out_shape=out_shape,
        scratch_shapes=scratch,
        compiler_params=pltpu.CompilerParams(vmem_limit_bytes=limit * 1024 * 1024),
        cost_estimate=pl.CostEstimate(flops=flops, bytes_accessed=size, transcendentals=0),
    )(*operands)


def face(speed):
    return (
        time_step * (jnp.maximum(speed, 0.0) + diffusion),
        time_step * (jnp.minimum(speed, 0.0) - diffusion),
    )


def edge_kernel(
    fields_hbm, velocity_hbm, even_x_ref, odd_x_ref, even_ref, odd_ref, block_ref, row_ref, sems
):
    copies = [
        pltpu.make_async_copy(fields_hbm.at[f], block_ref.at[f], sems.at[f]) for f in range(F)
    ]
    copies += [
        pltpu.make_async_copy(velocity_hbm.at[1], block_ref.at[F], sems.at[F]),
        pltpu.make_async_copy(velocity_hbm.at[0, pl.ds(0, 8)], row_ref, sems.at[F + 1]),
    ]
    for copy in copies:
        copy.start()
    lane = lax.broadcasted_iota(jnp.int32, (CX, 128), 1)
    sides = jnp.zeros((CX, 128), jnp.float32)
    for f in range(F + 1):
        copies[f].wait()
        tile = block_ref[f, :, 0:128]
        sides = jnp.where(lane == f, pltpu.roll(tile, f, 1) if f else tile, sides)
        if f < F:
            sides = jnp.where(
                lane == 16 + f, pltpu.roll(block_ref[f, :, 128:256], 17 + f, 1), sides
            )
    sides = jnp.transpose(sides)
    is_even = lax.rem(lax.axis_index("gy"), 2) == 0
    first, last = sides[0:16], sides[16:32]
    even_ref[0:16] = jnp.where(is_even, last, first)
    odd_ref[0:16] = jnp.where(is_even, first, last)
    for ref in (even_ref, odd_ref):
        ref[16:] = jnp.zeros((SIDE - 16, CX), jnp.float32)
    copies[F + 1].wait()
    rest = jnp.zeros((7, CY), jnp.float32)
    first = [block_ref[f, 0:1] for f in range(F)] + [row_ref[0:1], rest]
    last = [block_ref[f, CX - 1 : CX] for f in range(F)] + [row_ref[0:1], rest]
    first, last = jnp.concatenate(first, axis=0), jnp.concatenate(last, axis=0)
    is_even = lax.rem(lax.axis_index("gx"), 2) == 0
    even_x_ref[...] = jnp.where(is_even, last, first)
    odd_x_ref[...] = jnp.where(is_even, first, last)


def step_kernel(fields_ref, velocity_ref, odd_ref, even_ref, odd_x_ref, even_x_ref, *block_refs):
    *block_refs, held_ref = block_refs
    row = lax.broadcasted_iota(jnp.int32, (CX, CY), 0)
    col = lax.broadcasted_iota(jnp.int32, (CX, CY), 1)
    first_row, last_row = row == 0, row == CX - 1
    first_col, last_col = col == 0, col == CY - 1
    gx, gy = lax.axis_index("gx"), lax.axis_index("gy")
    open_w = jnp.where(gx > 0, 1.0, 0.0)
    open_e = jnp.where(gx < GX - 1, 1.0, 0.0)
    open_s = jnp.where(gy > 0, 1.0, 0.0)
    open_n = jnp.where(gy < GY - 1, 1.0, 0.0)
    is_even = lax.rem(gx, 2) == 0
    above = jnp.where(is_even, odd_x_ref[...], even_x_ref[...])
    below = jnp.where(is_even, even_x_ref[...], odd_x_ref[...])
    is_even = lax.rem(gy, 2) == 0
    before = jnp.transpose(jnp.where(is_even, odd_ref[0:16], even_ref[0:16]))
    after = jnp.transpose(jnp.where(is_even, even_ref[0:16], odd_ref[0:16]))
    low_w, high_w = (
        jnp.where(first_row, value * open_w, value) for value in face(velocity_ref[0])
    )
    low_e, high_e = (
        jnp.where(last_row, edge * open_e, pltpu.roll(value, CX - 1, 0))
        for value, edge in zip((low_w, high_w), face(below[F : F + 1]))
    )
    low_s, high_s = (
        jnp.where(first_col, value * open_s, value) for value in face(velocity_ref[1])
    )
    low_n, high_n = (
        jnp.where(last_col, edge * open_n, pltpu.roll(value, CY - 1, 1))
        for value, edge in zip((low_s, high_s), face(after[:, F : F + 1]))
    )
    own = 1.0 - low_e + high_w - low_n + high_s
    for f in range(F):
        block = fields_ref[f]
        west = jnp.where(first_row, above[f : f + 1], pltpu.roll(block, 1, 0))
        east = jnp.where(last_row, below[f : f + 1], pltpu.roll(block, CX - 1, 0))
        south = jnp.where(first_col, before[:, f : f + 1], pltpu.roll(block, 1, 1))
        north = jnp.where(last_col, after[:, f : f + 1], pltpu.roll(block, CY - 1, 1))
        held_ref[f] = (
            own * block + low_w * west - high_e * east + low_s * south - high_n * north
        )
    for k, ref in zip(PARTNERS, block_refs):
        ref[...] = held_ref[lax.bitwise_xor(gx, k)]


def fetch_kernel(table_ref, out_ref):
    out_ref[...] = table_ref[...]


def quarter_turn(index, t):
    place = lax.rem(index * t, 4)
    cosine = jnp.where(place == 0, 1.0, jnp.where(place == 2, -1.0, 0.0))
    sine = jnp.where(place == 1, 1.0, jnp.where(place == 3, -1.0, 0.0))
    return cosine.astype(jnp.float32), sine.astype(jnp.float32)


def forward_kernel(*refs):
    *block_refs, table_ref, period_ref, height_ref, weight_ref = refs[:-3]
    out_ref, columns_ref, parts_ref = refs[-3:]
    for k, ref in zip(PARTNERS, block_refs):
        source = lax.bitwise_xor(lax.axis_index("gx"), k)
        columns_ref[pl.ds(pl.multiple_of(source * CX, CX), CX), :] = ref[...]
    q = lax.broadcasted_iota(jnp.int32, (HALF, CY), 0)
    real = jnp.zeros((HALF, CY), jnp.float32)
    imag = jnp.zeros((HALF, CY), jnp.float32)
    for t in range(4):
        piece = split_dot(
            (table_ref[0:256], table_ref[256:512]), columns_ref[t * MX : (t + 1) * MX]
        )
        piece_r, piece_i = piece[:HALF], piece[HALF:]
        if t == 0:
            real, imag = piece_r, piece_i
        else:
            cosine, sine = quarter_turn(q, t)
            real = real + piece_r * cosine + piece_i * sine
            imag = imag + piece_i * cosine - piece_r * sine
    folded = jnp.sum(columns_ref[...].reshape(NX // 8, 8, CY), axis=0)
    last_r = jnp.sum(folded * period_ref[0], axis=0, keepdims=True)
    last_i = jnp.sum(folded * period_ref[1], axis=0, keepdims=True)
    row = lax.broadcasted_iota(jnp.int32, (HALF, HALF), 0)
    col = lax.broadcasted_iota(jnp.int32, (HALF, HALF), 1)
    mirror = jnp.where(row + col == HALF, 1.0, 0.0).astype(jnp.bfloat16)

    def reflect(block):
        high, low = pieces(block)
        return jnp.dot(mirror, high, preferred_element_type=jnp.float32) + jnp.dot(
            mirror, low, preferred_element_type=jnp.float32
        )

    parts_ref[0:HALF] = real
    parts_ref[HALF:MX] = jnp.where(q == 0, last_r, reflect(real))
    parts_ref[MX : MX + HALF] = imag
    parts_ref[MX + HALF :] = -jnp.where(q == 0, last_i, reflect(imag))
    mixed = split_dot((table_ref[512:1024], table_ref[1024:]), parts_ref[...], ((1,), (1,)))
    modes = (mixed[:MY, :MX] + mixed[MY:, MX:], mixed[:MY, MX:] - mixed[MY:, :MX])
    group = lax.broadcasted_iota(jnp.int32, (GY, 128), 1) // 32
    for low in range(4):
        for half in range(2):
            tiles = [
                modes[part][high * 128 + low * 32 : high * 128 + low * 32 + 32, half * 128 : half * 128 + 128]
                for part in range(2)
                for high in range(2)
            ]
            for s in range(4):
                gx = 4 * half + s
                value = None
                for k, tile in enumerate(tiles):
                    shift = (32 * (k - s)) % 128
                    moved = pltpu.roll(tile, shift, 1) if shift else tile
                    value = moved if value is None else jnp.where(group == k, moved, value)
                out_ref[gx * GY : (gx + 1) * GY, 0, low * 128 : (low + 1) * 128] = value
    out_ref[:, 0, 512:640] = height_ref[...]
    out_ref[:, 0, 640:768] = weight_ref[...]


def mix_kernel(got_ref, turn_ref, gain_ref, lift_ref, project_ref, out_ref):
    gy = lax.axis_index("gy")
    quarter = lax.rem(gy, 4)
    lane = lax.broadcasted_iota(jnp.int32, (F, 128), 1)
    is_real = lane < 64
    high_zero = (lane // 32) % 2 == 0
    coeffs = []
    for low in range(4):
        cosine = turn_ref[0, quarter, low]
        sine = turn_ref[1, quarter, low]
        straight, crossed = [], []
        for f in range(F):
            block = got_ref[f * GY : (f + 1) * GY, 0, low * 128 : (low + 1) * 128]
            straight.append(jnp.sum(block * cosine, axis=0, keepdims=True))
            crossed.append(jnp.sum(block * sine, axis=0, keepdims=True))
        crossed = pltpu.roll(jnp.concatenate(crossed, axis=0), 64, 1)
        total = jnp.concatenate(straight, axis=0) + jnp.where(is_real, crossed, -crossed)
        coeffs.append(jnp.transpose(total * SCALE_IN))
    lift_high, lift_low = pieces(lift_ref[...])
    high, low = pieces(jnp.concatenate(coeffs, axis=0))
    lifted = jnp.dot(
        jnp.concatenate((high, high, low), axis=1),
        jnp.concatenate((lift_high, lift_low, lift_high), axis=0),
        preferred_element_type=jnp.float32,
    )
    mixed = []
    for low in range(4):
        part = lifted[low * 128 : (low + 1) * 128]
        mixed_r, mixed_i = [], []
        for high in range(2):
            lift_r = part[high * 32 : high * 32 + 32]
            lift_i = part[64 + high * 32 : 96 + high * 32]
            gain_r = gain_ref[0, 4 * high + low]
            gain_i = gain_ref[1, 4 * high + low]
            mixed_r.append(gain_r * lift_r - gain_i * lift_i)
            mixed_i.append(gain_r * lift_i + gain_i * lift_r)
        mixed += mixed_r + mixed_i
    mixed = jnp.concatenate(mixed, axis=0)
    result = split_dot(pieces(project_ref[...]), mixed, ((1,), (1,)))
    for low in range(4):
        cosine = turn_ref[0, quarter, low]
        sine = turn_ref[1, quarter, low]
        outgoing = result[:, low * 128 : (low + 1) * 128]
        if low == 0:
            first = high_zero & (gy == 0)
            outgoing = outgoing * jnp.where(first, SCALE_OUT, 2.0 * SCALE_OUT)
        else:
            outgoing = outgoing * (2.0 * SCALE_OUT)
        swapped = pltpu.roll(outgoing, 64, 1)
        swapped = jnp.where(is_real, -swapped, swapped)
        for f in range(F):
            out_ref[f * GY : (f + 1) * GY, 0, low * 128 : (low + 1) * 128] = (
                outgoing[f : f + 1] * cosine + swapped[f : f + 1] * sine
            )


def backward_kernel(got_ref, table_ref, *refs):
    *out_refs, modes_ref, field_ref = refs
    group = lax.broadcasted_iota(jnp.int32, (GY, 128), 1) // 32
    for low in range(4):
        for half in range(2):
            tiles = [
                got_ref[gx * GY : (gx + 1) * GY, 0, low * 128 : (low + 1) * 128]
                for gx in range(4 * half, 4 * half + 4)
            ]
            for part in range(2):
                for high in range(2):
                    k = 2 * part + high
                    value = None
                    for s, tile in enumerate(tiles):
                        shift = (32 * (s - k)) % 128
                        moved = pltpu.roll(tile, shift, 1) if shift else tile
                        value = moved if value is None else jnp.where(group == s, moved, value)
                    lanes = part * MX + half * 128
                    start = high * 128 + low * 32
                    modes_ref[start : start + 32, lanes : lanes + 128] = value
    mixed = split_dot((table_ref[0:512], table_ref[512:1024]), modes_ref[...])
    real = mixed[:CY, :MX] - mixed[CY:, MX:]
    imag = mixed[:CY, MX:] + mixed[CY:, :MX]
    row = lax.broadcasted_iota(jnp.int32, (HALF, HALF), 0)
    col = lax.broadcasted_iota(jnp.int32, (HALF, HALF), 1)
    mirror = jnp.where(row + col == HALF, 1.0, 0.0).astype(jnp.bfloat16)

    def reflect(block):
        high, low = pieces(block)
        return jnp.dot(high, mirror, preferred_element_type=jnp.float32) + jnp.dot(
            low, mirror, preferred_element_type=jnp.float32
        )

    index = lax.broadcasted_iota(jnp.int32, (CY, HALF), 1)
    even = real[:, :HALF] + reflect(real[:, HALF:])
    odd = imag[:, :HALF] - reflect(imag[:, HALF:])
    odd = jnp.where(index == 0, real[:, HALF:], odd)
    pick = jnp.where(
        lax.broadcasted_iota(jnp.int32, (16, HALF), 1) == 0, 1.0, 0.0
    ).astype(jnp.bfloat16)
    last = split_dot((pick, jnp.zeros_like(pick)), imag[:, HALF:], ((1,), (1,)))[:8]
    place = lax.broadcasted_iota(jnp.int32, (8, CY), 0)
    sine = jnp.where(place % 4 == 0, 0.0, jnp.where(place % 2 == 0, 1.0, math.sqrt(0.5)))
    last = last * jnp.where(place < 4, sine, -sine)
    for t in range(4):
        turned = (even, odd)
        if t:
            cosine, sine = quarter_turn(index, t)
            turned = (even * cosine - odd * sine, odd * cosine + even * sine)
        block = split_dot(
            (table_ref[1024:1280], table_ref[1280:]),
            jnp.concatenate(turned, axis=1),
            ((1,), (1,)),
        )
        field_ref[t * MX : (t + 1) * MX] = (
            block.reshape(MX // 8, 8, CY) + last[None]
        ).reshape(MX, CY)
    for k, ref in zip(PARTNERS, out_refs):
        owner = lax.bitwise_xor(lax.axis_index("gx"), k)
        ref[...] = field_ref[pl.ds(pl.multiple_of(owner * CX, CX), CX), :]


def finish_kernel(*refs):
    step_refs, block_refs, refs = refs[:GX], refs[GX : 2 * GX], refs[2 * GX :]
    w_0, w_1, wh_0, wh_1, out_ref, gradient_ref = refs
    gx = lax.axis_index("gx")
    for k, step_ref, block_ref in zip(PARTNERS, step_refs, block_refs):
        out_ref[lax.bitwise_xor(gx, k)] = step_ref[...] + block_ref[...]
    gradient_ref[...] = out_ref[0] * (w_0[...] + w_1[...]) - (wh_0[...] + wh_1[...])


def exchange(blocks):
    return [blocks[0]] + [
        lax.ppermute(block, "gx", [(i, i ^ k) for i in range(GX)])
        for k, block in zip(PARTNERS[1:], blocks[1:])
    ]


def scatter_kernel(
    rows_ref, cols_ref, live_ref, got_ref, sum_w_ref, sum_wh_ref, a_ref, b_ref, acc_ref
):
    step = pl.program_id(0)
    weight = got_ref[:, 0, 640:] * live_ref[...]
    product = weight * got_ref[:, 0, 512:640]
    pieces = []
    for value in (weight, product):
        for _ in range(3):
            piece = value.astype(jnp.bfloat16)
            pieces.append(piece)
            value = value - piece.astype(jnp.float32)
    rows = rows_ref[...].astype(jnp.float32).astype(jnp.bfloat16)
    cols = cols_ref[...].astype(jnp.float32).astype(jnp.bfloat16)
    spot_r = lax.broadcasted_iota(jnp.int32, (CX, 128), 0).astype(jnp.float32).astype(jnp.bfloat16)
    spot_c = lax.broadcasted_iota(jnp.int32, (CY, 128), 0).astype(jnp.float32).astype(jnp.bfloat16)
    zero = jnp.zeros((CX, 128), jnp.bfloat16)
    one_c = jnp.ones((CY, 128), jnp.bfloat16)
    zero_c = jnp.zeros((CY, 128), jnp.bfloat16)
    for s in range(rows.shape[0]):
        lanes = pl.ds(s * 128, 128)
        hit = spot_r == jnp.broadcast_to(rows[s : s + 1], (CX, 128))
        for k, piece in enumerate(pieces):
            a_ref[pl.ds(k * CX, CX), lanes] = jnp.where(
                hit, jnp.broadcast_to(piece[s : s + 1], (CX, 128)), zero
            )
        hit = spot_c == jnp.broadcast_to(cols[s : s + 1], (CY, 128))
        b_ref[:, lanes] = jnp.where(hit, one_c, zero_c)
    part = lax.dot_general(
        a_ref[...], b_ref[...], (((1,), (1,)), ((), ())), preferred_element_type=jnp.float32
    )

    @pl.when(step == 0)
    def _():
        acc_ref[...] = part

    @pl.when(step > 0)
    def _():
        acc_ref[...] += part

    @pl.when(step == pl.num_programs(0) - 1)
    def _():
        sum_w_ref[...] = acc_ref[0:CX] + acc_ref[CX : 2 * CX] + acc_ref[2 * CX : 3 * CX]
        sum_wh_ref[...] = (
            acc_ref[3 * CX : 4 * CX] + acc_ref[4 * CX : 5 * CX] + acc_ref[5 * CX : 6 * CX]
        )


def scatter(rows, cols, live, got, start, stop, chunk):
    steps = (stop - start) // chunk
    block = pl.BlockSpec((chunk, 128), lambda i: (start // chunk + i, 0))
    whole = pl.BlockSpec((CX, CY), lambda i: (0, 0))
    return pl.pallas_call(
        scatter_kernel,
        grid=(steps,),
        in_specs=[block] * 3 + [pl.BlockSpec((chunk, 1, 768), lambda i: (start // chunk + i, 0, 0))],
        out_specs=[whole, whole],
        out_shape=[shape(CX, CY)] * 2,
        scratch_shapes=[
            pltpu.VMEM((6 * CX, chunk * 128), jnp.bfloat16),
            pltpu.VMEM((CY, chunk * 128), jnp.bfloat16),
            pltpu.VMEM((6 * CX, CY), jnp.float32),
        ],
        compiler_params=pltpu.CompilerParams(vmem_limit_bytes=20 * 1024 * 1024),
        cost_estimate=pl.CostEstimate(
            flops=2 * 6 * CX * CY * 128 * (stop - start),
            bytes_accessed=4 * 128 * 4 * (stop - start),
            transcendentals=0,
        ),
    )(rows, cols, live, got)


def body(
    fields,
    velocity,
    mode_gain,
    lift_weight,
    project_weight,
    obs_height,
    obs_weight,
    cell_rows,
    cell_cols,
    counts,
):
    even_pairs_x = [(i, i ^ 1) for i in range(GX)]
    odd_pairs_x = [(i, (i + 1) % GX if i % 2 else (i - 1) % GX) for i in range(GX)]
    even_pairs = [(i, i ^ 1) for i in range(GY)]
    odd_pairs = [(i, (i + 1) % GY if i % 2 else (i - 1) % GY) for i in range(GY)]
    even_x, odd_x, even, odd = local_kernel(
        edge_kernel,
        [shape(16, CY), shape(16, CY), shape(SIDE, CX), shape(SIDE, CX)],
        (fields, velocity),
        scratch=[
            pltpu.VMEM((F + 1, CX, CY), jnp.float32),
            pltpu.VMEM((8, CY), jnp.float32),
            pltpu.SemaphoreType.DMA((F + 2,)),
        ],
        in_place=True,
        limit=56,
    )
    odd = lax.ppermute(odd, "gy", odd_pairs)
    even = lax.ppermute(even, "gy", even_pairs)
    odd_x = lax.ppermute(odd_x, "gx", odd_pairs_x)
    even_x = lax.ppermute(even_x, "gx", even_pairs_x)
    stepped = local_kernel(
        step_kernel,
        [shape(CX, CY)] * GX,
        (fields, velocity, odd, even, odd_x, even_x),
        scratch=[pltpu.VMEM((F, CX, CY), jnp.float32)],
    )
    live = (jnp.arange(128, dtype=jnp.int32)[None, :] < counts[0][:, None]).astype(jnp.float32)
    gains = mode_gain.transpose(2, 1, 0, 3)
    project = project_weight.T
    *blocks, live, gains, project = lax.optimization_barrier(
        (*exchange(stepped), live, gains, project)
    )
    sent = local_kernel(
        forward_kernel,
        [shape(DEV, 1, 768)],
        (
            *blocks,
            jnp.asarray(FORE),
            jnp.asarray(PERIOD),
            obs_height[0],
            obs_weight[0],
        ),
        flops=3 * 2 * (256 * NX * CY + 512 * 256 * 512),
        scratch=[
            pltpu.VMEM((NX, CY), jnp.float32),
            pltpu.VMEM((2 * MX, CY), jnp.float32),
        ],
    )[0]
    got = all_to_all(sent, ("gx", "gy"))
    sent = local_kernel(
        mix_kernel,
        [shape(DEV, 1, 512)],
        (
            got,
            jnp.asarray(TURN),
            gains,
            lift_weight,
            project,
        ),
        flops=6 * 2 * 512 * 128 * 16,
    )[0]

    sent, table = lax.optimization_barrier((sent, jnp.asarray(BACK)))
    table = local_kernel(
        fetch_kernel, [jax.ShapeDtypeStruct(BACK.shape, jnp.bfloat16)], (table,)
    )[0]
    points = (cell_rows[0], cell_cols[0], live)
    w_0, wh_0 = scatter(*points, got, 0, 192, 48)

    back = all_to_all(sent, ("gx", "gy"))
    back, w_0, wh_0, table = lax.optimization_barrier((back, w_0, wh_0, table))
    blocks = local_kernel(
        backward_kernel,
        [shape(CX, CY)] * GX,
        (back, table),
        flops=3 * 2 * (512 * NX * CY + 512 * 256 * 512),
        scratch=[pltpu.VMEM((MY, 2 * MX), jnp.float32), pltpu.VMEM((NX, CY), jnp.float32)],
    )
    got, w_0 = lax.optimization_barrier((got, w_0))
    w_1, wh_1 = scatter(*points, got, 192, 256, 32)
    return tuple(
        local_kernel(
            finish_kernel,
            [shape(F, CX, CY), shape(CX, CY)],
            (
                *stepped,
                *exchange(blocks),
                w_0,
                w_1,
                wh_0,
                wh_1,
            ),
        )
    )


def solution(mesh):
    return jax.shard_map(
        body,
        mesh=mesh,
        in_specs=(
            P(None, "gx", "gy"),
            P(None, "gx", "gy"),
            P("gx", "gy", None, None),
            P(),
            P(),
            P(("gx", "gy"), None, None),
            P(("gx", "gy"), None, None),
            P(("gx", "gy"), None, None),
            P(("gx", "gy"), None, None),
            P(("gx", "gy"), None),
        ),
        out_specs=(P(None, "gx", "gy"), P("gx", "gy")),
        check_vma=False,
    )
```
